32 devices in a mesh: group: 2 (over y), tile: 4 (over z), band: 4 (over x, core).
Axes of the slice: x: 2, y: 2, z: 4, core: 2. Of those that a mesh axis runs over, the one named last changes fastest.
Arguments:
- features: bfloat16 [256, 1024, 24], P(('group', 'band'), 'tile'), parts along dimension 0, may hold values from -6 to 6
- land_mask: int32 [128, 1024], P('band', 'tile'), may hold values 0 or 1
- cell_blocks: int32 [4, 4, 81, 128], P('band', 'tile'), may hold values from 0 to 8192, as said below
- region_ids: int32 [4, 4, 81], P('band', 'tile'), may hold values from 0 to 13999
- targets: float32 [28160], P(('group', 'tile', 'band')), parts along dimension 0, may hold values from -6 to 6
- w_embed: bfloat16 [384, 256], replicated, may hold values from -0.3125 to 0.3125
- k_first: bfloat16 [9, 256], replicated, may hold values from -2 to 2
- w_mix: bfloat16 [256, 256], replicated, may hold values from -0.375 to 0.375
- k_deep: bfloat16 [9, 256], replicated, may hold values from -2 to 2
- w_head: bfloat16 [256, 16], replicated, may hold values from -0.375 to 0.375
Outputs:
- cell_pred: float32 [256, 1024], P(('group', 'band'), 'tile'), parts along dimension 0
- region_mean: float32 [28160], P(('group', 'tile', 'band')), parts along dimension 0
- loss_value: float32 [2], P('group'), parts along dimension 0
- input_grad: bfloat16 [256, 1024, 24], P(('group', 'band'), 'tile'), parts along dimension 0
The draws below stay inside these ranges and needn't reach their ends.
There are 2 independent parts, one for each index of `group`. The reference program is written for one: setup_inputs(seed, part) draws one part's arguments, and reference() takes and returns one part's arrays. A program takes and returns all parts, laid end to end along the dimension named above; an argument that names none is the same for every part. Nothing has to cross between parts.
Inputs may be any that keep to these rules, and one draw needn't show every extreme that they name: `cell_blocks`: each device's blocks name each of its 32 x 256 cells at most once, by its row-major index in that device's block of cells; the value 32 * 256 marks an empty slot.
All inputs are finite; a program needn't handle non-finite values. No bound on the sum of `land_mask` on one device may be relied on, other than what follows from the above.
Results may differ from the reference program's by a relative error of at most 0.014.
Values may be sent and summed in bfloat16 or wider, within the bound.
No kernel may reach another device: no remote copies, remote signals or barrier semaphores. Data moves between devices by JAX's collectives and lax.ppermute only.
A program may use at most 64 MiB of HBM per device.

```python
import jax
import jax.numpy as jnp
from jax import lax

C_IN = 24
CH = 256
REGIONS = 14000
BLK = 128
HD = 32
WD = 256
BANDS = 4
TILES = 4
NH = 128
NW = 1024
CELLS = 131072
NBLK = 81
REG_PAD = 14080


def draw_cell_blocks(key, part):
    device_count = BANDS * TILES
    cell_total = HD * WD
    slot_total = NBLK * BLK
    device_keys = jax.random.split(key, device_count)

    def fill_device(device_key):
        key_perm, key_len = jax.random.split(device_key)
        shuffled = jax.random.permutation(key_perm, slot_total).astype(jnp.int32)
        lengths = jax.random.randint(key_len, (NBLK, 1), BLK // 2, BLK + 1).astype(jnp.int32)
        position = jnp.arange(BLK, dtype=jnp.int32)[None, :]
        candidate = jnp.where(shuffled < cell_total, shuffled, cell_total).reshape(NBLK, BLK)
        return jnp.where(position < lengths, candidate, cell_total).astype(jnp.int32)
    return jax.vmap(fill_device)(device_keys).reshape(BANDS, TILES, NBLK, BLK)


def plant(drawn, own_key, smallest, top_value):
    shape = drawn.shape
    index_at = [jax.random.randint(jax.random.fold_in(own_key, axis), (), 0, shape[axis]) for axis in range(len(shape))]
    drawn = drawn.at[tuple(index_at)].set(smallest)
    longest = shape.index(max(shape))
    index_at[longest] = (index_at[longest] + 1) % shape[longest]
    return drawn.at[tuple(index_at)].set(top_value)


def steps_of(own_key, dims, cuts, smallest, high):
    gain = 1.0
    for axis_at, shards_of in cuts:
        heights = jax.random.uniform(jax.random.fold_in(jax.random.fold_in(own_key, 6), axis_at), (shards_of,), jnp.float32, smallest / len(cuts), high / len(cuts))
        gain = gain * jnp.repeat(jnp.exp(heights), dims[axis_at] // shards_of).reshape((-1,) + (1,) * (len(dims) - 1 - axis_at))
    return gain


def normal_values(stream_key, dims, spread, limit, cuts=(), kind=jnp.bfloat16):
    result = jax.random.normal(stream_key, dims, jnp.float32) * spread
    if len(cuts) > 0:
        result = steps_of(stream_key, dims, cuts, -0.22, 0.18) * result
    return jnp.clip(result, min=-limit, max=limit).astype(kind)


def setup_inputs(seed: int = 0, part: int = 0) -> dict:
    seeds = jax.random.split(jax.random.key(seed), 11)
    own_keys = jax.random.split(jax.random.fold_in(seeds[10], part), 11)
    features = normal_values(own_keys[0], (NH, NW, C_IN), 1.0, 6.0, ((0, 4), (1, 4)))
    land_mask = plant((jax.random.randint(seeds[1], (NH, NW), 0, 10) < 7).astype(jnp.int32), jax.random.fold_in(seeds[1], 1), 0, 1)
    cell_blocks = draw_cell_blocks(jax.random.fold_in(seeds[10], 71), part)
    region_ids = plant(jax.random.randint(seeds[3], (BANDS, TILES, NBLK), 0, REGIONS), jax.random.fold_in(seeds[3], 1), 0, REGIONS - 1).astype(jnp.int32)
    targets = normal_values(own_keys[4], (REG_PAD,), 1.0, 6.0, ((0, 16),), jnp.float32)
    w_embed = normal_values(seeds[5], (16 * C_IN, CH), (16 * C_IN) ** -0.5, 0.3125)
    k_first = normal_values(seeds[6], (9, CH), 9 ** -0.5, 2.0)
    w_mix = normal_values(seeds[7], (CH, CH), CH ** -0.5, 0.375)
    k_deep = normal_values(seeds[8], (9, CH), 9 ** -0.5, 2.0)
    w_head = normal_values(seeds[9], (CH, 16), CH ** -0.5, 0.375)
    return {"features": features, "land_mask": land_mask, "cell_blocks": cell_blocks, "region_ids": region_ids, "targets": targets, "w_embed": w_embed, "k_first": k_first, "w_mix": w_mix, "k_deep": k_deep, "w_head": w_head}


SQRT_HALF = 0.7071067811865476
INV_ROOT = 0.3989422804014327


def gelu_exact(inputs):
    return 0.5 * inputs * (1.0 + lax.erf(inputs * SQRT_HALF))


def gelu_slope(inputs):
    return 0.5 * (1.0 + lax.erf(inputs * SQRT_HALF)) + inputs * jnp.exp(-0.5 * inputs * inputs) * INV_ROOT


def to_coarse(grid_field):
    height, breadth, depth = grid_field.shape
    blocks = grid_field.reshape(height // 4, 4, breadth // 4, 4, depth)
    return blocks.transpose(0, 2, 1, 3, 4).reshape(height // 4, breadth // 4, 16 * depth)


def to_fine(coarse):
    height, breadth, depth = coarse.shape
    inner = depth // 16
    blocks = coarse.reshape(height, breadth, 4, 4, inner)
    return blocks.transpose(0, 2, 1, 3, 4).reshape(4 * height, 4 * breadth, inner)


def project(operand, matrix):
    leading = operand.shape[:-1]
    flat = operand.reshape(-1, operand.shape[-1])
    return jnp.dot(flat, matrix, preferred_element_type=jnp.float32).reshape(leading + (matrix.shape[-1],))


def depthwise(padded, kernel, row_count, col_count):
    kernel_wide = kernel.astype(jnp.float32)
    padded_wide = padded.astype(jnp.float32)
    running = jnp.zeros((row_count, col_count, kernel.shape[1]), jnp.float32)
    for row_off in range(3):
        for col_off in range(3):
            window = padded_wide[row_off:row_off + row_count, col_off:col_off + col_count]
            running = running + kernel_wide[3 * row_off + col_off] * window
    return running


def pad_grid(grid_field):
    return jnp.pad(grid_field, ((1, 1), (1, 1), (0, 0)))


def per_device(grid_field):
    return grid_field.reshape(BANDS, HD, TILES, WD).transpose(0, 2, 1, 3).reshape(BANDS, TILES, HD * WD)


def reference(features, land_mask, cell_blocks, region_ids, targets, w_embed, k_first, w_mix, k_deep, w_head):
    land_cells = land_mask.astype(jnp.float32)
    patches = to_coarse(features)
    pre_first = project(patches, w_embed)
    act_first = gelu_exact(pre_first).astype(jnp.bfloat16)
    row_count, col_count = act_first.shape[0], act_first.shape[1]
    mixed_in = depthwise(pad_grid(act_first), k_first, row_count, col_count).astype(jnp.bfloat16)
    pre_mix = project(mixed_in, w_mix)
    act_mix = (act_first.astype(jnp.float32) + gelu_exact(pre_mix)).astype(jnp.bfloat16)
    pre_deep = depthwise(pad_grid(act_mix), k_deep, row_count, col_count)
    act_deep = (act_mix.astype(jnp.float32) + gelu_exact(pre_deep)).astype(jnp.bfloat16)
    cell_pred = to_fine(project(act_deep, w_head))[:, :, 0] * land_cells

    spare = jnp.zeros((BANDS, TILES, 1), jnp.float32)
    flat_pred = jnp.concatenate([per_device(cell_pred), spare], axis=2)
    flat_land = jnp.concatenate([per_device(land_cells), spare], axis=2)
    slot_index = cell_blocks.reshape(BANDS, TILES, NBLK * BLK)
    block_sums = jnp.take_along_axis(flat_pred, slot_index, axis=2).reshape(BANDS, TILES, NBLK, BLK).sum(-1)
    block_counts = jnp.take_along_axis(flat_land, slot_index, axis=2).reshape(BANDS, TILES, NBLK, BLK).sum(-1)
    block_owner = region_ids.reshape(-1)
    region_sum = jax.ops.segment_sum(block_sums.reshape(-1), block_owner, num_segments=REG_PAD)
    region_count = jax.ops.segment_sum(block_counts.reshape(-1), block_owner, num_segments=REG_PAD)
    region_mean = region_sum / jnp.maximum(region_count, 1.0)
    inside = jnp.arange(REG_PAD) < REGIONS
    misfit = region_mean - targets
    loss_value = (jnp.sum(jnp.where(inside, region_count * misfit * misfit, 0.0)) / (2.0 * CELLS)).reshape(1)
    region_grad = jnp.where(inside, region_count * misfit / jnp.maximum(region_count, 1.0), 0.0)

    slot_grad = jnp.broadcast_to(region_grad[region_ids][..., None], (BANDS, TILES, NBLK, BLK)).reshape(BANDS, TILES, NBLK * BLK)

    def spread_back(slots_one, grads_one):
        return jnp.zeros((HD * WD + 1,), jnp.float32).at[slots_one].add(grads_one)

    gathered = jax.vmap(jax.vmap(spread_back))(slot_index, slot_grad)[:, :, :HD * WD]
    cell_grad = gathered.reshape(BANDS, TILES, HD, WD).transpose(0, 2, 1, 3).reshape(NH, NW) * land_cells
    grad_out = to_coarse(cell_grad[:, :, None]).astype(jnp.bfloat16)
    grad_deep = project(grad_out, w_head.T).astype(jnp.bfloat16)
    slope_deep = grad_deep.astype(jnp.float32) * gelu_slope(pre_deep)
    grad_mix = (grad_deep.astype(jnp.float32) + depthwise(pad_grid(slope_deep), k_deep[::-1], row_count, col_count)).astype(jnp.bfloat16)
    grad_pre_mix = (grad_mix.astype(jnp.float32) * gelu_slope(pre_mix)).astype(jnp.bfloat16)
    grad_mixed_in = project(grad_pre_mix, w_mix.T)
    grad_first = grad_mix.astype(jnp.float32) + depthwise(pad_grid(grad_mixed_in), k_first[::-1], row_count, col_count)
    grad_pre_first = (grad_first * gelu_slope(pre_first)).astype(jnp.bfloat16)
    input_grad = to_fine(project(grad_pre_first, w_embed.T)).astype(jnp.bfloat16)
    return cell_pred, region_mean, loss_value, input_grad
```

```python
import functools

import jax
import jax.numpy as jnp
from jax import lax
from jax.experimental import pallas as pl
from jax.experimental.pallas import tpu as pltpu
from jax.sharding import PartitionSpec as P

REGIONS = 14000
SQRT_HALF = 0.7071067811865476
INV_ROOT = 0.3989422804014327
F32 = jnp.float32
BF16 = jnp.bfloat16
LANES = 128
HALO = 4
OUTSIDE = -50.0
VMEM_LIMIT = 48 * 1024 * 1024


def gelu_exact(v):
    return 0.5 * v * (1.0 + lax.erf(v * SQRT_HALF))


def gelu_slope(v):
    return 0.5 * (1.0 + lax.erf(v * SQRT_HALF)) + v * jnp.exp(-0.5 * v * v) * INV_ROOT


def rounded(v):
    return v.astype(BF16).astype(F32)


def dot(a, b):
    return jnp.dot(a, b, preferred_element_type=F32)


def dot_nt(a, b):
    return lax.dot_general(a, b, (((1,), (1,)), ((), ())), preferred_element_type=F32)


def iota(shape, dim):
    return lax.broadcasted_iota(jnp.int32, shape, dim)


def spread_matrix(cols, transposed=False):
    quarter = cols // 4
    shape = (cols, cols)
    n = iota(shape, 0)
    c = iota(shape, 1)
    return jnp.where(c == 4 * (n % quarter) + n // quarter, 1.0, 0.0).astype(BF16)


def padded_embed(w_ref, c_in, c_pad):
    w = w_ref[...].astype(F32)
    zeros = jnp.zeros((c_pad - c_in, w.shape[1]), F32)
    parts = []
    for b in range(4):
        for a in range(4):
            start = (4 * a + b) * c_in
            parts += [w[start : start + c_in], zeros]
    return jnp.concatenate(parts, axis=0).astype(BF16)


def embed_kernel(
    flags, feat, w_embed, land, blocks, pre_out, act_out, bm_out, m1_out, m2_out, hot_a, hot_b
):
    rows, c_in, cols = feat.shape
    c_pad = 32
    crows, ccols = rows // 4, cols // 4
    nblk = blocks.shape[0]
    spread = spread_matrix(cols)
    field = feat[...].astype(F32)
    field = jnp.concatenate([field, jnp.zeros((rows, c_pad - c_in, cols), F32)], axis=1)
    field = field.reshape(rows * c_pad, cols).astype(BF16)
    moved = dot_nt(spread, field).astype(BF16)
    wide = 4 * c_pad
    lhs = jnp.concatenate(
        [
            jnp.concatenate(
                [
                    moved[b * ccols : (b + 1) * ccols, i * wide : (i + 1) * wide]
                    for b in range(4)
                ],
                axis=1,
            )
            for i in range(crows)
        ],
        axis=0,
    )
    pre = dot(lhs, padded_embed(w_embed, c_in, c_pad))
    pre_out[...] = pre
    act_out[...] = gelu_exact(pre).astype(BF16).reshape(crows, ccols, pre.shape[1])

    shift_row = cols.bit_length() - 1
    chunk = next(c for c in (9, 8, 7, 6, 5, 4, 3, 2, 1) if nblk % c == 0)
    total = jnp.zeros((ccols, LANES), F32)
    sub_a = iota((LANES, LANES), 0)
    sub_b = iota((ccols, LANES), 0)
    for first in range(0, nblk, chunk):
        for step in range(chunk):
            k = first + step
            cell = blocks[k : k + 1, :]
            named = cell < rows * cols
            q = jnp.where(named, (cell & 3) * rows + (cell >> shift_row), -1)
            j = (cell & (cols - 1)) >> 2
            span = slice(step * LANES, (step + 1) * LANES)
            hot_a[:, span] = jnp.where(sub_a == q, 1.0, 0.0).astype(BF16)
            hot_b[:, span] = jnp.where(sub_b == j, float(k + 1), 0.0).astype(BF16)
        total = total + dot_nt(hot_b[...], hot_a[...])
    land_moved = dot_nt(spread, land[...].astype(F32).astype(BF16))
    land_q = jnp.concatenate(
        [land_moved[b * ccols : (b + 1) * ccols, :] for b in range(4)], axis=1
    )
    bm = total * land_q
    bm_out[...] = bm
    half = ccols // 2
    bm_wide = jnp.concatenate([bm[:half], bm[half:]], axis=1).astype(BF16)
    chan = pre.shape[1]
    odd = flags[0]
    for out, start in ((m1_out, (1 - odd) * (crows - HALO)), (m2_out, odd * (crows - HALO))):
        out[0 : HALO * ccols] = act_out[pl.ds(start, HALO)].reshape(HALO * ccols, chan)
        out[HALO * ccols :] = bm_wide


def edges_kernel(flags, act, bm, p1, p2, m1_out, m2_out):
    crows, ccols, chan = act.shape
    odd_b = flags[0] == 1
    odd_t = flags[1] == 1
    n = HALO * ccols
    up = jnp.where(odd_b, p1[...].astype(F32), p2[...].astype(F32))
    down = jnp.where(odd_b, p2[...].astype(F32), p1[...].astype(F32))
    left, right = [], []
    for r in range(crows + 2 * HALO):
        if r < HALO:
            row = up[r * ccols : (r + 1) * ccols]
        elif r < HALO + crows:
            row = act[r - HALO].astype(F32)
        else:
            row = down[(r - HALO - crows) * ccols : (r - HALO - crows + 1) * ccols]
        left.append(row[:HALO])
        right.append(row[ccols - HALO :])
    half = ccols // 2
    own = bm[...]
    zeros = jnp.zeros((10, LANES), F32)
    bm_left = [up[n : n + 2, :LANES], own[0:2], down[n : n + 2, :LANES], zeros]
    bm_right = [
        up[n + half - 2 : n + half, LANES:],
        own[ccols - 2 :],
        down[n + half - 2 : n + half, LANES:],
        zeros,
    ]
    def message(cells, maps):
        maps = jnp.concatenate(maps, axis=0)
        maps = jnp.concatenate([maps, jnp.zeros((16, chan - LANES), F32)], axis=1)
        return jnp.concatenate(cells + [maps], axis=0)

    left = message(left, bm_left)
    right = message(right, bm_right)
    m1_out[...] = jnp.where(odd_t, left, right).astype(BF16)
    m2_out[...] = jnp.where(odd_t, right, left).astype(BF16)


def conv_pass(src, count, kernel, emit, chan):
    width = src.shape[1]
    for h in range(0, chan, LANES):
        span = slice(h, h + LANES)
        taps = [kernel[t : t + 1, span] for t in range(9)]

        def body(r, carry, span=span, taps=taps):
            older, newer = carry
            x = src[r, :, span]
            before = pltpu.roll(x, 1, 0)
            after = pltpu.roll(x, width - 1, 0)
            parts = [
                taps[3 * a] * before + taps[3 * a + 1] * x + taps[3 * a + 2] * after
                for a in range(3)
            ]
            emit(jnp.maximum(r - 2, 0), span, older + parts[2])
            return newer + parts[1], parts[0]

        zero = jnp.zeros((width, LANES), F32)
        lax.fori_loop(0, count, body, (zero, zero))


def forward_kernel(
    flags, act, bm, p1, p2, t1, t2, w_mix, k_first, k_deep, wall, msg_in,
    pre_mix, pre_deep, pred_out, msg_out, field, mixed,
):
    crows, ccols, chan = act.shape
    width = ccols + 2 * HALO
    odd_b = flags[0] == 1
    odd_t = flags[1] == 1
    nrow = crows + 2 * HALO
    n = HALO * ccols
    up = jnp.where(odd_b, p1[0:n].astype(F32), p2[0:n].astype(F32))
    down = jnp.where(odd_b, p2[0:n].astype(F32), p1[0:n].astype(F32))
    m = HALO * nrow
    left = jnp.where(odd_t, t1[0:m].astype(F32), t2[0:m].astype(F32))
    right = jnp.where(odd_t, t2[0:m].astype(F32), t1[0:m].astype(F32))
    for r in range(nrow):
        if r < HALO:
            row = up[r * ccols : (r + 1) * ccols]
        elif r < HALO + crows:
            row = act[r - HALO].astype(F32)
        else:
            row = down[(r - HALO - crows) * ccols : (r - HALO - crows + 1) * ccols]
        field[r, 0:ccols, :] = row
        field[r, ccols:, :] = jnp.concatenate(
            [right[HALO * r : HALO * (r + 1)], left[HALO * r : HALO * (r + 1)]], axis=0
        )

    def keep_mixed(r, span, value):
        mixed[r, :, span] = value

    conv_pass(field, nrow, k_first[...].astype(F32), keep_mixed, chan)

    col = iota((1, width, chan), 1)
    col_ok = (col < ccols) | ((col < ccols + HALO) & (flags[5] == 0)) | (
        (col >= ccols + HALO) & (flags[4] == 0)
    )
    first_row = flags[2] * (HALO - 1)
    last_row = nrow - 2 - flags[3] * (HALO - 1)
    weights = w_mix[...]

    def mix(g, carry):
        pair = mixed[pl.ds(2 * g, 2)].reshape(2 * width, chan).astype(BF16)
        pre = dot(pair, weights).reshape(2, width, chan)
        row = iota((2, width, chan), 0) + 2 * g
        ok = col_ok & (row >= first_row) & (row < last_row)
        pre = jnp.where(ok, pre, OUTSIDE)
        pre_mix[pl.ds(2 * g, 2)] = pre
        mixed[pl.ds(2 * g, 2)] = rounded(field[pl.ds(2 * g + 1, 2)] + gelu_exact(pre))
        return carry

    lax.fori_loop(0, (nrow - 2) // 2, mix, 0)

    def keep_deep(r, span, value):
        pre_deep[r, :, span] = value

    conv_pass(mixed, nrow - 2, k_deep[...].astype(F32), keep_deep, chan)

    head = wall[...]
    head_row = (iota(head.shape, 0) % (4 * crows)) // 4

    def deep(i, pred):
        pre = pre_deep[i + 2, 0:ccols, :]
        out = (mixed[i + 3, 0:ccols, :] + gelu_exact(pre)).astype(BF16)
        return pred + dot_nt(out, jnp.where(head_row == i, head, 0.0).astype(BF16))

    pred = lax.fori_loop(0, crows, deep, jnp.zeros((ccols, LANES), F32))
    pred_out[...] = pred

    maps = bm[...]
    slots = iota((LANES, LANES), 0).astype(F32)[:88]
    sums = jnp.zeros((88, LANES), F32)
    counts = jnp.zeros((88, LANES), F32)
    for j in range(ccols):
        hit = maps[j : j + 1, :] == slots
        sums = sums + jnp.where(hit, pred[j : j + 1, :], 0.0)
        counts = counts + jnp.where(hit, 1.0, 0.0)
    msg_out[...] = msg_in[...]
    used = iota((1, LANES), 1) > 0
    rest = jnp.zeros((LANES - 88, LANES), F32)
    for at, acc in enumerate((sums, counts)):
        across = jnp.concatenate([acc, rest], axis=0).T
        msg_out[at : at + 1, :] = jnp.where(used, jnp.sum(across, axis=0, keepdims=True), 0.0)


def slope_kernel(src, out):
    out[...] = gelu_slope(src[...])


def slope_pred_kernel(src, pred, land, out, cells):
    rows, cols = land.shape
    out[...] = gelu_slope(src[...])
    turned = pred[...].T
    wide = jnp.concatenate([turned[b * rows : (b + 1) * rows] for b in range(4)], axis=1)
    high = wide.astype(BF16)
    low = (wide - high.astype(F32)).astype(BF16)
    spread = spread_matrix(cols)
    cells[...] = (dot(high, spread) + dot(low, spread)) * land[...].astype(F32)


def backward_kernel(
    flags, msgs, bm, p1, p2, t1, t2, slope_deep, slope_mix, slope_first,
    w_mix, k_first, k_deep, wall, w_embed,
    mean_out, loss_out, grad_out,
    targets, table, grads, field, mixing, proj, share_rows, share, count, loss_scale, c_in,
):
    ndev = msgs.shape[0]
    crows = slope_first.shape[0]
    ccols = slope_first.shape[1]
    chan = slope_first.shape[2]
    width = ccols + 2 * HALO
    me = flags[6]
    height = ndev * share_rows
    chunk = min(16, ndev)
    first_target = msgs.shape[1] - share_rows
    sub = iota((height, LANES), 0).astype(F32)
    sub_lo = iota((LANES, LANES), 0).astype(F32)

    def gather_chunk(c, acc):
        hot_hi, hot_lo = [], []
        for o in range(chunk):
            owner = c * chunk + o
            m = msgs[owner ^ me]
            hot_hi.append(jnp.where(sub == m[2:3], 1.0, 0.0).astype(BF16))
            low_hit = sub_lo == m[3:4]
            high = rounded(m[0:1])
            parts = [high, m[0:1] - high, m[1:2]]
            hot_lo.append(
                jnp.concatenate(
                    [jnp.where(low_hit, part, 0.0).astype(BF16) for part in parts], axis=0
                )
            )
            targets[pl.ds(owner * share_rows, share_rows)] = m[first_target:]
        return acc + dot_nt(
            jnp.concatenate(hot_hi, axis=1), jnp.concatenate(hot_lo, axis=1)
        )

    acc = jnp.zeros((height, 3 * LANES), F32)
    if ndev == chunk:
        acc = gather_chunk(0, acc)
    else:
        acc = lax.fori_loop(0, ndev // chunk, gather_chunk, acc)
    region_sum = acc[:, :LANES] + acc[:, LANES : 2 * LANES]
    region_count = acc[:, 2 * LANES :]
    at_least = jnp.maximum(region_count, 1.0)
    mean = region_sum / at_least
    table[...] = mean
    misfit = mean - targets[...]
    row = iota((height, LANES), 0)
    place = (row % share_rows) * LANES + iota((height, LANES), 1)
    inside = (place < share) & ((row // share_rows) * share + place < REGIONS)
    terms = jnp.where(inside, region_count * misfit * misfit, 0.0)
    loss_out[...] = jnp.sum(
        jnp.sum(terms, axis=0, keepdims=True), axis=1, keepdims=True
    ) * loss_scale
    grads[...] = jnp.where(inside, region_count * misfit / at_least, 0.0)
    mean_out[...] = table[pl.ds(me * share_rows, share_rows)]

    sub8 = iota((8, LANES), 0).astype(F32)

    def block_grads(slot):
        m = msgs[slot]
        low = jnp.broadcast_to(jnp.maximum(m[3:4], 0.0), (8, LANES)).astype(jnp.int32)
        high = m[2:3]
        total = jnp.zeros((8, LANES), F32)
        for at in range(0, height, 8):
            found = jnp.take_along_axis(grads[at : at + 8], low, axis=1)
            total = total + jnp.where(high == sub8 + float(at), found, 0.0)
        return jnp.sum(total, axis=0, keepdims=True)

    n = HALO * ccols
    half = ccols // 2
    odd_b = flags[0] == 1
    odd_t = flags[1] == 1
    up = jnp.where(odd_b, p1[n:].astype(F32), p2[n:].astype(F32))
    down = jnp.where(odd_b, p2[n:].astype(F32), p1[n:].astype(F32))
    m = HALO * (crows + 2 * HALO)
    left = jnp.where(odd_t, t1[m:].astype(F32), t2[m:].astype(F32))[:, :LANES]
    right = jnp.where(odd_t, t2[m:].astype(F32), t1[m:].astype(F32))[:, :LANES]
    maps = [
        jnp.concatenate([up[:, :LANES], up[:, LANES:]], axis=0),
        bm[...],
        jnp.concatenate([down[:, :LANES], down[:, LANES:]], axis=0),
    ]
    cells = []
    gap = jnp.zeros((4, LANES), F32)
    for v in range(3):
        mid = block_grads(flags[8 + 3 * v + 1])
        lo = block_grads(flags[8 + 3 * v])
        hi = block_grads(flags[8 + 3 * v + 2])
        source = jnp.broadcast_to(mid, (8, LANES))
        parts = [
            jnp.take_along_axis(source, maps[v][at : at + 8].astype(jnp.int32), axis=1)
            for at in range(0, ccols, 8)
        ]
        edge = jnp.concatenate(
            [right[2 * v : 2 * v + 2], gap, left[2 * v : 2 * v + 2]], axis=0
        ).astype(jnp.int32)
        source = jnp.concatenate(
            [jnp.broadcast_to(hi, (4, LANES)), jnp.broadcast_to(lo, (4, LANES))], axis=0
        )
        parts.append(jnp.take_along_axis(source, edge, axis=1))
        cells.append(jnp.concatenate(parts, axis=0).astype(BF16))

    head = wall[...]
    head_row = (iota(head.shape, 0) % (4 * crows)) // 4
    nrow = crows + 4
    for r in range(nrow):
        v = 0 if r < 2 else 1 if r < crows + 2 else 2
        i = (crows - 2 + r) if v == 0 else (r - 2) if v == 1 else r - crows - 2
        weights = jnp.where(head_row == i, head, 0.0).astype(BF16)
        deep = rounded(dot(cells[v], weights))
        mixing[r] = deep
        field[r] = deep * slope_deep[r]

    def keep_mix(r, span, value):
        mixing[r + 1, :, span] = rounded(mixing[r + 1, :, span] + value)

    def reversed_taps(k):
        k = k[...].astype(F32)
        return jnp.concatenate([k[t : t + 1] for t in range(8, -1, -1)], axis=0)

    def first_pass():
        kernel = reversed_taps(k_deep)
        for h in range(0, chan, LANES):
            span = slice(h, h + LANES)
            taps = [kernel[t : t + 1, span] for t in range(9)]

            def parts_of(r):
                x = field[r, :, span]
                before = pltpu.roll(x, 1, 0)
                after = pltpu.roll(x, width - 1, 0)
                return [
                    taps[3 * a] * before + taps[3 * a + 1] * x + taps[3 * a + 2] * after
                    for a in range(3)
                ]

            def body(r, carry):
                older, newer = carry
                p = parts_of(r)
                keep_mix(r - 2, span, older + p[2])
                return newer + p[1], p[0]

            a = parts_of(0)
            b = parts_of(1)
            lax.fori_loop(2, nrow, body, (a[0] + b[1], b[0]))

    first_pass()
    weights = w_mix[...]

    def unmix(g, carry):
        pre = (mixing[pl.ds(2 * g + 1, 2)] * slope_mix[pl.ds(2 * g + 2, 2)]).reshape(
            2 * width, chan
        )
        field[pl.ds(2 * g, 2)] = dot_nt(pre.astype(BF16), weights).reshape(2, width, chan)
        return carry

    lax.fori_loop(0, (nrow - 2) // 2, unmix, 0)

    def keep_first(r, span, value):
        total = mixing[r + 2, 0:ccols, span] + value[0:ccols]
        proj[r, :, span] = (total * slope_first[r, :, span]).astype(BF16)

    conv_pass(field, nrow - 2, reversed_taps(k_first), keep_first, chan)

    c_pad = 32
    out = dot_nt(
        padded_embed(w_embed, c_in, c_pad), proj[...].reshape(crows * ccols, chan)
    ).astype(BF16)
    wide = 4 * c_pad
    lhs = jnp.concatenate(
        [
            jnp.concatenate(
                [
                    out[b * wide : (b + 1) * wide, i * ccols : (i + 1) * ccols]
                    for b in range(4)
                ],
                axis=1,
            )
            for i in range(crows)
        ],
        axis=0,
    )
    fine = dot(lhs, spread_matrix(4 * ccols))
    for r in range(4 * crows):
        grad_out[r] = fine[r * c_pad : r * c_pad + c_in].astype(BF16)


def call(kernel, outs, scratch=(), flops=10**6, smem=True):
    def run(*args):
        space = [pl.BlockSpec(memory_space=pltpu.VMEM)] * len(args)
        if smem:
            space[0] = pl.BlockSpec(memory_space=pltpu.SMEM)
        return pl.pallas_call(
            kernel,
            out_shape=[jax.ShapeDtypeStruct(s, d) for s, d in outs],
            in_specs=space,
            out_specs=[pl.BlockSpec(memory_space=pltpu.VMEM)] * len(outs),
            scratch_shapes=[pltpu.VMEM(s, d) for s, d in scratch],
            compiler_params=pltpu.CompilerParams(vmem_limit_bytes=VMEM_LIMIT),
            cost_estimate=pl.CostEstimate(flops=flops, bytes_accessed=10**6, transcendentals=0),
        )(*args)

    return run


def exchange(m1, m2, axis):
    size = lax.axis_size(axis)
    even = [(i, i + 1) for i in range(0, size - 1, 2)]
    odd = [(i, i + 1) for i in range(1, size - 1, 2)]
    both = lambda pairs: pairs + [(j, i) for i, j in pairs]
    return lax.ppermute(m1, axis, both(even)), lax.ppermute(m2, axis, both(odd))


def per_device(
    features, land_mask, cell_blocks, region_ids, targets, w_embed, k_first, w_mix, k_deep, w_head
):
    rows, cols = land_mask.shape
    crows, ccols = rows // 4, cols // 4
    c_in = features.shape[2]
    chan = w_embed.shape[1]
    width = ccols + 2 * HALO
    nblk = cell_blocks.shape[-2]
    bands, tiles = lax.axis_size("band"), lax.axis_size("tile")
    band, tile = lax.axis_index("band"), lax.axis_index("tile")
    ndev = bands * tiles
    share = targets.shape[0]
    share_rows = pl.next_power_of_2(pl.cdiv(share, LANES))
    msg_rows = pl.cdiv(4 + share_rows, 8) * 8
    me = tile * bands + band

    slots = []
    for v in (-1, 0, 1):
        for t in (-1, 0, 1):
            nb, nt = band + v, tile + t
            ok = (nb >= 0) & (nb < bands) & (nt >= 0) & (nt < tiles)
            slots.append(jnp.where(ok, (nt * bands + nb) ^ me, 0))
    flags = jnp.stack(
        [
            band % 2, tile % 2, band == 0, band == bands - 1, tile == 0, tile == tiles - 1, me, me,
        ]
        + slots
    ).astype(jnp.int32)

    rid = region_ids.reshape(1, nblk)
    owner, place = rid // share, rid % share
    pad = ((0, 0), (1, LANES - 1 - nblk))
    high = jnp.pad(owner * share_rows + place // LANES, pad, constant_values=-1)
    low = jnp.pad(place % LANES, pad, constant_values=-1)
    blank = jnp.zeros((1, LANES), F32)
    tgt = jnp.pad(targets, (0, share_rows * LANES - share)).reshape(share_rows, LANES)
    msg_in = jnp.concatenate(
        [blank, blank, high.astype(F32), low.astype(F32)]
        + [jnp.zeros((msg_rows - 4 - share_rows, LANES), F32), tgt],
        axis=0,
    )
    head = w_head.T.reshape(4, 4, chan).transpose(1, 0, 2).astype(F32)
    wall = jnp.broadcast_to(head[:, None], (4, crows, 4, chan)).reshape(16 * crows, chan)

    feat = features.transpose(0, 2, 1)
    msg1 = HALO * ccols + ccols // 2
    pre_first, act, bm, m1, m2 = call(
        embed_kernel,
        [
            ((crows * ccols, chan), F32),
            ((crows, ccols, chan), BF16),
            ((ccols, LANES), F32),
            ((msg1, chan), BF16),
            ((msg1, chan), BF16),
        ],
        [((LANES, 9 * LANES), BF16), ((ccols, 9 * LANES), BF16)],
    )(flags, feat, w_embed, land_mask, cell_blocks.reshape(nblk, LANES))
    p1, p2 = exchange(m1, m2, "band")
    msg2 = HALO * (crows + 2 * HALO) + 16
    m1, m2 = call(edges_kernel, [((msg2, chan), BF16)] * 2)(flags, act, bm, p1, p2)
    t1, t2 = exchange(m1, m2, "tile")
    nrow = crows + 2 * HALO
    pre_mix, pre_deep, pred, msg = call(
        forward_kernel,
        [
            ((nrow - 2, width, chan), F32),
            ((nrow - 4, width, chan), F32),
            ((ccols, LANES), F32),
            ((msg_rows, LANES), F32),
        ],
        [((nrow, width, chan), F32), ((nrow - 2, width, chan), F32)],
    )(flags, act, bm, p1, p2, t1, t2, w_mix, k_first, k_deep, wall, msg_in)

    (slope_first,) = call(slope_kernel, [((crows * ccols, chan), F32)], smem=False)(pre_first)
    (slope_mix,) = call(slope_kernel, [((nrow - 2, width, chan), F32)], smem=False)(pre_mix)
    slope_deep, cell_pred = call(
        slope_pred_kernel, [((nrow - 4, width, chan), F32), ((rows, cols), F32)], smem=False
    )(pre_deep, pred, land_mask)

    msgs = msg[None]
    for axis, size in (("band", bands), ("tile", tiles)):
        step = 1
        while step < size:
            other = lax.ppermute(msgs, axis, [(i, i ^ step) for i in range(size)])
            msgs = jnp.concatenate([msgs, other], axis=0)
            step *= 2

    height = ndev * share_rows
    mean, loss, grad = call(
        functools.partial(
            backward_kernel,
            share_rows=share_rows,
            share=share,
            count=ndev,
            loss_scale=1.0 / (2.0 * rows * cols * ndev),
            c_in=c_in,
        ),
        [((share_rows, LANES), F32), ((1, 1), F32), ((rows, c_in, cols), BF16)],
        [
            ((height, LANES), F32),
            ((height, LANES), F32),
            ((height, LANES), F32),
            ((nrow - 4, width, chan), F32),
            ((nrow - 4, width, chan), F32),
            ((crows, ccols, chan), BF16),
        ],
    )(
        flags, msgs, bm, p1, p2, t1, t2, slope_deep, slope_mix,
        slope_first.reshape(crows, ccols, chan), w_mix, k_first, k_deep, wall, w_embed,
    )
    return (
        cell_pred,
        mean.reshape(-1)[:share],
        loss.reshape(1),
        grad.transpose(0, 2, 1),
    )


def solution(mesh):
    in_specs = (
        P(("group", "band"), "tile", None),
        P("band", "tile"),
        P("band", "tile", None, None),
        P("band", "tile", None),
        P(("group", "tile", "band")),
        P(),
        P(),
        P(),
        P(),
        P(),
    )
    out_specs = (
        P(("group", "band"), "tile"),
        P(("group", "tile", "band")),
        P("group"),
        P(("group", "band"), "tile", None),
    )
    return jax.shard_map(
        per_device, mesh=mesh, in_specs=in_specs, out_specs=out_specs, check_vma=False
    )
```

```python
import functools

import jax
import jax.numpy as jnp
from jax import lax
from jax.experimental import pallas as pl
from jax.experimental.pallas import tpu as pltpu
from jax.sharding import PartitionSpec as P

REGIONS = 14000
SQRT_HALF = 0.7071067811865476
INV_ROOT = 0.3989422804014327
F32 = jnp.float32
BF16 = jnp.bfloat16
LANES = 128
HALO = 4
OUTSIDE = -50.0
VMEM_LIMIT = 48 * 1024 * 1024


def gelu_exact(v):
    return 0.5 * v * (1.0 + lax.erf(v * SQRT_HALF))


def gelu_slope(v):
    return 0.5 * (1.0 + lax.erf(v * SQRT_HALF)) + v * jnp.exp(-0.5 * v * v) * INV_ROOT


def rounded(v):
    return v.astype(BF16).astype(F32)


def dot(a, b):
    return jnp.dot(a, b, preferred_element_type=F32)


def dot_nt(a, b):
    return lax.dot_general(a, b, (((1,), (1,)), ((), ())), preferred_element_type=F32)


def iota(shape, dim):
    return lax.broadcasted_iota(jnp.int32, shape, dim)


def spread_matrix(cols, transposed=False):
    quarter = cols // 4
    shape = (cols, cols)
    n = iota(shape, 0)
    c = iota(shape, 1)
    return jnp.where(c == 4 * (n % quarter) + n // quarter, 1.0, 0.0).astype(BF16)


def padded_embed(w_ref, c_in, c_pad):
    w = w_ref[...].astype(F32)
    zeros = jnp.zeros((c_pad - c_in, w.shape[1]), F32)
    parts = []
    for b in range(4):
        for a in range(4):
            start = (4 * a + b) * c_in
            parts += [w[start : start + c_in], zeros]
    return jnp.concatenate(parts, axis=0).astype(BF16)


def parity(axis):
    return lax.axis_index(axis) % 2


def embed_kernel(
    feat_hbm, w_hbm, land_hbm, blocks_hbm, pre_out, act_out, bm_out, m1_out, m2_out, w_out,
    feat, w_embed, land, blocks, hot_a, hot_b, sems,
):
    pairs = ((blocks_hbm, blocks), (land_hbm, land), (feat_hbm, feat), (w_hbm, w_embed))
    copies = [pltpu.make_async_copy(src, dst, sems.at[n]) for n, (src, dst) in enumerate(pairs)]
    for copy in copies:
        copy.start()
    rows, c_in, cols = feat.shape
    c_pad = 32
    crows, ccols = rows // 4, cols // 4
    nblk = blocks.shape[0]
    spread = spread_matrix(cols)

    copies[0].wait()
    shift_row = cols.bit_length() - 1
    chunk = hot_a.shape[1] // LANES
    total = jnp.zeros((ccols, LANES), F32)
    sub_a = iota((LANES, LANES), 0)
    sub_b = iota((ccols, LANES), 0)
    for first in range(0, nblk, chunk):
        for step in range(chunk):
            k = first + step
            cell = blocks[k]
            named = cell < rows * cols
            q = jnp.where(named, (cell & 3) * rows + (cell >> shift_row), -1)
            j = (cell & (cols - 1)) >> 2
            span = slice(step * LANES, (step + 1) * LANES)
            hot_a[:, span] = jnp.where(sub_a == q, 1.0, 0.0).astype(BF16)
            hot_b[:, span] = jnp.where(sub_b == j, float(k + 1), 0.0).astype(BF16)
        total = total + dot_nt(hot_b[...], hot_a[...])
    copies[1].wait()
    land_moved = dot_nt(spread, land[...].astype(F32).astype(BF16))
    land_q = jnp.concatenate(
        [land_moved[b * ccols : (b + 1) * ccols, :] for b in range(4)], axis=1
    )
    bm = total * land_q
    bm_out[...] = bm

    copies[2].wait()
    copies[3].wait()
    field = feat[...].astype(F32)
    field = jnp.concatenate([field, jnp.zeros((rows, c_pad - c_in, cols), F32)], axis=1)
    field = field.reshape(rows * c_pad, cols).astype(BF16)
    moved = dot_nt(spread, field).astype(BF16)
    wide = 4 * c_pad
    lhs = jnp.concatenate(
        [
            jnp.concatenate(
                [
                    moved[b * ccols : (b + 1) * ccols, i * wide : (i + 1) * wide]
                    for b in range(4)
                ],
                axis=1,
            )
            for i in range(crows)
        ],
        axis=0,
    )
    weights = padded_embed(w_embed, c_in, c_pad)
    w_out[...] = weights
    pre = dot(lhs, weights)
    chan = pre.shape[1]
    pre_out[...] = pre
    act_out[...] = gelu_exact(pre).astype(BF16).reshape(crows, ccols, chan)
    half = ccols // 2
    bm_wide = jnp.concatenate([bm[:half], bm[half:]], axis=1).astype(BF16)
    odd = parity("band")
    for out, start in ((m1_out, (1 - odd) * (crows - HALO)), (m2_out, odd * (crows - HALO))):
        out[0 : HALO * ccols] = act_out[pl.ds(start, HALO)].reshape(HALO * ccols, chan)
        out[HALO * ccols :] = bm_wide


def edges_kernel(act, bm, p1, p2, m1_out, m2_out):
    crows, ccols, chan = act.shape
    odd_b = parity("band") == 1
    odd_t = parity("tile") == 1
    n = HALO * ccols
    up = jnp.where(odd_b, p1[...].astype(F32), p2[...].astype(F32))
    down = jnp.where(odd_b, p2[...].astype(F32), p1[...].astype(F32))
    left, right = [], []
    for r in range(crows + 2 * HALO):
        if r < HALO:
            row = up[r * ccols : (r + 1) * ccols]
        elif r < HALO + crows:
            row = act[r - HALO].astype(F32)
        else:
            row = down[(r - HALO - crows) * ccols : (r - HALO - crows + 1) * ccols]
        left.append(row[:HALO])
        right.append(row[ccols - HALO :])
    half = ccols // 2
    own = bm[...]
    zeros = jnp.zeros((10, LANES), F32)
    bm_left = [up[n : n + 2, :LANES], own[0:2], down[n : n + 2, :LANES], zeros]
    bm_right = [
        up[n + half - 2 : n + half, LANES:],
        own[ccols - 2 :],
        down[n + half - 2 : n + half, LANES:],
        zeros,
    ]
    def message(cells, maps):
        maps = jnp.concatenate(maps, axis=0)
        maps = jnp.concatenate([maps, jnp.zeros((16, chan - LANES), F32)], axis=1)
        return jnp.concatenate(cells + [maps], axis=0)

    left = message(left, bm_left)
    right = message(right, bm_right)
    m1_out[...] = jnp.where(odd_t, left, right).astype(BF16)
    m2_out[...] = jnp.where(odd_t, right, left).astype(BF16)


def conv_pass(src, count, kernel, emit, chan):
    width = src.shape[1]
    for h in range(0, chan, LANES):
        span = slice(h, h + LANES)
        taps = [kernel[t : t + 1, span] for t in range(9)]

        def body(r, carry, span=span, taps=taps):
            older, newer = carry
            x = src[r, :, span]
            before = pltpu.roll(x, 1, 0)
            after = pltpu.roll(x, width - 1, 0)
            parts = [
                taps[3 * a] * before + taps[3 * a + 1] * x + taps[3 * a + 2] * after
                for a in range(3)
            ]
            emit(jnp.maximum(r - 2, 0), span, older + parts[2])
            return newer + parts[1], parts[0]

        zero = jnp.zeros((width, LANES), F32)
        lax.fori_loop(0, count, body, (zero, zero))


def halo_rows(act, p1, p2, t1, t2):
    crows, ccols, chan = act.shape
    odd_b = parity("band") == 1
    odd_t = parity("tile") == 1

    def edge(first, second, odd, at, n):
        return jnp.where(odd, first[at : at + n].astype(F32), second[at : at + n].astype(F32))

    def row(r):
        if r < HALO:
            own = edge(p1, p2, odd_b, r * ccols, ccols)
        elif r < HALO + crows:
            own = act[r - HALO].astype(F32)
        else:
            own = edge(p2, p1, odd_b, (r - HALO - crows) * ccols, ccols)
        base = HALO * r // 16 * 16
        at = HALO * r - base
        left = edge(t1, t2, odd_t, base, 16)[at : at + HALO]
        right = edge(t2, t1, odd_t, base, 16)[at : at + HALO]
        return own, jnp.concatenate([right, left], axis=0)

    return row


def inside_columns(shape, ccols):
    tile = lax.axis_index("tile")
    first = tile == 0
    last = tile == lax.axis_size("tile") - 1
    col = iota(shape, len(shape) - 2)
    low = jnp.where(last, ccols, ccols + HALO)
    high = jnp.where(first, ccols + 2 * HALO, ccols + HALO)
    return (col < low) | (col >= high)


def mix_pair(pair, base, weights, ok):
    _, width, chan = pair.shape
    pre = dot(pair.reshape(2 * width, chan).astype(BF16), weights).reshape(2, width, chan)
    pre = jnp.where(ok, pre, OUTSIDE)
    return pre, rounded(base + gelu_exact(pre))


def forward_kernel(
    act, bm, p1, p2, t1, t2, w_mix, k_first, k_deep, wall, msg_in,
    field, act_mix, pre_mix, pre_deep, pred_out, msg_out, mixed,
):
    crows, ccols, chan = act.shape
    width = ccols + 2 * HALO
    row = halo_rows(act, p1, p2, t1, t2)
    for r in range(crows + 4):
        own, edge = row(r + 2)
        field[r, 0:ccols, :] = own
        field[r, ccols:, :] = edge

    def keep_mixed(r, span, value):
        mixed[r, :, span] = value

    conv_pass(field, crows + 4, k_first[...].astype(F32), keep_mixed, chan)

    shape = (2, width, chan)
    col_ok = inside_columns(shape, ccols)
    band = lax.axis_index("band")
    first_row = jnp.where(band == 0, 1, 0)
    last_row = jnp.where(band == lax.axis_size("band") - 1, crows + 1, crows + 2)
    weights = w_mix[...]
    for g in range((crows + 2) // 2):
        at = iota(shape, 0) + 2 * g
        ok = col_ok & (at >= first_row) & (at < last_row)
        pair = slice(2 * g, 2 * g + 2)
        pre, post = mix_pair(mixed[pair], field[2 * g + 1 : 2 * g + 3], weights, ok)
        pre_mix[pair] = pre
        act_mix[pair] = post

    def keep_deep(r, span, value):
        pre_deep[r, :, span] = value

    conv_pass(act_mix, crows + 2, k_deep[...].astype(F32), keep_deep, chan)

    head = wall[...]
    head_row = (iota(head.shape, 0) % (4 * crows)) // 4
    pred = jnp.zeros((ccols, LANES), F32)
    for i in range(crows):
        out = act_mix[i + 1, 0:ccols, :] + gelu_exact(pre_deep[i, 0:ccols, :])
        pred = pred + dot_nt(
            out.astype(BF16), jnp.where(head_row == i, head, 0.0).astype(BF16)
        )
    pred_out[...] = pred

    maps = bm[...]
    slots = iota((LANES, LANES), 0).astype(F32)[:88]
    sums = jnp.zeros((88, LANES), F32)
    for j in range(ccols):
        sums = sums + jnp.where(maps[j : j + 1, :] == slots, pred[j : j + 1, :], 0.0)
    msg_out[...] = msg_in[...]
    msg_out[0:1, :] = across_lanes(sums)


def across_lanes(acc):
    rest = jnp.zeros((LANES - acc.shape[0], LANES), F32)
    turned = jnp.concatenate([acc, rest], axis=0).T
    total = jnp.sum(turned, axis=0, keepdims=True)
    return jnp.where(iota((1, LANES), 1) > 0, total, 0.0)


def count_kernel(pre_first, bm, msg_in, slope_first, msg_out):
    slope_first[...] = gelu_slope(pre_first[...])
    maps = bm[...]
    slots = iota((LANES, LANES), 0).astype(F32)[:88]
    counts = jnp.zeros((88, LANES), F32)
    for j in range(maps.shape[0]):
        counts = counts + jnp.where(maps[j : j + 1, :] == slots, 1.0, 0.0)
    msg_out[...] = msg_in[...]
    msg_out[1:2, :] = across_lanes(counts)


def rim_kernel(
    after, act, p1, p2, t1, t2, w_mix, k_first, k_deep, field, act_mix, slope_rim,
    ext, mixed,
):
    del after
    crows, ccols, chan = act.shape
    width = ccols + 2 * HALO
    row = halo_rows(act, p1, p2, t1, t2)
    first, second = k_first[...].astype(F32), k_deep[...].astype(F32)
    weights = w_mix[...]
    shape = (2, width, chan)
    col_ok = inside_columns(shape, ccols)
    band = lax.axis_index("band")
    for side in range(2):
        outer = (0, 1) if side == 0 else (crows + 6, crows + 7)
        inner = (0, 1) if side == 0 else (crows + 2, crows + 3)
        spots = (0, 1) if side == 0 else (2, 3)
        for r, at in zip(outer, spots):
            own, edge = row(r)
            ext[at, 0:ccols, :] = own
            ext[at, ccols:, :] = edge
        for r, at in zip(inner, (2, 3) if side == 0 else (0, 1)):
            ext[at] = field[r]

        def keep_mixed(r, span, value):
            mixed[r, :, span] = value

        conv_pass(ext, 4, first, keep_mixed, chan)
        edge_band = 0 if side == 0 else lax.axis_size("band") - 1
        ok = col_ok & (band != edge_band)
        _, post = mix_pair(mixed[...], ext[1:3], weights, ok)
        have = (0, 1) if side == 0 else (crows, crows + 1)
        for n in range(2):
            ext[spots[n]] = post[n]
            ext[(2, 3)[n] if side == 0 else n] = act_mix[have[n]]

        def keep_deep(r, span, value):
            mixed[r, :, span] = value

        conv_pass(ext, 4, second, keep_deep, chan)
        slope_rim[2 * side : 2 * side + 2] = gelu_slope(mixed[...])


def slope_kernel(after, src, out):
    del after
    out[...] = gelu_slope(src[...])


def slope_pred_kernel(after, src, pred, land, out, cells):
    del after
    rows, cols = land.shape
    out[...] = gelu_slope(src[...])
    turned = pred[...].T
    wide = jnp.concatenate([turned[b * rows : (b + 1) * rows] for b in range(4)], axis=1)
    high = wide.astype(BF16)
    low = (wide - high.astype(F32)).astype(BF16)
    spread = spread_matrix(cols)
    cells[...] = (dot(high, spread) + dot(low, spread)) * land[...].astype(F32)


def backward_kernel(
    msgs, bm, p1, p2, t1, t2, slope_deep, slope_rim, slope_mix, slope_first,
    w_mix, k_first, k_deep, wall, w_wide,
    mean_out, loss_out, grad_out,
    targets, table, grads, field, mixing, proj, share_rows, share, loss_scale, c_in,
):
    ndev = msgs.shape[0]
    crows = slope_first.shape[0]
    ccols = slope_first.shape[1]
    chan = slope_first.shape[2]
    width = ccols + 2 * HALO
    band, tile = lax.axis_index("band"), lax.axis_index("tile")
    bands, tiles = lax.axis_size("band"), lax.axis_size("tile")
    me = tile * bands + band

    def slot_of(v, t):
        other_band, other_tile = band + v, tile + t
        ok = (other_band >= 0) & (other_band < bands) & (other_tile >= 0) & (other_tile < tiles)
        return jnp.where(ok, (other_tile * bands + other_band) ^ me, 0)

    height = ndev * share_rows
    chunk = min(16, ndev)
    first_target = msgs.shape[1] - share_rows
    sub = iota((height, LANES), 0).astype(F32)
    sub_lo = iota((LANES, LANES), 0).astype(F32)

    def gather_chunk(c, acc):
        hot_hi, hot_lo = [], []
        for o in range(chunk):
            owner = c * chunk + o
            m = msgs[owner ^ me]
            hot_hi.append(jnp.where(sub == m[2:3], 1.0, 0.0).astype(BF16))
            low_hit = sub_lo == m[3:4]
            high = rounded(m[0:1])
            parts = [high, m[0:1] - high, m[1:2]]
            hot_lo.append(
                jnp.concatenate(
                    [jnp.where(low_hit, part, 0.0).astype(BF16) for part in parts], axis=0
                )
            )
            targets[pl.ds(owner * share_rows, share_rows)] = m[first_target:]
        return acc + dot_nt(
            jnp.concatenate(hot_hi, axis=1), jnp.concatenate(hot_lo, axis=1)
        )

    acc = jnp.zeros((height, 3 * LANES), F32)
    if ndev == chunk:
        acc = gather_chunk(0, acc)
    else:
        acc = lax.fori_loop(0, ndev // chunk, gather_chunk, acc)
    region_sum = acc[:, :LANES] + acc[:, LANES : 2 * LANES]
    region_count = acc[:, 2 * LANES :]
    at_least = jnp.maximum(region_count, 1.0)
    mean = region_sum / at_least
    table[...] = mean
    misfit = mean - targets[...]
    row = iota((height, LANES), 0)
    place = (row % share_rows) * LANES + iota((height, LANES), 1)
    inside = (place < share) & ((row // share_rows) * share + place < REGIONS)
    terms = jnp.where(inside, region_count * misfit * misfit, 0.0)
    loss_out[...] = jnp.sum(
        jnp.sum(terms, axis=0, keepdims=True), axis=1, keepdims=True
    ) * loss_scale
    grads[...] = jnp.where(inside, region_count * misfit / at_least, 0.0)
    mean_out[...] = table[pl.ds(me * share_rows, share_rows)]

    sub8 = iota((8, LANES), 0).astype(F32)

    def block_grads(slot):
        m = msgs[slot]
        low = jnp.broadcast_to(jnp.maximum(m[3:4], 0.0), (8, LANES)).astype(jnp.int32)
        high = m[2:3]
        total = jnp.zeros((8, LANES), F32)
        for at in range(0, height, 8):
            found = jnp.take_along_axis(grads[at : at + 8], low, axis=1)
            total = total + jnp.where(high == sub8 + float(at), found, 0.0)
        return jnp.sum(total, axis=0, keepdims=True)

    n = HALO * ccols
    half = ccols // 2
    odd_b = parity("band") == 1
    odd_t = parity("tile") == 1
    up = jnp.where(odd_b, p1[n:].astype(F32), p2[n:].astype(F32))
    down = jnp.where(odd_b, p2[n:].astype(F32), p1[n:].astype(F32))
    m = HALO * (crows + 2 * HALO)
    left = jnp.where(odd_t, t1[m:].astype(F32), t2[m:].astype(F32))[:, :LANES]
    right = jnp.where(odd_t, t2[m:].astype(F32), t1[m:].astype(F32))[:, :LANES]
    maps = [
        jnp.concatenate([up[:, :LANES], up[:, LANES:]], axis=0),
        bm[...],
        jnp.concatenate([down[:, :LANES], down[:, LANES:]], axis=0),
    ]
    cells = []
    gap = jnp.zeros((4, LANES), F32)
    for v in range(3):
        mid = block_grads(slot_of(v - 1, 0))
        lo = block_grads(slot_of(v - 1, -1))
        hi = block_grads(slot_of(v - 1, 1))
        source = jnp.broadcast_to(mid, (8, LANES))
        parts = [
            jnp.take_along_axis(source, maps[v][at : at + 8].astype(jnp.int32), axis=1)
            for at in range(0, ccols, 8)
        ]
        edge = jnp.concatenate(
            [right[2 * v : 2 * v + 2], gap, left[2 * v : 2 * v + 2]], axis=0
        ).astype(jnp.int32)
        source = jnp.concatenate(
            [jnp.broadcast_to(hi, (4, LANES)), jnp.broadcast_to(lo, (4, LANES))], axis=0
        )
        parts.append(jnp.take_along_axis(source, edge, axis=1))
        cells.append(jnp.concatenate(parts, axis=0).astype(BF16))

    head = wall[...]
    head_row = (iota(head.shape, 0) % (4 * crows)) // 4
    nrow = crows + 4
    for r in range(nrow):
        v = 0 if r < 2 else 1 if r < crows + 2 else 2
        i = (crows - 2 + r) if v == 0 else (r - 2) if v == 1 else r - crows - 2
        weights = jnp.where(head_row == i, head, 0.0).astype(BF16)
        deep = rounded(dot(cells[v], weights))
        mixing[r] = deep
        slope = slope_rim[r] if v == 0 else slope_deep[i] if v == 1 else slope_rim[r - crows]
        field[r] = deep * slope

    def keep_mix(r, span, value):
        mixing[r + 1, :, span] = rounded(mixing[r + 1, :, span] + value)

    def reversed_taps(k):
        k = k[...].astype(F32)
        return jnp.concatenate([k[t : t + 1] for t in range(8, -1, -1)], axis=0)

    def first_pass():
        kernel = reversed_taps(k_deep)
        for h in range(0, chan, LANES):
            span = slice(h, h + LANES)
            taps = [kernel[t : t + 1, span] for t in range(9)]

            def parts_of(r):
                x = field[r, :, span]
                before = pltpu.roll(x, 1, 0)
                after = pltpu.roll(x, width - 1, 0)
                return [
                    taps[3 * a] * before + taps[3 * a + 1] * x + taps[3 * a + 2] * after
                    for a in range(3)
                ]

            def body(r, carry):
                older, newer = carry
                p = parts_of(r)
                keep_mix(r - 2, span, older + p[2])
                return newer + p[1], p[0]

            a = parts_of(0)
            b = parts_of(1)
            lax.fori_loop(2, nrow, body, (a[0] + b[1], b[0]))

    first_pass()
    weights = w_mix[...]

    for g in range((nrow - 2) // 2):
        pre = (mixing[2 * g + 1 : 2 * g + 3] * slope_mix[2 * g : 2 * g + 2]).reshape(
            2 * width, chan
        )
        field[2 * g : 2 * g + 2] = dot_nt(pre.astype(BF16), weights).reshape(2, width, chan)

    def keep_first(r, span, value):
        total = mixing[r + 2, 0:ccols, span] + value[0:ccols]
        proj[r, :, span] = (total * slope_first[r, :, span]).astype(BF16)

    conv_pass(field, nrow - 2, reversed_taps(k_first), keep_first, chan)

    c_pad = 32
    out = dot_nt(w_wide[...], proj[...].reshape(crows * ccols, chan)).astype(BF16)
    wide = 4 * c_pad
    lhs = jnp.concatenate(
        [
            jnp.concatenate(
                [
                    out[b * wide : (b + 1) * wide, i * ccols : (i + 1) * ccols]
                    for b in range(4)
                ],
                axis=1,
            )
            for i in range(crows)
        ],
        axis=0,
    )
    fine = dot(lhs, spread_matrix(4 * ccols))
    for r in range(4 * crows):
        grad_out[r] = fine[r * c_pad : r * c_pad + c_in].astype(BF16)


def call(kernel, outs, scratch=(), hbm=0):
    def run(*args):
        space = [pl.BlockSpec(memory_space=pl.ANY)] * hbm
        space += [pl.BlockSpec(memory_space=pltpu.VMEM)] * (len(args) - hbm)
        return pl.pallas_call(
            kernel,
            out_shape=[jax.ShapeDtypeStruct(s, d) for s, d in outs],
            in_specs=space,
            out_specs=[pl.BlockSpec(memory_space=pltpu.VMEM)] * len(outs),
            scratch_shapes=[
                pltpu.SemaphoreType.DMA(s) if d is None else pltpu.VMEM(s, d)
                for s, d in scratch
            ],
            compiler_params=pltpu.CompilerParams(vmem_limit_bytes=VMEM_LIMIT),
            cost_estimate=pl.CostEstimate(
                flops=10**6, bytes_accessed=10**6, transcendentals=0
            ),
        )(*args)

    return run


def exchange(m1, m2, axis):
    size = lax.axis_size(axis)
    even = [(i, i + 1) for i in range(0, size - 1, 2)]
    odd = [(i, i + 1) for i in range(1, size - 1, 2)]
    both = lambda pairs: pairs + [(j, i) for i, j in pairs]
    return lax.ppermute(m1, axis, both(even)), lax.ppermute(m2, axis, both(odd))


def per_device(
    features, land_mask, cell_blocks, region_ids, targets, w_embed, k_first, w_mix, k_deep, w_head
):
    rows, cols = land_mask.shape
    crows, ccols = rows // 4, cols // 4
    c_in = features.shape[2]
    chan = w_embed.shape[1]
    width = ccols + 2 * HALO
    nblk = cell_blocks.shape[-2]
    bands, tiles = lax.axis_size("band"), lax.axis_size("tile")
    ndev = bands * tiles
    share = targets.shape[0]
    share_rows = pl.next_power_of_2(pl.cdiv(share, LANES))
    msg_rows = pl.cdiv(4 + share_rows, 8) * 8

    rid = region_ids.reshape(1, nblk)
    owner, place = rid // share, rid % share
    pad = ((0, 0), (1, LANES - 1 - nblk))
    high = jnp.pad(owner * share_rows + place // LANES, pad, constant_values=-1)
    low = jnp.pad(place % LANES, pad, constant_values=-1)
    blank = jnp.zeros((1, LANES), F32)
    tgt = jnp.pad(targets, (0, share_rows * LANES - share)).reshape(share_rows, LANES)
    msg_in = jnp.concatenate(
        [blank, blank, high.astype(F32), low.astype(F32)]
        + [jnp.zeros((msg_rows - 4 - share_rows, LANES), F32), tgt],
        axis=0,
    )
    head = w_head.T.reshape(4, 4, chan).transpose(1, 0, 2).astype(F32)
    wall = jnp.broadcast_to(head[:, None], (4, crows, 4, chan)).reshape(16 * crows, chan)

    feat = features.transpose(0, 2, 1)
    msg1 = HALO * ccols + ccols // 2
    chunk = next(c for c in (9, 8, 7, 6, 5, 4, 3, 2, 1) if nblk % c == 0)
    pre_first, act, bm, m1, m2, w_wide = call(
        embed_kernel,
        [
            ((crows * ccols, chan), F32),
            ((crows, ccols, chan), BF16),
            ((ccols, LANES), F32),
            ((msg1, chan), BF16),
            ((msg1, chan), BF16),
            ((512, chan), BF16),
        ],
        [
            ((rows, c_in, cols), BF16),
            ((16 * c_in, chan), BF16),
            ((rows, cols), jnp.int32),
            ((nblk, 1, LANES), jnp.int32),
            ((LANES, chunk * LANES), BF16),
            ((ccols, chunk * LANES), BF16),
            ((4,), None),
        ],
        hbm=4,
    )(
        *(
            pltpu.with_memory_space_constraint(x, pltpu.HBM)
            for x in (feat, w_embed, land_mask, cell_blocks.reshape(nblk, 1, LANES))
        )
    )
    p1, p2 = exchange(m1, m2, "band")
    msg2 = HALO * (crows + 2 * HALO) + 16
    m1, m2 = call(edges_kernel, [((msg2, chan), BF16)] * 2)(act, bm, p1, p2)
    t1, t2 = exchange(m1, m2, "tile")
    slope_first, msg_in = call(
        count_kernel, [((crows * ccols, chan), F32), ((msg_rows, LANES), F32)]
    )(pre_first, bm, msg_in)
    nrow = crows + 2 * HALO
    field, act_mix, pre_mix, pre_deep, pred, msg = call(
        forward_kernel,
        [
            ((crows + 4, width, chan), F32),
            ((crows + 2, width, chan), F32),
            ((crows + 2, width, chan), F32),
            ((crows, width, chan), F32),
            ((ccols, LANES), F32),
            ((msg_rows, LANES), F32),
        ],
        [((crows + 2, width, chan), F32)],
    )(act, bm, p1, p2, t1, t2, w_mix, k_first, k_deep, wall, msg_in)

    def slopes_mix(after):
        return call(slope_kernel, [((crows + 2, width, chan), F32)], hbm=1)(after, pre_mix)

    def slopes_deep(after):
        return call(
            slope_pred_kernel,
            [((crows, width, chan), F32), ((rows, cols), F32)],
            hbm=1,
        )(after, pre_deep, pred, land_mask)

    def slopes_rim(after):
        return call(
            rim_kernel,
            [((4, width, chan), F32)],
            [((4, width, chan), F32), ((2, width, chan), F32)],
            hbm=1,
        )(after, act, p1, p2, t1, t2, w_mix, k_first, k_deep, field, act_mix)

    beside = {1: slopes_mix, 2: slopes_deep, 3: slopes_rim}
    made = {}
    msgs = msg[None]
    at = 0
    for axis, size in (("band", bands), ("tile", tiles)):
        step = 1
        while step < size:
            if at in beside:
                made[at] = beside[at](msgs)
            other = lax.ppermute(msgs, axis, [(i, i ^ step) for i in range(size)])
            msgs = jnp.concatenate([msgs, other], axis=0)
            step *= 2
            at += 1
    (slope_mix,) = made[1]
    slope_deep, cell_pred = made[2]
    (slope_rim,) = made[3]

    height = ndev * share_rows
    mean, loss, grad = call(
        functools.partial(
            backward_kernel,
            share_rows=share_rows,
            share=share,
            loss_scale=1.0 / (2.0 * rows * cols * ndev),
            c_in=c_in,
        ),
        [((share_rows, LANES), F32), ((1, 1), F32), ((rows, c_in, cols), BF16)],
        [
            ((height, LANES), F32),
            ((height, LANES), F32),
            ((height, LANES), F32),
            ((nrow - 4, width, chan), F32),
            ((nrow - 4, width, chan), F32),
            ((crows, ccols, chan), BF16),
        ],
    )(
        msgs, bm, p1, p2, t1, t2, slope_deep, slope_rim, slope_mix,
        slope_first.reshape(crows, ccols, chan), w_mix, k_first, k_deep, wall, w_wide,
    )
    return (
        cell_pred,
        mean.reshape(-1)[:share],
        loss.reshape(1),
        grad.transpose(0, 2, 1),
    )


def solution(mesh):
    in_specs = (
        P(("group", "band"), "tile", None),
        P("band", "tile"),
        P("band", "tile", None, None),
        P("band", "tile", None),
        P(("group", "tile", "band")),
        P(),
        P(),
        P(),
        P(),
        P(),
    )
    out_specs = (
        P(("group", "band"), "tile"),
        P(("group", "tile", "band")),
        P("group"),
        P(("group", "band"), "tile", None),
    )
    return jax.shard_map(
        per_device, mesh=mesh, in_specs=in_specs, out_specs=out_specs, check_vma=False
    )
```

```python
import functools

import jax
import jax.numpy as jnp
from jax import lax
from jax.experimental import pallas as pl
from jax.experimental.pallas import tpu as pltpu
from jax.sharding import PartitionSpec as P

REGIONS = 14000
SQRT_HALF = 0.7071067811865476
INV_ROOT = 0.3989422804014327
F32 = jnp.float32
BF16 = jnp.bfloat16
LANES = 128
HALO = 4
OUTSIDE = -50.0
VMEM_LIMIT = 48 * 1024 * 1024


def gelu_exact(v):
    return 0.5 * v * (1.0 + lax.erf(v * SQRT_HALF))


def gelu_slope(v):
    return 0.5 * (1.0 + lax.erf(v * SQRT_HALF)) + v * jnp.exp(-0.5 * v * v) * INV_ROOT


def rounded(v):
    return v.astype(BF16).astype(F32)


def dot(a, b):
    return jnp.dot(a, b, preferred_element_type=F32)


def dot_nt(a, b):
    return lax.dot_general(a, b, (((1,), (1,)), ((), ())), preferred_element_type=F32)


def iota(shape, dim):
    return lax.broadcasted_iota(jnp.int32, shape, dim)


def spread_matrix(cols, transposed=False):
    quarter = cols // 4
    shape = (cols, cols)
    n = iota(shape, 0)
    c = iota(shape, 1)
    return jnp.where(c == 4 * (n % quarter) + n // quarter, 1.0, 0.0).astype(BF16)


def padded_embed(w_ref, c_in, c_pad):
    w = w_ref[...].astype(F32)
    zeros = jnp.zeros((c_pad - c_in, w.shape[1]), F32)
    parts = []
    for b in range(4):
        for a in range(4):
            start = (4 * a + b) * c_in
            parts += [w[start : start + c_in], zeros]
    return jnp.concatenate(parts, axis=0).astype(BF16)


def parity(axis):
    return lax.axis_index(axis) % 2


def embed_kernel(
    feat_hbm, w_hbm, land_hbm, blocks_hbm, pre_out, act_out, bm_out, m1_out, m2_out, w_out,
    feat, w_embed, land, blocks, sems,
):
    rows, c_in, cols = feat.shape
    part = rows // 4
    pairs = [(blocks_hbm, blocks), (land_hbm, land), (w_hbm, w_embed)]
    pairs += [
        (feat_hbm.at[pl.ds(part * n, part)], feat.at[pl.ds(part * n, part)]) for n in range(4)
    ]
    copies = [pltpu.make_async_copy(src, dst, sems.at[n]) for n, (src, dst) in enumerate(pairs)]
    for copy in copies:
        copy.start()
    c_pad = 32
    crows, ccols = rows // 4, cols // 4
    nblk = blocks.shape[0]
    spread = spread_matrix(cols)

    for copy in copies:
        copy.wait()
    shift_row = cols.bit_length() - 1
    chunk = next(c for c in (9, 8, 7, 6, 5, 4, 3, 2, 1) if nblk % c == 0)
    total = jnp.zeros((ccols, LANES), F32)
    sub_a = iota((LANES, LANES), 0).astype(F32).astype(BF16)
    sub_b = iota((ccols, LANES), 0).astype(F32).astype(BF16)
    one, none = jnp.ones((), BF16), jnp.zeros((), BF16)
    for first in range(0, nblk, chunk):
        hot_q, hot_j = [], []
        for step in range(chunk):
            k = first + step
            cell = blocks[k]
            named = cell < rows * cols
            q = jnp.where(named, (cell & 3) * rows + (cell >> shift_row), -1)
            j = (cell & (cols - 1)) >> 2
            hot_q.append(jnp.where(sub_a == q.astype(F32).astype(BF16), one, none))
            hot_j.append(
                jnp.where(sub_b == j.astype(F32).astype(BF16), jnp.array(k + 1, BF16), none)
            )
        total = total + dot_nt(
            jnp.concatenate(hot_j, axis=1), jnp.concatenate(hot_q, axis=1)
        )
    land_moved = dot_nt(spread, land[...].astype(F32).astype(BF16))
    land_q = jnp.concatenate(
        [land_moved[b * ccols : (b + 1) * ccols, :] for b in range(4)], axis=1
    )
    bm = total * land_q
    bm_out[...] = bm

    field = feat[...].astype(F32)
    field = jnp.concatenate([field, jnp.zeros((rows, c_pad - c_in, cols), F32)], axis=1)
    field = field.reshape(rows * c_pad, cols).astype(BF16)
    moved = dot_nt(spread, field).astype(BF16)
    wide = 4 * c_pad
    lhs = jnp.concatenate(
        [
            jnp.concatenate(
                [
                    moved[b * ccols : (b + 1) * ccols, i * wide : (i + 1) * wide]
                    for b in range(4)
                ],
                axis=1,
            )
            for i in range(crows)
        ],
        axis=0,
    )
    weights = padded_embed(w_embed, c_in, c_pad)
    w_out[...] = weights
    pre = dot(lhs, weights)
    chan = pre.shape[1]
    pre_out[...] = pre
    act_out[...] = gelu_exact(pre).astype(BF16).reshape(crows, ccols, chan)
    half = ccols // 2
    bm_wide = jnp.concatenate([bm[:half], bm[half:]], axis=1).astype(BF16)
    odd = parity("band")
    for out, start in ((m1_out, (1 - odd) * (crows - HALO)), (m2_out, odd * (crows - HALO))):
        out[0 : HALO * ccols] = act_out[pl.ds(start, HALO)].reshape(HALO * ccols, chan)
        out[HALO * ccols :] = bm_wide


def edges_kernel(act, bm, p1, p2, m1_out, m2_out):
    crows, ccols, chan = act.shape
    odd_b = parity("band") == 1
    odd_t = parity("tile") == 1
    n = HALO * ccols
    up = jnp.where(odd_b, p1[...].astype(F32), p2[...].astype(F32))
    down = jnp.where(odd_b, p2[...].astype(F32), p1[...].astype(F32))
    left, right = [], []
    for r in range(crows + 2 * HALO):
        if r < HALO:
            row = up[r * ccols : (r + 1) * ccols]
        elif r < HALO + crows:
            row = act[r - HALO].astype(F32)
        else:
            row = down[(r - HALO - crows) * ccols : (r - HALO - crows + 1) * ccols]
        left.append(row[:HALO])
        right.append(row[ccols - HALO :])
    half = ccols // 2
    own = bm[...]
    zeros = jnp.zeros((10, LANES), F32)
    bm_left = [up[n : n + 2, :LANES], own[0:2], down[n : n + 2, :LANES], zeros]
    bm_right = [
        up[n + half - 2 : n + half, LANES:],
        own[ccols - 2 :],
        down[n + half - 2 : n + half, LANES:],
        zeros,
    ]
    def message(cells, maps):
        maps = jnp.concatenate(maps, axis=0)
        maps = jnp.concatenate([maps, jnp.zeros((16, chan - LANES), F32)], axis=1)
        return jnp.concatenate(cells + [maps], axis=0)

    left = message(left, bm_left)
    right = message(right, bm_right)
    m1_out[...] = jnp.where(odd_t, left, right).astype(BF16)
    m2_out[...] = jnp.where(odd_t, right, left).astype(BF16)


def conv_pass(src, count, kernel, emit, chan):
    width = src.shape[1]
    for h in range(0, chan, LANES):
        span = slice(h, h + LANES)
        taps = [kernel[t : t + 1, span] for t in range(9)]

        def body(r, carry, span=span, taps=taps):
            older, newer = carry
            x = src[r, :, span]
            before = pltpu.roll(x, 1, 0)
            after = pltpu.roll(x, width - 1, 0)
            parts = [
                taps[3 * a] * before + taps[3 * a + 1] * x + taps[3 * a + 2] * after
                for a in range(3)
            ]
            emit(jnp.maximum(r - 2, 0), span, older + parts[2])
            return newer + parts[1], parts[0]

        zero = jnp.zeros((width, LANES), F32)
        lax.fori_loop(0, count, body, (zero, zero))


def halo_rows(act, p1, p2, t1, t2):
    crows, ccols, chan = act.shape
    odd_b = parity("band") == 1
    odd_t = parity("tile") == 1

    def edge(first, second, odd, at, n):
        return jnp.where(odd, first[at : at + n].astype(F32), second[at : at + n].astype(F32))

    def row(r):
        if r < HALO:
            own = edge(p1, p2, odd_b, r * ccols, ccols)
        elif r < HALO + crows:
            own = act[r - HALO].astype(F32)
        else:
            own = edge(p2, p1, odd_b, (r - HALO - crows) * ccols, ccols)
        base = HALO * r // 16 * 16
        at = HALO * r - base
        left = edge(t1, t2, odd_t, base, 16)[at : at + HALO]
        right = edge(t2, t1, odd_t, base, 16)[at : at + HALO]
        return own, jnp.concatenate([right, left], axis=0)

    return row


def inside_columns(shape, ccols):
    tile = lax.axis_index("tile")
    first = tile == 0
    last = tile == lax.axis_size("tile") - 1
    col = iota(shape, len(shape) - 2)
    low = jnp.where(last, ccols, ccols + HALO)
    high = jnp.where(first, ccols + 2 * HALO, ccols + HALO)
    return (col < low) | (col >= high)


def mix_pair(pair, base, weights, ok):
    _, width, chan = pair.shape
    pre = dot(pair.reshape(2 * width, chan).astype(BF16), weights).reshape(2, width, chan)
    pre = jnp.where(ok, pre, OUTSIDE)
    return pre, rounded(base + gelu_exact(pre))


def forward_kernel(
    act, bm, p1, p2, t1, t2, w_mix, k_first, k_deep, wall, msg_in,
    field, act_mix, pre_mix, pre_deep, pred_out, msg_out, mixed,
):
    crows, ccols, chan = act.shape
    width = ccols + 2 * HALO
    row = halo_rows(act, p1, p2, t1, t2)
    for r in range(crows + 4):
        own, edge = row(r + 2)
        field[r, 0:ccols, :] = own
        field[r, ccols:, :] = edge

    def keep_mixed(r, span, value):
        mixed[r, :, span] = value

    conv_pass(field, crows + 4, k_first[...].astype(F32), keep_mixed, chan)

    shape = (2, width, chan)
    col_ok = inside_columns(shape, ccols)
    band = lax.axis_index("band")
    first_row = jnp.where(band == 0, 1, 0)
    last_row = jnp.where(band == lax.axis_size("band") - 1, crows + 1, crows + 2)
    weights = w_mix[...]
    for g in range((crows + 2) // 2):
        at = iota(shape, 0) + 2 * g
        ok = col_ok & (at >= first_row) & (at < last_row)
        pair = slice(2 * g, 2 * g + 2)
        pre, post = mix_pair(mixed[pair], field[2 * g + 1 : 2 * g + 3], weights, ok)
        pre_mix[pair] = pre
        act_mix[pair] = post

    def keep_deep(r, span, value):
        pre_deep[r, :, span] = value

    conv_pass(act_mix, crows + 2, k_deep[...].astype(F32), keep_deep, chan)

    head = wall[...]
    head_row = (iota(head.shape, 0) % (4 * crows)) // 4
    pred = jnp.zeros((ccols, LANES), F32)
    for i in range(crows):
        out = act_mix[i + 1, 0:ccols, :] + gelu_exact(pre_deep[i, 0:ccols, :])
        pred = pred + dot_nt(
            out.astype(BF16), jnp.where(head_row == i, head, 0.0).astype(BF16)
        )
    pred_out[...] = pred

    maps = bm[...]
    slots = iota((LANES, LANES), 0).astype(F32)[:88]
    sums = jnp.zeros((88, LANES), F32)
    for j in range(ccols):
        sums = sums + jnp.where(maps[j : j + 1, :] == slots, pred[j : j + 1, :], 0.0)
    msg_out[...] = msg_in[...]
    msg_out[0:1, :] = across_lanes(sums)


def across_lanes(acc):
    rest = jnp.zeros((LANES - acc.shape[0], LANES), F32)
    turned = jnp.concatenate([acc, rest], axis=0).T
    total = jnp.sum(turned, axis=0, keepdims=True)
    return jnp.where(iota((1, LANES), 1) > 0, total, 0.0)


def count_kernel(pre_first, bm, msg_in, slope_first, msg_out):
    slope_first[...] = gelu_slope(pre_first[...])
    maps = bm[...]
    slots = iota((LANES, LANES), 0).astype(F32)[:88]
    counts = jnp.zeros((88, LANES), F32)
    for j in range(maps.shape[0]):
        counts = counts + jnp.where(maps[j : j + 1, :] == slots, 1.0, 0.0)
    msg_out[...] = msg_in[...]
    msg_out[1:2, :] = across_lanes(counts)


def rim_kernel(
    after, act, p1, p2, t1, t2, w_mix, k_first, k_deep, field, act_mix, slope_rim,
    ext, mixed, side,
):
    del after
    crows, ccols, chan = act.shape
    width = ccols + 2 * HALO
    row = halo_rows(act, p1, p2, t1, t2)
    outer = (0, 1) if side == 0 else (crows + 6, crows + 7)
    inner = (0, 1) if side == 0 else (crows + 2, crows + 3)
    near = (2, 3) if side == 0 else (0, 1)
    far = (0, 1) if side == 0 else (2, 3)
    for r, at in zip(outer, far):
        own, edge = row(r)
        ext[at, 0:ccols, :] = own
        ext[at, ccols:, :] = edge
    for r, at in zip(inner, near):
        ext[at] = field[r]

    def keep(r, span, value):
        mixed[r, :, span] = value

    conv_pass(ext, 4, k_first[...].astype(F32), keep, chan)
    edge_band = 0 if side == 0 else lax.axis_size("band") - 1
    ok = inside_columns((2, width, chan), ccols) & (lax.axis_index("band") != edge_band)
    _, post = mix_pair(mixed[...], ext[1:3], w_mix[...], ok)
    have = (0, 1) if side == 0 else (crows, crows + 1)
    for n in range(2):
        ext[far[n]] = post[n]
        ext[near[n]] = act_mix[have[n]]
    conv_pass(ext, 4, k_deep[...].astype(F32), keep, chan)
    slope_rim[...] = gelu_slope(mixed[...])


def slope_kernel(after, mix, deep, pred, land, slope_mix, slope_deep, cells):
    del after
    slope_mix[...] = gelu_slope(mix[...])
    slope_deep[...] = gelu_slope(deep[...])
    rows, cols = land.shape
    turned = pred[...].T
    wide = jnp.concatenate([turned[b * rows : (b + 1) * rows] for b in range(4)], axis=1)
    high = wide.astype(BF16)
    low = (wide - high.astype(F32)).astype(BF16)
    spread = spread_matrix(cols)
    cells[...] = (dot(high, spread) + dot(low, spread)) * land[...].astype(F32)


def backward_kernel(
    gathered, bm, p1, p2, t1, t2, slope_deep, rim_above, rim_below, slope_mix,
    slope_first,
    w_mix, k_first, k_deep, wall, w_wide,
    mean_out, loss_out, grad_out,
    targets, table, grads, field, mixing, proj, share_rows, share, loss_scale, c_in,
):
    ndev = gathered.shape[0]
    crows = slope_first.shape[0]
    ccols = slope_first.shape[1]
    chan = slope_first.shape[2]
    width = ccols + 2 * HALO
    band, tile = lax.axis_index("band"), lax.axis_index("tile")
    bands, tiles = lax.axis_size("band"), lax.axis_size("tile")
    me = tile * bands + band
    masks = hop_masks(bands, tiles)

    def slot_at(owner):
        apart = owner ^ me
        return sum(jnp.where(apart & mask > 0, 2**n, 0) for n, mask in enumerate(masks))

    def slot_of(v, t):
        other_band, other_tile = band + v, tile + t
        ok = (other_band >= 0) & (other_band < bands) & (other_tile >= 0) & (other_tile < tiles)
        return jnp.where(ok, slot_at(other_tile * bands + other_band), 0)

    height = ndev * share_rows
    chunk = min(16, ndev)
    first_target = gathered.shape[1] - share_rows
    sub = iota((height, LANES), 0).astype(F32).astype(BF16)
    sub_lo = iota((LANES, LANES), 0).astype(F32).astype(BF16)
    one, none = jnp.ones((), BF16), jnp.zeros((), BF16)

    def gather_chunk(c, acc):
        hot_hi, hot_lo = [], []
        for o in range(chunk):
            owner = c * chunk + o
            m = gathered[slot_at(owner)]
            hot_hi.append(jnp.where(sub == m[2:3].astype(BF16), one, none))
            low_hit = sub_lo == m[3:4].astype(BF16)
            high = rounded(m[0:1])
            parts = [high, m[0:1] - high, m[1:2]]
            hot_lo.append(
                jnp.concatenate(
                    [jnp.where(low_hit, part.astype(BF16), none) for part in parts], axis=0
                )
            )
            targets[pl.ds(owner * share_rows, share_rows)] = m[first_target:]
        return acc + dot_nt(
            jnp.concatenate(hot_hi, axis=1), jnp.concatenate(hot_lo, axis=1)
        )

    acc = jnp.zeros((height, 3 * LANES), F32)
    if ndev == chunk:
        acc = gather_chunk(0, acc)
    else:
        acc = lax.fori_loop(0, ndev // chunk, gather_chunk, acc)
    region_sum = acc[:, :LANES] + acc[:, LANES : 2 * LANES]
    region_count = acc[:, 2 * LANES :]
    at_least = jnp.maximum(region_count, 1.0)
    mean = region_sum / at_least
    table[...] = mean
    misfit = mean - targets[...]
    row = iota((height, LANES), 0)
    place = (row % share_rows) * LANES + iota((height, LANES), 1)
    inside = (place < share) & ((row // share_rows) * share + place < REGIONS)
    terms = jnp.where(inside, region_count * misfit * misfit, 0.0)
    loss_out[...] = jnp.sum(
        jnp.sum(terms, axis=0, keepdims=True), axis=1, keepdims=True
    ) * loss_scale
    grads[...] = jnp.where(inside, region_count * misfit / at_least, 0.0)
    mean_out[...] = table[pl.ds(me * share_rows, share_rows)]

    sub8 = iota((8, LANES), 0).astype(F32)

    def block_grads(slot):
        m = gathered[slot]
        low = jnp.broadcast_to(jnp.maximum(m[3:4], 0.0), (8, LANES)).astype(jnp.int32)
        high = m[2:3]
        total = jnp.zeros((8, LANES), F32)
        for at in range(0, height, 8):
            found = jnp.take_along_axis(grads[at : at + 8], low, axis=1)
            total = total + jnp.where(high == sub8 + float(at), found, 0.0)
        return jnp.sum(total, axis=0, keepdims=True)

    n = HALO * ccols
    half = ccols // 2
    odd_b = parity("band") == 1
    odd_t = parity("tile") == 1
    up = jnp.where(odd_b, p1[n:].astype(F32), p2[n:].astype(F32))
    down = jnp.where(odd_b, p2[n:].astype(F32), p1[n:].astype(F32))
    m = HALO * (crows + 2 * HALO)
    left = jnp.where(odd_t, t1[m:].astype(F32), t2[m:].astype(F32))[:, :LANES]
    right = jnp.where(odd_t, t2[m:].astype(F32), t1[m:].astype(F32))[:, :LANES]
    maps = [
        jnp.concatenate([up[:, :LANES], up[:, LANES:]], axis=0),
        bm[...],
        jnp.concatenate([down[:, :LANES], down[:, LANES:]], axis=0),
    ]
    cells = []
    gap = jnp.zeros((4, LANES), F32)
    for v in range(3):
        mid = block_grads(slot_of(v - 1, 0))
        lo = block_grads(slot_of(v - 1, -1))
        hi = block_grads(slot_of(v - 1, 1))
        source = jnp.broadcast_to(mid, (8, LANES))
        parts = [
            jnp.take_along_axis(source, maps[v][at : at + 8].astype(jnp.int32), axis=1)
            for at in range(0, ccols, 8)
        ]
        edge = jnp.concatenate(
            [right[2 * v : 2 * v + 2], gap, left[2 * v : 2 * v + 2]], axis=0
        ).astype(jnp.int32)
        source = jnp.concatenate(
            [jnp.broadcast_to(hi, (4, LANES)), jnp.broadcast_to(lo, (4, LANES))], axis=0
        )
        parts.append(jnp.take_along_axis(source, edge, axis=1))
        cells.append(jnp.concatenate(parts, axis=0).astype(BF16))

    head = wall[...]
    head_row = (iota(head.shape, 0) % (4 * crows)) // 4
    nrow = crows + 4
    for r in range(nrow):
        v = 0 if r < 2 else 1 if r < crows + 2 else 2
        i = (crows - 2 + r) if v == 0 else (r - 2) if v == 1 else r - crows - 2
        weights = jnp.where(head_row == i, head, 0.0).astype(BF16)
        deep = rounded(dot(cells[v], weights))
        mixing[r] = deep
        slope = rim_above[r] if v == 0 else slope_deep[i] if v == 1 else rim_below[r - crows - 2]
        field[r] = deep * slope

    def keep_mix(r, span, value):
        mixing[r + 1, :, span] = rounded(mixing[r + 1, :, span] + value)

    def reversed_taps(k):
        k = k[...].astype(F32)
        return jnp.concatenate([k[t : t + 1] for t in range(8, -1, -1)], axis=0)

    def first_pass():
        kernel = reversed_taps(k_deep)
        for h in range(0, chan, LANES):
            span = slice(h, h + LANES)
            taps = [kernel[t : t + 1, span] for t in range(9)]

            def parts_of(r):
                x = field[r, :, span]
                before = pltpu.roll(x, 1, 0)
                after = pltpu.roll(x, width - 1, 0)
                return [
                    taps[3 * a] * before + taps[3 * a + 1] * x + taps[3 * a + 2] * after
                    for a in range(3)
                ]

            def body(r, carry):
                older, newer = carry
                p = parts_of(r)
                keep_mix(r - 2, span, older + p[2])
                return newer + p[1], p[0]

            a = parts_of(0)
            b = parts_of(1)
            lax.fori_loop(2, nrow, body, (a[0] + b[1], b[0]))

    first_pass()
    weights = w_mix[...]

    for g in range((nrow - 2) // 2):
        pre = (mixing[2 * g + 1 : 2 * g + 3] * slope_mix[2 * g : 2 * g + 2]).reshape(
            2 * width, chan
        )
        field[2 * g : 2 * g + 2] = dot_nt(pre.astype(BF16), weights).reshape(2, width, chan)

    def keep_first(r, span, value):
        total = mixing[r + 2, 0:ccols, span] + value[0:ccols]
        proj[r, :, span] = (total * slope_first[r, :, span]).astype(BF16)

    conv_pass(field, nrow - 2, reversed_taps(k_first), keep_first, chan)

    c_pad = 32
    out = dot_nt(w_wide[...], proj[...].reshape(crows * ccols, chan)).astype(BF16)
    wide = 4 * c_pad
    spread = spread_matrix(4 * ccols)
    group = crows // 4
    for g in range(4):
        lhs = jnp.concatenate(
            [
                jnp.concatenate(
                    [
                        out[b * wide : (b + 1) * wide, i * ccols : (i + 1) * ccols]
                        for b in range(4)
                    ],
                    axis=1,
                )
                for i in range(g * group, (g + 1) * group)
            ],
            axis=0,
        )
        fine = dot(lhs, spread)
        for r in range(4 * group):
            grad_out[4 * group * g + r] = fine[r * c_pad : r * c_pad + c_in].astype(BF16)


def call(kernel, outs, scratch=(), hbm=0):
    def run(*args):
        space = [pl.BlockSpec(memory_space=pl.ANY)] * hbm
        space += [pl.BlockSpec(memory_space=pltpu.VMEM)] * (len(args) - hbm)
        return pl.pallas_call(
            kernel,
            out_shape=[jax.ShapeDtypeStruct(s, d) for s, d in outs],
            in_specs=space,
            out_specs=[pl.BlockSpec(memory_space=pltpu.VMEM)] * len(outs),
            scratch_shapes=[
                pltpu.SemaphoreType.DMA(s) if d is None else pltpu.VMEM(s, d)
                for s, d in scratch
            ],
            compiler_params=pltpu.CompilerParams(vmem_limit_bytes=VMEM_LIMIT),
            cost_estimate=pl.CostEstimate(
                flops=10**6, bytes_accessed=10**6, transcendentals=0
            ),
        )(*args)

    return run


def hop_masks(bands, tiles):
    return [2**n for n in range((bands * tiles).bit_length() - 2, -1, -1)]


def exchange(m1, m2, axis):
    size = lax.axis_size(axis)
    even = [(i, i + 1) for i in range(0, size - 1, 2)]
    odd = [(i, i + 1) for i in range(1, size - 1, 2)]
    both = lambda pairs: pairs + [(j, i) for i, j in pairs]
    return lax.ppermute(m1, axis, both(even)), lax.ppermute(m2, axis, both(odd))


def per_device(
    features, land_mask, cell_blocks, region_ids, targets, w_embed, k_first, w_mix, k_deep, w_head
):
    rows, cols = land_mask.shape
    crows, ccols = rows // 4, cols // 4
    c_in = features.shape[2]
    chan = w_embed.shape[1]
    width = ccols + 2 * HALO
    nblk = cell_blocks.shape[-2]
    bands, tiles = lax.axis_size("band"), lax.axis_size("tile")
    ndev = bands * tiles
    share = targets.shape[0]
    share_rows = pl.next_power_of_2(pl.cdiv(share, LANES))
    msg_rows = pl.cdiv(4 + share_rows, 8) * 8

    rid = region_ids.reshape(1, nblk)
    owner, place = rid // share, rid % share
    pad = ((0, 0), (1, LANES - 1 - nblk))
    high = jnp.pad(owner * share_rows + place // LANES, pad, constant_values=-1)
    low = jnp.pad(place % LANES, pad, constant_values=-1)
    blank = jnp.zeros((1, LANES), F32)
    tgt = jnp.pad(targets, (0, share_rows * LANES - share)).reshape(share_rows, LANES)
    msg_in = jnp.concatenate(
        [blank, blank, high.astype(F32), low.astype(F32)]
        + [jnp.zeros((msg_rows - 4 - share_rows, LANES), F32), tgt],
        axis=0,
    )
    head = w_head.T.reshape(4, 4, chan).transpose(1, 0, 2).astype(F32)
    wall = jnp.broadcast_to(head[:, None], (4, crows, 4, chan)).reshape(16 * crows, chan)

    feat = features.transpose(0, 2, 1)
    msg1 = HALO * ccols + ccols // 2
    pre_first, act, bm, m1, m2, w_wide = call(
        embed_kernel,
        [
            ((crows * ccols, chan), F32),
            ((crows, ccols, chan), BF16),
            ((ccols, LANES), F32),
            ((msg1, chan), BF16),
            ((msg1, chan), BF16),
            ((512, chan), BF16),
        ],
        [
            ((rows, c_in, cols), BF16),
            ((16 * c_in, chan), BF16),
            ((rows, cols), jnp.int32),
            ((nblk, 1, LANES), jnp.int32),
            ((7,), None),
        ],
        hbm=4,
    )(
        *(
            pltpu.with_memory_space_constraint(x, pltpu.HBM)
            for x in (feat, w_embed, land_mask, cell_blocks.reshape(nblk, 1, LANES))
        )
    )
    p1, p2 = exchange(m1, m2, "band")
    msg2 = HALO * (crows + 2 * HALO) + 16
    m1, m2 = call(edges_kernel, [((msg2, chan), BF16)] * 2)(act, bm, p1, p2)
    t1, t2 = exchange(m1, m2, "tile")
    slope_first, msg_in = call(
        count_kernel, [((crows * ccols, chan), F32), ((msg_rows, LANES), F32)]
    )(pre_first, bm, msg_in)
    nrow = crows + 2 * HALO
    field, act_mix, pre_mix, pre_deep, pred, msg = call(
        forward_kernel,
        [
            ((crows + 4, width, chan), F32),
            ((crows + 2, width, chan), F32),
            ((crows + 2, width, chan), F32),
            ((crows, width, chan), F32),
            ((ccols, LANES), F32),
            ((msg_rows, LANES), F32),
        ],
        [((crows + 2, width, chan), F32)],
    )(act, bm, p1, p2, t1, t2, w_mix, k_first, k_deep, wall, msg_in)

    def slopes(after):
        return call(
            slope_kernel,
            [
                ((crows + 2, width, chan), F32),
                ((crows, width, chan), F32),
                ((rows, cols), F32),
            ],
            hbm=1,
        )(after, pre_mix, pre_deep, pred, land_mask)

    def rim(side, after):
        return call(
            functools.partial(rim_kernel, side=side),
            [((2, width, chan), F32)],
            [((4, width, chan), F32), ((2, width, chan), F32)],
            hbm=1,
        )(after, act, p1, p2, t1, t2, w_mix, k_first, k_deep, field, act_mix)

    def send(x, mask):
        pairs = [(n, n ^ mask) for n in range(ndev)]
        return lax.ppermute(x, ("tile", "band"), pairs)

    masks = hop_masks(bands, tiles)
    beside = [slopes, functools.partial(rim, 0), functools.partial(rim, 1)]
    made = []
    msgs = msg[None]
    for n, mask in enumerate(masks):
        if n < len(beside):
            made.append(beside[n](msgs))
        msgs = jnp.concatenate([msgs, send(msgs, mask)], axis=0)
    (slope_mix, slope_deep, cell_pred), (rim_above,), (rim_below,) = made

    height = ndev * share_rows
    mean, loss, grad = call(
        functools.partial(
            backward_kernel,
            share_rows=share_rows,
            share=share,
            loss_scale=1.0 / (2.0 * rows * cols * ndev),
            c_in=c_in,
        ),
        [((share_rows, LANES), F32), ((1, 1), F32), ((rows, c_in, cols), BF16)],
        [
            ((height, LANES), F32),
            ((height, LANES), F32),
            ((height, LANES), F32),
            ((nrow - 4, width, chan), F32),
            ((nrow - 4, width, chan), F32),
            ((crows, ccols, chan), BF16),
        ],
    )(
        msgs, bm, p1, p2, t1, t2, slope_deep, rim_above, rim_below, slope_mix,
        slope_first.reshape(crows, ccols, chan), w_mix, k_first, k_deep, wall, w_wide,
    )
    return (
        cell_pred,
        mean.reshape(-1)[:share],
        loss.reshape(1),
        grad.transpose(0, 2, 1),
    )


def solution(mesh):
    in_specs = (
        P(("group", "band"), "tile", None),
        P("band", "tile"),
        P("band", "tile", None, None),
        P("band", "tile", None),
        P(("group", "tile", "band")),
        P(),
        P(),
        P(),
        P(),
        P(),
    )
    out_specs = (
        P(("group", "band"), "tile"),
        P(("group", "tile", "band")),
        P("group"),
        P(("group", "band"), "tile", None),
    )
    return jax.shard_map(
        per_device, mesh=mesh, in_specs=in_specs, out_specs=out_specs, check_vma=False
    )
```

```python
import functools

import jax
import jax.numpy as jnp
from jax import lax
from jax.experimental import pallas as pl
from jax.experimental.pallas import tpu as pltpu
from jax.sharding import PartitionSpec as P

REGIONS = 14000
SQRT_HALF = 0.7071067811865476
INV_ROOT = 0.3989422804014327
F32 = jnp.float32
BF16 = jnp.bfloat16
LANES = 128
HALO = 4
OUTSIDE = -50.0
VMEM_LIMIT = 48 * 1024 * 1024


def gelu_exact(v):
    return 0.5 * v * (1.0 + lax.erf(v * SQRT_HALF))


def gelu_slope(v):
    return 0.5 * (1.0 + lax.erf(v * SQRT_HALF)) + v * jnp.exp(-0.5 * v * v) * INV_ROOT


def rounded(v):
    return v.astype(BF16).astype(F32)


def dot(a, b):
    return jnp.dot(a, b, preferred_element_type=F32)


def dot_nt(a, b):
    return lax.dot_general(a, b, (((1,), (1,)), ((), ())), preferred_element_type=F32)


def iota(shape, dim):
    return lax.broadcasted_iota(jnp.int32, shape, dim)


def spread_matrix(cols, transposed=False):
    quarter = cols // 4
    shape = (cols, cols)
    n = iota(shape, 0)
    c = iota(shape, 1)
    return jnp.where(c == 4 * (n % quarter) + n // quarter, 1.0, 0.0).astype(BF16)


def padded_embed(w_ref, c_in, c_pad):
    w = w_ref[...].astype(F32)
    zeros = jnp.zeros((c_pad - c_in, w.shape[1]), F32)
    parts = []
    for b in range(4):
        for a in range(4):
            start = (4 * a + b) * c_in
            parts += [w[start : start + c_in], zeros]
    return jnp.concatenate(parts, axis=0).astype(BF16)


def parity(axis):
    return lax.axis_index(axis) % 2


def embed_kernel(
    feat_hbm, w_hbm, land_hbm, blocks_hbm, pre_out, act_out, bm_out, m2_out, w_out,
    feat, w_embed, land, blocks, sems,
):
    rows, c_in, cols = feat.shape
    part = rows // 4
    pairs = [(blocks_hbm, blocks), (land_hbm, land), (w_hbm, w_embed)]
    pairs += [
        (feat_hbm.at[pl.ds(part * n, part)], feat.at[pl.ds(part * n, part)]) for n in range(4)
    ]
    copies = [pltpu.make_async_copy(src, dst, sems.at[n]) for n, (src, dst) in enumerate(pairs)]
    for copy in copies:
        copy.start()
    c_pad = 32
    crows, ccols = rows // 4, cols // 4
    nblk = blocks.shape[0]
    spread = spread_matrix(cols)

    for copy in copies:
        copy.wait()
    shift_row = cols.bit_length() - 1
    chunk = next(c for c in (9, 8, 7, 6, 5, 4, 3, 2, 1) if nblk % c == 0)
    total = jnp.zeros((ccols, LANES), F32)
    sub_a = iota((LANES, LANES), 0).astype(F32).astype(BF16)
    sub_b = iota((ccols, LANES), 0).astype(F32).astype(BF16)
    one, none = jnp.ones((), BF16), jnp.zeros((), BF16)
    for first in range(0, nblk, chunk):
        hot_q, hot_j = [], []
        for step in range(chunk):
            k = first + step
            cell = blocks[k]
            named = cell < rows * cols
            q = jnp.where(named, (cell & 3) * rows + (cell >> shift_row), -1)
            j = (cell & (cols - 1)) >> 2
            hot_q.append(jnp.where(sub_a == q.astype(F32).astype(BF16), one, none))
            hot_j.append(
                jnp.where(sub_b == j.astype(F32).astype(BF16), jnp.array(k + 1, BF16), none)
            )
        total = total + dot_nt(
            jnp.concatenate(hot_j, axis=1), jnp.concatenate(hot_q, axis=1)
        )
    land_moved = dot_nt(spread, land[...].astype(F32).astype(BF16))
    land_q = jnp.concatenate(
        [land_moved[b * ccols : (b + 1) * ccols, :] for b in range(4)], axis=1
    )
    bm = total * land_q
    bm_out[...] = bm

    field = feat[...].astype(F32)
    field = jnp.concatenate([field, jnp.zeros((rows, c_pad - c_in, cols), F32)], axis=1)
    field = field.reshape(rows * c_pad, cols).astype(BF16)
    moved = dot_nt(spread, field).astype(BF16)
    wide = 4 * c_pad
    lhs = jnp.concatenate(
        [
            jnp.concatenate(
                [
                    moved[b * ccols : (b + 1) * ccols, i * wide : (i + 1) * wide]
                    for b in range(4)
                ],
                axis=1,
            )
            for i in range(crows)
        ],
        axis=0,
    )
    weights = padded_embed(w_embed, c_in, c_pad)
    w_out[...] = weights
    pre = dot(lhs, weights)
    chan = pre.shape[1]
    pre_out[...] = pre
    act_out[...] = gelu_exact(pre).astype(BF16).reshape(crows, ccols, chan)
    pack(act_out, bm, parity("band"), m2_out)


def pack(act, bm, low, out):
    crows, ccols, chan = act.shape
    half = ccols // 2
    start = low * (crows - HALO)
    out[0 : HALO * ccols] = act[pl.ds(start, HALO)].reshape(HALO * ccols, chan)
    out[HALO * ccols :] = jnp.concatenate([bm[:half], bm[half:]], axis=1).astype(BF16)


def pack_kernel(act, bm, m1_out):
    pack(act, bm[...], 1 - parity("band"), m1_out)


def edges_kernel(act, bm, p1, p2, out, second):
    crows, ccols, chan = act.shape
    odd_b = parity("band") == 1
    odd_t = parity("tile") == 1
    n = HALO * ccols
    up = jnp.where(odd_b, p1[...].astype(F32), p2[...].astype(F32))
    down = jnp.where(odd_b, p2[...].astype(F32), p1[...].astype(F32))
    left, right = [], []
    for r in range(crows + 2 * HALO):
        if r < HALO:
            row = up[r * ccols : (r + 1) * ccols]
        elif r < HALO + crows:
            row = act[r - HALO].astype(F32)
        else:
            row = down[(r - HALO - crows) * ccols : (r - HALO - crows + 1) * ccols]
        left.append(row[:HALO])
        right.append(row[ccols - HALO :])
    half = ccols // 2
    own = bm[...]
    zeros = jnp.zeros((10, LANES), F32)
    bm_left = [up[n : n + 2, :LANES], own[0:2], down[n : n + 2, :LANES], zeros]
    bm_right = [
        up[n + half - 2 : n + half, LANES:],
        own[ccols - 2 :],
        down[n + half - 2 : n + half, LANES:],
        zeros,
    ]
    def message(cells, maps):
        maps = jnp.concatenate(maps, axis=0)
        maps = jnp.concatenate([maps, jnp.zeros((16, chan - LANES), F32)], axis=1)
        return jnp.concatenate(cells + [maps], axis=0)

    left = message(left, bm_left)
    right = message(right, bm_right)
    low = ~odd_t if second else odd_t
    out[...] = jnp.where(low, left, right).astype(BF16)


def conv_pass(src, count, kernel, emit, chan):
    width = src.shape[1]
    for h in range(0, chan, LANES):
        span = slice(h, h + LANES)
        taps = [kernel[t : t + 1, span] for t in range(9)]
        sums = [None] * (count - 2)
        for r in range(count):
            x = src[r, :, span]
            before = pltpu.roll(x, 1, 0)
            after = pltpu.roll(x, width - 1, 0)
            for a in range(3):
                if 0 <= r - a < count - 2:
                    part = taps[3 * a] * before + taps[3 * a + 1] * x + taps[3 * a + 2] * after
                    sums[r - a] = part if a == 0 else sums[r - a] + part
            if r >= 2:
                emit(r - 2, span, sums[r - 2])


def halo_rows(act, p1, p2, t1, t2):
    crows, ccols, chan = act.shape
    odd_b = parity("band") == 1
    odd_t = parity("tile") == 1

    def edge(first, second, odd, at, n):
        return jnp.where(odd, first[at : at + n].astype(F32), second[at : at + n].astype(F32))

    def row(r):
        if r < HALO:
            own = edge(p1, p2, odd_b, r * ccols, ccols)
        elif r < HALO + crows:
            own = act[r - HALO].astype(F32)
        else:
            own = edge(p2, p1, odd_b, (r - HALO - crows) * ccols, ccols)
        base = HALO * r // 16 * 16
        at = HALO * r - base
        left = edge(t1, t2, odd_t, base, 16)[at : at + HALO]
        right = edge(t2, t1, odd_t, base, 16)[at : at + HALO]
        return own, jnp.concatenate([right, left], axis=0)

    return row


def inside_columns(shape, ccols):
    tile = lax.axis_index("tile")
    first = tile == 0
    last = tile == lax.axis_size("tile") - 1
    col = iota(shape, len(shape) - 2)
    low = jnp.where(last, ccols, ccols + HALO)
    high = jnp.where(first, ccols + 2 * HALO, ccols + HALO)
    return (col < low) | (col >= high)


def mix_pair(pair, base, weights, ok):
    _, width, chan = pair.shape
    pre = dot(pair.reshape(2 * width, chan).astype(BF16), weights).reshape(2, width, chan)
    pre = jnp.where(ok, pre, OUTSIDE)
    return pre, rounded(base + gelu_exact(pre))


def forward_kernel(
    act, bm, p1, p2, t1, t2, w_mix, k_first, k_deep, wall, msg_in,
    field, act_mix, pre_mix, pre_deep, pred_out, msg_out, mixed,
):
    crows, ccols, chan = act.shape
    width = ccols + 2 * HALO
    row = halo_rows(act, p1, p2, t1, t2)
    for r in range(crows + 4):
        own, edge = row(r + 2)
        field[r, 0:ccols, :] = own
        field[r, ccols:, :] = edge

    def keep_mixed(r, span, value):
        mixed[r, :, span] = value

    conv_pass(field, crows + 4, k_first[...].astype(F32), keep_mixed, chan)

    shape = (2, width, chan)
    col_ok = inside_columns(shape, ccols)
    band = lax.axis_index("band")
    first_row = jnp.where(band == 0, 1, 0)
    last_row = jnp.where(band == lax.axis_size("band") - 1, crows + 1, crows + 2)
    weights = w_mix[...]
    for g in range((crows + 2) // 2):
        at = iota(shape, 0) + 2 * g
        ok = col_ok & (at >= first_row) & (at < last_row)
        pair = slice(2 * g, 2 * g + 2)
        pre, post = mix_pair(mixed[pair], field[2 * g + 1 : 2 * g + 3], weights, ok)
        pre_mix[pair] = pre
        act_mix[pair] = post

    def keep_deep(r, span, value):
        pre_deep[r, :, span] = value

    conv_pass(act_mix, crows + 2, k_deep[...].astype(F32), keep_deep, chan)

    head = wall[...]
    head_row = (iota(head.shape, 0) % (4 * crows)) // 4
    pred = jnp.zeros((ccols, LANES), F32)
    for i in range(crows):
        out = act_mix[i + 1, 0:ccols, :] + gelu_exact(pre_deep[i, 0:ccols, :])
        pred = pred + dot_nt(
            out.astype(BF16), jnp.where(head_row == i, head, 0.0).astype(BF16)
        )
    pred_out[...] = pred

    maps = bm[...]
    slots = iota((LANES, LANES), 0).astype(F32)[:88]
    sums = jnp.zeros((88, LANES), F32)
    for j in range(ccols):
        sums = sums + jnp.where(maps[j : j + 1, :] == slots, pred[j : j + 1, :], 0.0)
    msg_out[...] = msg_in[...]
    msg_out[0:1, :] = across_lanes(sums)


def across_lanes(acc):
    rest = jnp.zeros((LANES - acc.shape[0], LANES), F32)
    turned = jnp.concatenate([acc, rest], axis=0).T
    total = jnp.sum(turned, axis=0, keepdims=True)
    return jnp.where(iota((1, LANES), 1) > 0, total, 0.0)


def count_kernel(pre_first, bm, msg_in, slope_first, msg_out):
    slope_first[...] = gelu_slope(pre_first[...])
    maps = bm[...]
    slots = iota((LANES, LANES), 0).astype(F32)[:88]
    counts = jnp.zeros((88, LANES), F32)
    for j in range(maps.shape[0]):
        counts = counts + jnp.where(maps[j : j + 1, :] == slots, 1.0, 0.0)
    msg_out[...] = msg_in[...]
    msg_out[1:2, :] = across_lanes(counts)


def rim_kernel(
    after, act, p1, p2, t1, t2, w_mix, k_first, k_deep, field, act_mix, slope_rim,
    ext, mixed, side,
):
    del after
    crows, ccols, chan = act.shape
    width = ccols + 2 * HALO
    row = halo_rows(act, p1, p2, t1, t2)
    outer = (0, 1) if side == 0 else (crows + 6, crows + 7)
    inner = (0, 1) if side == 0 else (crows + 2, crows + 3)
    near = (2, 3) if side == 0 else (0, 1)
    far = (0, 1) if side == 0 else (2, 3)
    for r, at in zip(outer, far):
        own, edge = row(r)
        ext[at, 0:ccols, :] = own
        ext[at, ccols:, :] = edge
    for r, at in zip(inner, near):
        ext[at] = field[r]

    def keep(r, span, value):
        mixed[r, :, span] = value

    conv_pass(ext, 4, k_first[...].astype(F32), keep, chan)
    edge_band = 0 if side == 0 else lax.axis_size("band") - 1
    ok = inside_columns((2, width, chan), ccols) & (lax.axis_index("band") != edge_band)
    _, post = mix_pair(mixed[...], ext[1:3], w_mix[...], ok)
    have = (0, 1) if side == 0 else (crows, crows + 1)
    for n in range(2):
        ext[far[n]] = post[n]
        ext[near[n]] = act_mix[have[n]]
    conv_pass(ext, 4, k_deep[...].astype(F32), keep, chan)
    slope_rim[...] = gelu_slope(mixed[...])


def slope_kernel(after, mix, deep, pred, land, slope_mix, slope_deep, cells):
    del after
    slope_mix[...] = gelu_slope(mix[...])
    slope_deep[...] = gelu_slope(deep[...])
    rows, cols = land.shape
    turned = pred[...].T
    wide = jnp.concatenate([turned[b * rows : (b + 1) * rows] for b in range(4)], axis=1)
    high = wide.astype(BF16)
    low = (wide - high.astype(F32)).astype(BF16)
    spread = spread_matrix(cols)
    cells[...] = (dot(high, spread) + dot(low, spread)) * land[...].astype(F32)


def backward_kernel(
    gathered, bm, p1, p2, t1, t2, slope_deep, rim_above, rim_below, slope_mix,
    slope_first,
    w_mix, k_first, k_deep, wall, w_wide,
    mean_out, loss_out, grad_out,
    targets, table, grads, field, mixing, proj, share_rows, share, loss_scale, c_in,
):
    ndev = gathered.shape[0]
    crows = slope_first.shape[0]
    ccols = slope_first.shape[1]
    chan = slope_first.shape[2]
    width = ccols + 2 * HALO
    band, tile = lax.axis_index("band"), lax.axis_index("tile")
    bands, tiles = lax.axis_size("band"), lax.axis_size("tile")
    me = tile * bands + band
    masks = hop_masks(bands, tiles)

    def slot_at(owner):
        apart = owner ^ me
        return sum(jnp.where(apart & mask > 0, 2**n, 0) for n, mask in enumerate(masks))

    def slot_of(v, t):
        other_band, other_tile = band + v, tile + t
        ok = (other_band >= 0) & (other_band < bands) & (other_tile >= 0) & (other_tile < tiles)
        return jnp.where(ok, slot_at(other_tile * bands + other_band), 0)

    height = ndev * share_rows
    chunk = min(16, ndev)
    first_target = gathered.shape[1] - share_rows
    sub = iota((height, LANES), 0).astype(F32).astype(BF16)
    sub_lo = iota((LANES, LANES), 0).astype(F32).astype(BF16)
    one, none = jnp.ones((), BF16), jnp.zeros((), BF16)

    def gather_chunk(c, acc):
        hot_hi, hot_lo = [], []
        for o in range(chunk):
            owner = c * chunk + o
            m = gathered[slot_at(owner)]
            hot_hi.append(jnp.where(sub == m[2:3].astype(BF16), one, none))
            low_hit = sub_lo == m[3:4].astype(BF16)
            high = rounded(m[0:1])
            parts = [high, m[0:1] - high, m[1:2]]
            hot_lo.append(
                jnp.concatenate(
                    [jnp.where(low_hit, part.astype(BF16), none) for part in parts], axis=0
                )
            )
            targets[pl.ds(owner * share_rows, share_rows)] = m[first_target:]
        return acc + dot_nt(
            jnp.concatenate(hot_hi, axis=1), jnp.concatenate(hot_lo, axis=1)
        )

    acc = jnp.zeros((height, 3 * LANES), F32)
    if ndev == chunk:
        acc = gather_chunk(0, acc)
    else:
        acc = lax.fori_loop(0, ndev // chunk, gather_chunk, acc)
    region_sum = acc[:, :LANES] + acc[:, LANES : 2 * LANES]
    region_count = acc[:, 2 * LANES :]
    at_least = jnp.maximum(region_count, 1.0)
    mean = region_sum / at_least
    table[...] = mean
    misfit = mean - targets[...]
    row = iota((height, LANES), 0)
    place = (row % share_rows) * LANES + iota((height, LANES), 1)
    inside = (place < share) & ((row // share_rows) * share + place < REGIONS)
    terms = jnp.where(inside, region_count * misfit * misfit, 0.0)
    loss_out[...] = jnp.sum(
        jnp.sum(terms, axis=0, keepdims=True), axis=1, keepdims=True
    ) * loss_scale
    grads[...] = jnp.where(inside, region_count * misfit / at_least, 0.0)
    mean_out[...] = table[pl.ds(me * share_rows, share_rows)]

    sub8 = iota((8, LANES), 0).astype(F32)

    def block_grads(slot):
        m = gathered[slot]
        low = jnp.broadcast_to(jnp.maximum(m[3:4], 0.0), (8, LANES)).astype(jnp.int32)
        high = m[2:3]
        total = jnp.zeros((8, LANES), F32)
        for at in range(0, height, 8):
            found = jnp.take_along_axis(grads[at : at + 8], low, axis=1)
            total = total + jnp.where(high == sub8 + float(at), found, 0.0)
        return jnp.sum(total, axis=0, keepdims=True)

    n = HALO * ccols
    half = ccols // 2
    odd_b = parity("band") == 1
    odd_t = parity("tile") == 1
    up = jnp.where(odd_b, p1[n:].astype(F32), p2[n:].astype(F32))
    down = jnp.where(odd_b, p2[n:].astype(F32), p1[n:].astype(F32))
    m = HALO * (crows + 2 * HALO)
    left = jnp.where(odd_t, t1[m:].astype(F32), t2[m:].astype(F32))[:, :LANES]
    right = jnp.where(odd_t, t2[m:].astype(F32), t1[m:].astype(F32))[:, :LANES]
    maps = [
        jnp.concatenate([up[:, :LANES], up[:, LANES:]], axis=0),
        bm[...],
        jnp.concatenate([down[:, :LANES], down[:, LANES:]], axis=0),
    ]
    cells = []
    gap = jnp.zeros((4, LANES), F32)
    for v in range(3):
        mid = block_grads(slot_of(v - 1, 0))
        lo = block_grads(slot_of(v - 1, -1))
        hi = block_grads(slot_of(v - 1, 1))
        source = jnp.broadcast_to(mid, (8, LANES))
        parts = [
            jnp.take_along_axis(source, maps[v][at : at + 8].astype(jnp.int32), axis=1)
            for at in range(0, ccols, 8)
        ]
        edge = jnp.concatenate(
            [right[2 * v : 2 * v + 2], gap, left[2 * v : 2 * v + 2]], axis=0
        ).astype(jnp.int32)
        source = jnp.concatenate(
            [jnp.broadcast_to(hi, (4, LANES)), jnp.broadcast_to(lo, (4, LANES))], axis=0
        )
        parts.append(jnp.take_along_axis(source, edge, axis=1))
        cells.append(jnp.concatenate(parts, axis=0).astype(BF16))

    head = wall[...]
    head_row = (iota(head.shape, 0) % (4 * crows)) // 4
    nrow = crows + 4
    for r in range(nrow):
        v = 0 if r < 2 else 1 if r < crows + 2 else 2
        i = (crows - 2 + r) if v == 0 else (r - 2) if v == 1 else r - crows - 2
        weights = jnp.where(head_row == i, head, 0.0).astype(BF16)
        deep = rounded(dot(cells[v], weights))
        mixing[r] = deep
        slope = rim_above[r] if v == 0 else slope_deep[i] if v == 1 else rim_below[r - crows - 2]
        field[r] = deep * slope

    def keep_mix(r, span, value):
        mixing[r + 1, :, span] = rounded(mixing[r + 1, :, span] + value)

    def reversed_taps(k):
        k = k[...].astype(F32)
        return jnp.concatenate([k[t : t + 1] for t in range(8, -1, -1)], axis=0)

    conv_pass(field, nrow, reversed_taps(k_deep), keep_mix, chan)
    weights = w_mix[...]

    for g in range((nrow - 2) // 2):
        pre = (mixing[2 * g + 1 : 2 * g + 3] * slope_mix[2 * g : 2 * g + 2]).reshape(
            2 * width, chan
        )
        field[2 * g : 2 * g + 2] = dot_nt(pre.astype(BF16), weights).reshape(2, width, chan)

    def keep_first(r, span, value):
        total = mixing[r + 2, 0:ccols, span] + value[0:ccols]
        proj[r, :, span] = (total * slope_first[r, :, span]).astype(BF16)

    conv_pass(field, nrow - 2, reversed_taps(k_first), keep_first, chan)

    c_pad = 32
    out = dot_nt(w_wide[...], proj[...].reshape(crows * ccols, chan)).astype(BF16)
    wide = 4 * c_pad
    spread = spread_matrix(4 * ccols)
    group = crows // 4
    for g in range(4):
        lhs = jnp.concatenate(
            [
                jnp.concatenate(
                    [
                        out[b * wide : (b + 1) * wide, i * ccols : (i + 1) * ccols]
                        for b in range(4)
                    ],
                    axis=1,
                )
                for i in range(g * group, (g + 1) * group)
            ],
            axis=0,
        )
        fine = dot(lhs, spread)
        for r in range(4 * group):
            grad_out[4 * group * g + r] = fine[r * c_pad : r * c_pad + c_in].astype(BF16)


def call(kernel, outs, scratch=(), hbm=0):
    def run(*args):
        space = [pl.BlockSpec(memory_space=pl.ANY)] * hbm
        space += [pl.BlockSpec(memory_space=pltpu.VMEM)] * (len(args) - hbm)
        return pl.pallas_call(
            kernel,
            out_shape=[jax.ShapeDtypeStruct(s, d) for s, d in outs],
            in_specs=space,
            out_specs=[pl.BlockSpec(memory_space=pltpu.VMEM)] * len(outs),
            scratch_shapes=[
                pltpu.SemaphoreType.DMA(s) if d is None else pltpu.VMEM(s, d)
                for s, d in scratch
            ],
            compiler_params=pltpu.CompilerParams(vmem_limit_bytes=VMEM_LIMIT),
            cost_estimate=pl.CostEstimate(
                flops=10**6, bytes_accessed=10**6, transcendentals=0
            ),
        )(*args)

    return run


def hop_masks(bands, tiles):
    return [2**n for n in range((bands * tiles).bit_length() - 2, -1, -1)]


def exchange(first, second, axis):
    size = lax.axis_size(axis)
    results = []
    for message, start in ((second, 1), (first, 0)):
        pairs = [(i, i + 1) for i in range(start, size - 1, 2)]
        results.append(lax.ppermute(message(), axis, pairs + [(j, i) for i, j in pairs]))
    return results[1], results[0]


def per_device(
    features, land_mask, cell_blocks, region_ids, targets, w_embed, k_first, w_mix, k_deep, w_head
):
    rows, cols = land_mask.shape
    crows, ccols = rows // 4, cols // 4
    c_in = features.shape[2]
    chan = w_embed.shape[1]
    width = ccols + 2 * HALO
    nblk = cell_blocks.shape[-2]
    bands, tiles = lax.axis_size("band"), lax.axis_size("tile")
    ndev = bands * tiles
    share = targets.shape[0]
    share_rows = pl.next_power_of_2(pl.cdiv(share, LANES))
    msg_rows = pl.cdiv(4 + share_rows, 8) * 8

    rid = region_ids.reshape(1, nblk)
    owner, place = rid // share, rid % share
    pad = ((0, 0), (1, LANES - 1 - nblk))
    high = jnp.pad(owner * share_rows + place // LANES, pad, constant_values=-1)
    low = jnp.pad(place % LANES, pad, constant_values=-1)
    blank = jnp.zeros((1, LANES), F32)
    tgt = jnp.pad(targets, (0, share_rows * LANES - share)).reshape(share_rows, LANES)
    msg_in = jnp.concatenate(
        [blank, blank, high.astype(F32), low.astype(F32)]
        + [jnp.zeros((msg_rows - 4 - share_rows, LANES), F32), tgt],
        axis=0,
    )
    head = w_head.T.reshape(4, 4, chan).transpose(1, 0, 2).astype(F32)
    wall = jnp.broadcast_to(head[:, None], (4, crows, 4, chan)).reshape(16 * crows, chan)

    feat = features.transpose(0, 2, 1)
    msg1 = HALO * ccols + ccols // 2
    pre_first, act, bm, m2, w_wide = call(
        embed_kernel,
        [
            ((crows * ccols, chan), F32),
            ((crows, ccols, chan), BF16),
            ((ccols, LANES), F32),
            ((msg1, chan), BF16),
            ((512, chan), BF16),
        ],
        [
            ((rows, c_in, cols), BF16),
            ((16 * c_in, chan), BF16),
            ((rows, cols), jnp.int32),
            ((nblk, 1, LANES), jnp.int32),
            ((7,), None),
        ],
        hbm=4,
    )(
        *(
            pltpu.with_memory_space_constraint(x, pltpu.HBM)
            for x in (feat, w_embed, land_mask, cell_blocks.reshape(nblk, 1, LANES))
        )
    )
    def pack_first():
        return call(pack_kernel, [((msg1, chan), BF16)])(act, bm)[0]

    p1, p2 = exchange(pack_first, lambda: m2, "band")
    msg2 = HALO * (crows + 2 * HALO) + 16

    def edges(second):
        kernel = functools.partial(edges_kernel, second=second)
        return call(kernel, [((msg2, chan), BF16)])(act, bm, p1, p2)[0]

    t1, t2 = exchange(lambda: edges(False), lambda: edges(True), "tile")
    slope_first, msg_in = call(
        count_kernel, [((crows * ccols, chan), F32), ((msg_rows, LANES), F32)]
    )(pre_first, bm, msg_in)
    nrow = crows + 2 * HALO
    field, act_mix, pre_mix, pre_deep, pred, msg = call(
        forward_kernel,
        [
            ((crows + 4, width, chan), F32),
            ((crows + 2, width, chan), F32),
            ((crows + 2, width, chan), F32),
            ((crows, width, chan), F32),
            ((ccols, LANES), F32),
            ((msg_rows, LANES), F32),
        ],
        [((crows + 2, width, chan), F32)],
    )(act, bm, p1, p2, t1, t2, w_mix, k_first, k_deep, wall, msg_in)

    def slopes(after):
        return call(
            slope_kernel,
            [
                ((crows + 2, width, chan), F32),
                ((crows, width, chan), F32),
                ((rows, cols), F32),
            ],
            hbm=1,
        )(after, pre_mix, pre_deep, pred, land_mask)

    def rim(side, after):
        return call(
            functools.partial(rim_kernel, side=side),
            [((2, width, chan), F32)],
            [((4, width, chan), F32), ((2, width, chan), F32)],
            hbm=1,
        )(after, act, p1, p2, t1, t2, w_mix, k_first, k_deep, field, act_mix)

    def send(x, mask):
        pairs = [(n, n ^ mask) for n in range(ndev)]
        return lax.ppermute(x, ("tile", "band"), pairs)

    masks = hop_masks(bands, tiles)
    beside = [slopes, functools.partial(rim, 0), functools.partial(rim, 1)]
    made = []
    msgs = msg[None]
    for n, mask in enumerate(masks):
        if n < len(beside):
            made.append(beside[n](msgs))
        msgs = jnp.concatenate([msgs, send(msgs, mask)], axis=0)
    (slope_mix, slope_deep, cell_pred), (rim_above,), (rim_below,) = made

    height = ndev * share_rows
    mean, loss, grad = call(
        functools.partial(
            backward_kernel,
            share_rows=share_rows,
            share=share,
            loss_scale=1.0 / (2.0 * rows * cols * ndev),
            c_in=c_in,
        ),
        [((share_rows, LANES), F32), ((1, 1), F32), ((rows, c_in, cols), BF16)],
        [
            ((height, LANES), F32),
            ((height, LANES), F32),
            ((height, LANES), F32),
            ((nrow - 4, width, chan), F32),
            ((nrow - 4, width, chan), F32),
            ((crows, ccols, chan), BF16),
        ],
    )(
        msgs, bm, p1, p2, t1, t2, slope_deep, rim_above, rim_below, slope_mix,
        slope_first.reshape(crows, ccols, chan), w_mix, k_first, k_deep, wall, w_wide,
    )
    return (
        cell_pred,
        mean.reshape(-1)[:share],
        loss.reshape(1),
        grad.transpose(0, 2, 1),
    )


def solution(mesh):
    in_specs = (
        P(("group", "band"), "tile", None),
        P("band", "tile"),
        P("band", "tile", None, None),
        P("band", "tile", None),
        P(("group", "tile", "band")),
        P(),
        P(),
        P(),
        P(),
        P(),
    )
    out_specs = (
        P(("group", "band"), "tile"),
        P(("group", "tile", "band")),
        P("group"),
        P(("group", "band"), "tile", None),
    )
    return jax.shard_map(
        per_device, mesh=mesh, in_specs=in_specs, out_specs=out_specs, check_vma=False
    )
```

```python
import functools

import jax
import jax.numpy as jnp
from jax import lax
from jax.experimental import pallas as pl
from jax.experimental.pallas import tpu as pltpu
from jax.sharding import PartitionSpec as P

REGIONS = 14000
SQRT_HALF = 0.7071067811865476
INV_ROOT = 0.3989422804014327
F32 = jnp.float32
BF16 = jnp.bfloat16
LANES = 128
HALO = 4
OUTSIDE = -50.0
VMEM_LIMIT = 48 * 1024 * 1024


def gelu_exact(v):
    return 0.5 * v * (1.0 + lax.erf(v * SQRT_HALF))


def gelu_slope(v):
    return 0.5 * (1.0 + lax.erf(v * SQRT_HALF)) + v * jnp.exp(-0.5 * v * v) * INV_ROOT


def rounded(v):
    return v.astype(BF16).astype(F32)


def dot(a, b):
    return jnp.dot(a, b, preferred_element_type=F32)


def dot_nt(a, b):
    return lax.dot_general(a, b, (((1,), (1,)), ((), ())), preferred_element_type=F32)


def iota(shape, dim):
    return lax.broadcasted_iota(jnp.int32, shape, dim)


def spread_matrix(cols, transposed=False):
    quarter = cols // 4
    shape = (cols, cols)
    n = iota(shape, 0)
    c = iota(shape, 1)
    return jnp.where(c == 4 * (n % quarter) + n // quarter, 1.0, 0.0).astype(BF16)


def padded_embed(w_ref, c_in, c_pad):
    w = w_ref[...].astype(F32)
    zeros = jnp.zeros((c_pad - c_in, w.shape[1]), F32)
    parts = []
    for b in range(4):
        for a in range(4):
            start = (4 * a + b) * c_in
            parts += [w[start : start + c_in], zeros]
    return jnp.concatenate(parts, axis=0).astype(BF16)


def parity(axis):
    return lax.axis_index(axis) % 2


def embed_kernel(
    feat_hbm, w_hbm, land_hbm, blocks_hbm, pre_out, act_out, bm_out, m2_out, w_out,
    feat, w_embed, land, blocks, sems,
):
    rows, c_in, cols = feat.shape
    part = rows // 4
    pairs = [(blocks_hbm, blocks), (land_hbm, land), (w_hbm, w_embed)]
    pairs += [
        (feat_hbm.at[pl.ds(part * n, part)], feat.at[pl.ds(part * n, part)]) for n in range(4)
    ]
    copies = [pltpu.make_async_copy(src, dst, sems.at[n]) for n, (src, dst) in enumerate(pairs)]
    for copy in copies:
        copy.start()
    c_pad = 32
    crows, ccols = rows // 4, cols // 4
    nblk = blocks.shape[0]
    spread = spread_matrix(cols)

    for copy in copies:
        copy.wait()
    shift_row = cols.bit_length() - 1
    chunk = next(c for c in (9, 8, 7, 6, 5, 4, 3, 2, 1) if nblk % c == 0)
    total = jnp.zeros((ccols, LANES), F32)
    sub_a = iota((LANES, LANES), 0).astype(F32).astype(BF16)
    sub_b = iota((ccols, LANES), 0).astype(F32).astype(BF16)
    one, none = jnp.ones((), BF16), jnp.zeros((), BF16)
    cells = blocks[...].reshape(nblk, LANES)
    named = cells < rows * cols
    all_q = jnp.where(named, (cells & 3) * rows + (cells >> shift_row), -1).astype(F32)
    all_j = ((cells & (cols - 1)) >> 2).astype(F32)
    for first in range(0, nblk, chunk):
        hot_q, hot_j = [], []
        for k in range(first, first + chunk):
            q = all_q[k : k + 1].astype(BF16)
            j = all_j[k : k + 1].astype(BF16)
            hot_q.append(jnp.where(sub_a == q, one, none))
            hot_j.append(jnp.where(sub_b == j, jnp.array(k + 1, BF16), none))
        total = total + dot_nt(
            jnp.concatenate(hot_j, axis=1), jnp.concatenate(hot_q, axis=1)
        )
    land_moved = dot_nt(spread, land[...].astype(F32).astype(BF16))
    land_q = jnp.concatenate(
        [land_moved[b * ccols : (b + 1) * ccols, :] for b in range(4)], axis=1
    )
    bm = total * land_q
    bm_out[...] = bm

    field = feat[...].astype(F32)
    field = jnp.concatenate([field, jnp.zeros((rows, c_pad - c_in, cols), F32)], axis=1)
    field = field.reshape(rows * c_pad, cols).astype(BF16)
    moved = dot_nt(spread, field).astype(BF16)
    wide = 4 * c_pad
    lhs = jnp.concatenate(
        [
            jnp.concatenate(
                [
                    moved[b * ccols : (b + 1) * ccols, i * wide : (i + 1) * wide]
                    for b in range(4)
                ],
                axis=1,
            )
            for i in range(crows)
        ],
        axis=0,
    )
    weights = padded_embed(w_embed, c_in, c_pad)
    w_out[...] = weights
    pre = dot(lhs, weights)
    chan = pre.shape[1]
    pre_out[...] = pre
    act_out[...] = gelu_exact(pre).astype(BF16).reshape(crows, ccols, chan)
    pack(act_out, bm, parity("band"), m2_out)


def pack(act, bm, low, out):
    crows, ccols, chan = act.shape
    half = ccols // 2
    start = low * (crows - HALO)
    out[0 : HALO * ccols] = act[pl.ds(start, HALO)].reshape(HALO * ccols, chan)
    out[HALO * ccols :] = jnp.concatenate([bm[:half], bm[half:]], axis=1).astype(BF16)


def pack_kernel(act, bm, m1_out):
    pack(act, bm[...], 1 - parity("band"), m1_out)


def edges_kernel(act, bm, p1, p2, out, second):
    crows, ccols, chan = act.shape
    odd_b = parity("band") == 1
    odd_t = parity("tile") == 1
    n = HALO * ccols
    up = jnp.where(odd_b, p1[...].astype(F32), p2[...].astype(F32))
    down = jnp.where(odd_b, p2[...].astype(F32), p1[...].astype(F32))
    left, right = [], []
    for r in range(crows + 2 * HALO):
        if r < HALO:
            row = up[r * ccols : (r + 1) * ccols]
        elif r < HALO + crows:
            row = act[r - HALO].astype(F32)
        else:
            row = down[(r - HALO - crows) * ccols : (r - HALO - crows + 1) * ccols]
        left.append(row[:HALO])
        right.append(row[ccols - HALO :])
    half = ccols // 2
    own = bm[...]
    zeros = jnp.zeros((10, LANES), F32)
    bm_left = [up[n : n + 2, :LANES], own[0:2], down[n : n + 2, :LANES], zeros]
    bm_right = [
        up[n + half - 2 : n + half, LANES:],
        own[ccols - 2 :],
        down[n + half - 2 : n + half, LANES:],
        zeros,
    ]
    def message(cells, maps):
        maps = jnp.concatenate(maps, axis=0)
        maps = jnp.concatenate([maps, jnp.zeros((16, chan - LANES), F32)], axis=1)
        return jnp.concatenate(cells + [maps], axis=0)

    left = message(left, bm_left)
    right = message(right, bm_right)
    low = ~odd_t if second else odd_t
    out[...] = jnp.where(low, left, right).astype(BF16)


def conv_pass(src, count, kernel, emit, chan):
    width = src.shape[1]
    for h in range(0, chan, LANES):
        span = slice(h, h + LANES)
        taps = [kernel[t : t + 1, span] for t in range(9)]
        sums = [None] * (count - 2)
        for r in range(count):
            x = src[r, :, span]
            before = pltpu.roll(x, 1, 0)
            after = pltpu.roll(x, width - 1, 0)
            for a in range(3):
                if 0 <= r - a < count - 2:
                    part = taps[3 * a] * before + taps[3 * a + 1] * x + taps[3 * a + 2] * after
                    sums[r - a] = part if a == 0 else sums[r - a] + part
            if r >= 2:
                emit(r - 2, span, sums[r - 2])


def halo_rows(act, p1, p2, t1, t2):
    crows, ccols, chan = act.shape
    odd_b = parity("band") == 1
    odd_t = parity("tile") == 1

    def edge(first, second, odd, at, n):
        return jnp.where(odd, first[at : at + n].astype(F32), second[at : at + n].astype(F32))

    def row(r):
        if r < HALO:
            own = edge(p1, p2, odd_b, r * ccols, ccols)
        elif r < HALO + crows:
            own = act[r - HALO].astype(F32)
        else:
            own = edge(p2, p1, odd_b, (r - HALO - crows) * ccols, ccols)
        base = HALO * r // 16 * 16
        at = HALO * r - base
        left = edge(t1, t2, odd_t, base, 16)[at : at + HALO]
        right = edge(t2, t1, odd_t, base, 16)[at : at + HALO]
        return own, jnp.concatenate([right, left], axis=0)

    return row


def inside_columns(shape, ccols):
    tile = lax.axis_index("tile")
    first = tile == 0
    last = tile == lax.axis_size("tile") - 1
    col = iota(shape, len(shape) - 2)
    low = jnp.where(last, ccols, ccols + HALO)
    high = jnp.where(first, ccols + 2 * HALO, ccols + HALO)
    return (col < low) | (col >= high)


def mix_pair(pair, base, weights, ok):
    _, width, chan = pair.shape
    pre = dot(pair.reshape(2 * width, chan).astype(BF16), weights).reshape(2, width, chan)
    pre = jnp.where(ok, pre, OUTSIDE)
    return pre, rounded(base + gelu_exact(pre))


def forward_kernel(
    act, bm, p1, p2, t1, t2, w_mix, k_first, k_deep, wall, msg_in,
    field, act_mix, pre_mix, pre_deep, pred_out, msg_out, mixed,
):
    crows, ccols, chan = act.shape
    width = ccols + 2 * HALO
    row = halo_rows(act, p1, p2, t1, t2)
    for r in range(crows + 4):
        own, edge = row(r + 2)
        field[r, 0:ccols, :] = own
        field[r, ccols:, :] = edge

    def keep_mixed(r, span, value):
        mixed[r, :, span] = value

    conv_pass(field, crows + 4, k_first[...].astype(F32), keep_mixed, chan)

    shape = (2, width, chan)
    col_ok = inside_columns(shape, ccols)
    band = lax.axis_index("band")
    first_row = jnp.where(band == 0, 1, 0)
    last_row = jnp.where(band == lax.axis_size("band") - 1, crows + 1, crows + 2)
    weights = w_mix[...]
    for g in range((crows + 2) // 2):
        at = iota(shape, 0) + 2 * g
        ok = col_ok & (at >= first_row) & (at < last_row)
        pair = slice(2 * g, 2 * g + 2)
        pre, post = mix_pair(mixed[pair], field[2 * g + 1 : 2 * g + 3], weights, ok)
        pre_mix[pair] = pre
        act_mix[pair] = post

    def keep_deep(r, span, value):
        pre_deep[r, :, span] = value

    conv_pass(act_mix, crows + 2, k_deep[...].astype(F32), keep_deep, chan)

    head = wall[...]
    head_row = (iota(head.shape, 0) % (4 * crows)) // 4
    pred = jnp.zeros((ccols, LANES), F32)
    for i in range(crows):
        out = act_mix[i + 1, 0:ccols, :] + gelu_exact(pre_deep[i, 0:ccols, :])
        pred = pred + dot_nt(
            out.astype(BF16), jnp.where(head_row == i, head, 0.0).astype(BF16)
        )
    pred_out[...] = pred

    maps = bm[...]
    slots = iota((LANES, LANES), 0).astype(F32)[:88]
    sums = jnp.zeros((88, LANES), F32)
    for j in range(ccols):
        sums = sums + jnp.where(maps[j : j + 1, :] == slots, pred[j : j + 1, :], 0.0)
    msg_out[...] = msg_in[...]
    msg_out[0:1, :] = across_lanes(sums)


def across_lanes(acc):
    rest = jnp.zeros((LANES - acc.shape[0], LANES), F32)
    turned = jnp.concatenate([acc, rest], axis=0).T
    total = jnp.sum(turned, axis=0, keepdims=True)
    return jnp.where(iota((1, LANES), 1) > 0, total, 0.0)


def count_kernel(pre_first, bm, msg_in, slope_first, msg_out):
    slope_first[...] = gelu_slope(pre_first[...])
    maps = bm[...]
    slots = iota((LANES, LANES), 0).astype(F32)[:88]
    counts = jnp.zeros((88, LANES), F32)
    for j in range(maps.shape[0]):
        counts = counts + jnp.where(maps[j : j + 1, :] == slots, 1.0, 0.0)
    msg_out[...] = msg_in[...]
    msg_out[1:2, :] = across_lanes(counts)


def rim_kernel(
    after, act, p1, p2, t1, t2, w_mix, k_first, k_deep, field, act_mix, slope_rim,
    ext, mixed, side,
):
    del after
    crows, ccols, chan = act.shape
    width = ccols + 2 * HALO
    row = halo_rows(act, p1, p2, t1, t2)
    outer = (0, 1) if side == 0 else (crows + 6, crows + 7)
    inner = (0, 1) if side == 0 else (crows + 2, crows + 3)
    near = (2, 3) if side == 0 else (0, 1)
    far = (0, 1) if side == 0 else (2, 3)
    for r, at in zip(outer, far):
        own, edge = row(r)
        ext[at, 0:ccols, :] = own
        ext[at, ccols:, :] = edge
    for r, at in zip(inner, near):
        ext[at] = field[r]

    def keep(r, span, value):
        mixed[r, :, span] = value

    conv_pass(ext, 4, k_first[...].astype(F32), keep, chan)
    edge_band = 0 if side == 0 else lax.axis_size("band") - 1
    ok = inside_columns((2, width, chan), ccols) & (lax.axis_index("band") != edge_band)
    _, post = mix_pair(mixed[...], ext[1:3], w_mix[...], ok)
    have = (0, 1) if side == 0 else (crows, crows + 1)
    for n in range(2):
        ext[far[n]] = post[n]
        ext[near[n]] = act_mix[have[n]]
    conv_pass(ext, 4, k_deep[...].astype(F32), keep, chan)
    slope_rim[...] = gelu_slope(mixed[...])


def slope_kernel(after, mix, deep, pred, land, slope_mix, slope_deep, cells):
    del after
    slope_mix[...] = gelu_slope(mix[...])
    slope_deep[...] = gelu_slope(deep[...])
    rows, cols = land.shape
    turned = pred[...].T
    wide = jnp.concatenate([turned[b * rows : (b + 1) * rows] for b in range(4)], axis=1)
    high = wide.astype(BF16)
    low = (wide - high.astype(F32)).astype(BF16)
    spread = spread_matrix(cols)
    cells[...] = (dot(high, spread) + dot(low, spread)) * land[...].astype(F32)


def backward_kernel(
    gathered, bm, p1, p2, t1, t2, slope_deep, rim_above, rim_below, slope_mix,
    slope_first,
    w_mix, k_first, k_deep, wall, w_wide,
    mean_out, loss_out, grad_out,
    targets, table, grads, field, mixing, proj, share_rows, share, loss_scale, c_in,
):
    ndev = gathered.shape[0]
    crows = slope_first.shape[0]
    ccols = slope_first.shape[1]
    chan = slope_first.shape[2]
    width = ccols + 2 * HALO
    band, tile = lax.axis_index("band"), lax.axis_index("tile")
    bands, tiles = lax.axis_size("band"), lax.axis_size("tile")
    me = tile * bands + band
    masks = hop_masks(bands, tiles)

    def slot_at(owner):
        apart = owner ^ me
        return sum(jnp.where(apart & mask > 0, 2**n, 0) for n, mask in enumerate(masks))

    def slot_of(v, t):
        other_band, other_tile = band + v, tile + t
        ok = (other_band >= 0) & (other_band < bands) & (other_tile >= 0) & (other_tile < tiles)
        return jnp.where(ok, slot_at(other_tile * bands + other_band), 0)

    height = ndev * share_rows
    chunk = min(16, ndev)
    first_target = gathered.shape[1] - share_rows
    sub = iota((height, LANES), 0).astype(F32).astype(BF16)
    sub_lo = iota((LANES, LANES), 0).astype(F32).astype(BF16)
    one, none = jnp.ones((), BF16), jnp.zeros((), BF16)

    def gather_chunk(c, acc):
        hot_hi, hot_lo = [], []
        for o in range(chunk):
            owner = c * chunk + o
            m = gathered[slot_at(owner)]
            hot_hi.append(jnp.where(sub == m[2:3].astype(BF16), one, none))
            low_hit = sub_lo == m[3:4].astype(BF16)
            high = rounded(m[0:1])
            parts = [high, m[0:1] - high, m[1:2]]
            hot_lo.append(
                jnp.concatenate(
                    [jnp.where(low_hit, part.astype(BF16), none) for part in parts], axis=0
                )
            )
            targets[pl.ds(owner * share_rows, share_rows)] = m[first_target:]
        return acc + dot_nt(
            jnp.concatenate(hot_hi, axis=1), jnp.concatenate(hot_lo, axis=1)
        )

    acc = jnp.zeros((height, 3 * LANES), F32)
    if ndev == chunk:
        acc = gather_chunk(0, acc)
    else:
        acc = lax.fori_loop(0, ndev // chunk, gather_chunk, acc)
    region_sum = acc[:, :LANES] + acc[:, LANES : 2 * LANES]
    region_count = acc[:, 2 * LANES :]
    at_least = jnp.maximum(region_count, 1.0)
    mean = region_sum / at_least
    table[...] = mean
    misfit = mean - targets[...]
    row = iota((height, LANES), 0)
    place = (row % share_rows) * LANES + iota((height, LANES), 1)
    inside = (place < share) & ((row // share_rows) * share + place < REGIONS)
    terms = jnp.where(inside, region_count * misfit * misfit, 0.0)
    loss_out[...] = jnp.sum(
        jnp.sum(terms, axis=0, keepdims=True), axis=1, keepdims=True
    ) * loss_scale
    grads[...] = jnp.where(inside, region_count * misfit / at_least, 0.0)
    mean_out[...] = table[pl.ds(me * share_rows, share_rows)]

    sub8 = iota((8, LANES), 0).astype(F32)

    def block_grads(slot):
        m = gathered[slot]
        low = jnp.broadcast_to(jnp.maximum(m[3:4], 0.0), (8, LANES)).astype(jnp.int32)
        high = m[2:3]
        total = jnp.zeros((8, LANES), F32)
        for at in range(0, height, 8):
            found = jnp.take_along_axis(grads[at : at + 8], low, axis=1)
            total = total + jnp.where(high == sub8 + float(at), found, 0.0)
        return jnp.sum(total, axis=0, keepdims=True)

    n = HALO * ccols
    half = ccols // 2
    odd_b = parity("band") == 1
    odd_t = parity("tile") == 1
    up = jnp.where(odd_b, p1[n:].astype(F32), p2[n:].astype(F32))
    down = jnp.where(odd_b, p2[n:].astype(F32), p1[n:].astype(F32))
    m = HALO * (crows + 2 * HALO)
    left = jnp.where(odd_t, t1[m:].astype(F32), t2[m:].astype(F32))[:, :LANES]
    right = jnp.where(odd_t, t2[m:].astype(F32), t1[m:].astype(F32))[:, :LANES]
    maps = [
        jnp.concatenate([up[:, :LANES], up[:, LANES:]], axis=0),
        bm[...],
        jnp.concatenate([down[:, :LANES], down[:, LANES:]], axis=0),
    ]
    cells = []
    gap = jnp.zeros((4, LANES), F32)
    for v in range(3):
        mid = block_grads(slot_of(v - 1, 0))
        lo = block_grads(slot_of(v - 1, -1))
        hi = block_grads(slot_of(v - 1, 1))
        source = jnp.broadcast_to(mid, (8, LANES))
        parts = [
            jnp.take_along_axis(source, maps[v][at : at + 8].astype(jnp.int32), axis=1)
            for at in range(0, ccols, 8)
        ]
        edge = jnp.concatenate(
            [right[2 * v : 2 * v + 2], gap, left[2 * v : 2 * v + 2]], axis=0
        ).astype(jnp.int32)
        source = jnp.concatenate(
            [jnp.broadcast_to(hi, (4, LANES)), jnp.broadcast_to(lo, (4, LANES))], axis=0
        )
        parts.append(jnp.take_along_axis(source, edge, axis=1))
        cells.append(jnp.concatenate(parts, axis=0).astype(BF16))

    head = wall[...]
    head_row = (iota(head.shape, 0) % (4 * crows)) // 4
    nrow = crows + 4
    for r in range(nrow):
        v = 0 if r < 2 else 1 if r < crows + 2 else 2
        i = (crows - 2 + r) if v == 0 else (r - 2) if v == 1 else r - crows - 2
        weights = jnp.where(head_row == i, head, 0.0).astype(BF16)
        deep = rounded(dot(cells[v], weights))
        mixing[r] = deep
        slope = rim_above[r] if v == 0 else slope_deep[i] if v == 1 else rim_below[r - crows - 2]
        field[r] = deep * slope

    def keep_mix(r, span, value):
        mixing[r + 1, :, span] = rounded(mixing[r + 1, :, span] + value)

    def reversed_taps(k):
        k = k[...].astype(F32)
        return jnp.concatenate([k[t : t + 1] for t in range(8, -1, -1)], axis=0)

    conv_pass(field, nrow, reversed_taps(k_deep), keep_mix, chan)
    weights = w_mix[...]

    for g in range((nrow - 2) // 2):
        pre = (mixing[2 * g + 1 : 2 * g + 3] * slope_mix[2 * g : 2 * g + 2]).reshape(
            2 * width, chan
        )
        field[2 * g : 2 * g + 2] = dot_nt(pre.astype(BF16), weights).reshape(2, width, chan)

    def keep_first(r, span, value):
        total = mixing[r + 2, 0:ccols, span] + value[0:ccols]
        proj[r, :, span] = (total * slope_first[r, :, span]).astype(BF16)

    conv_pass(field, nrow - 2, reversed_taps(k_first), keep_first, chan)

    c_pad = 32
    out = dot_nt(w_wide[...], proj[...].reshape(crows * ccols, chan))
    wide = 4 * c_pad
    spread = spread_matrix(4 * ccols)
    group = crows // 4
    for g in range(4):
        lhs = jnp.concatenate(
            [
                jnp.concatenate(
                    [
                        out[b * wide : (b + 1) * wide, i * ccols : (i + 1) * ccols]
                        for b in range(4)
                    ],
                    axis=1,
                )
                for i in range(g * group, (g + 1) * group)
            ],
            axis=0,
        )
        fine = dot(lhs.astype(BF16), spread)
        for r in range(4 * group):
            grad_out[4 * group * g + r] = fine[r * c_pad : r * c_pad + c_in].astype(BF16)


def call(kernel, outs, scratch=(), hbm=0):
    def run(*args):
        space = [pl.BlockSpec(memory_space=pl.ANY)] * hbm
        space += [pl.BlockSpec(memory_space=pltpu.VMEM)] * (len(args) - hbm)
        return pl.pallas_call(
            kernel,
            out_shape=[jax.ShapeDtypeStruct(s, d) for s, d in outs],
            in_specs=space,
            out_specs=[pl.BlockSpec(memory_space=pltpu.VMEM)] * len(outs),
            scratch_shapes=[
                pltpu.SemaphoreType.DMA(s) if d is None else pltpu.VMEM(s, d)
                for s, d in scratch
            ],
            compiler_params=pltpu.CompilerParams(vmem_limit_bytes=VMEM_LIMIT),
            cost_estimate=pl.CostEstimate(
                flops=10**6, bytes_accessed=10**6, transcendentals=0
            ),
        )(*args)

    return run


def hop_masks(bands, tiles):
    return [2**n for n in range((bands * tiles).bit_length() - 2, -1, -1)]


def exchange(first, second, axis):
    size = lax.axis_size(axis)
    results = []
    for message, start in ((second, 1), (first, 0)):
        pairs = [(i, i + 1) for i in range(start, size - 1, 2)]
        results.append(lax.ppermute(message(), axis, pairs + [(j, i) for i, j in pairs]))
    return results[1], results[0]


def per_device(
    features, land_mask, cell_blocks, region_ids, targets, w_embed, k_first, w_mix, k_deep, w_head
):
    rows, cols = land_mask.shape
    crows, ccols = rows // 4, cols // 4
    c_in = features.shape[2]
    chan = w_embed.shape[1]
    width = ccols + 2 * HALO
    nblk = cell_blocks.shape[-2]
    bands, tiles = lax.axis_size("band"), lax.axis_size("tile")
    ndev = bands * tiles
    share = targets.shape[0]
    share_rows = pl.next_power_of_2(pl.cdiv(share, LANES))
    msg_rows = pl.cdiv(4 + share_rows, 8) * 8

    rid = region_ids.reshape(1, nblk)
    owner, place = rid // share, rid % share
    pad = ((0, 0), (1, LANES - 1 - nblk))
    high = jnp.pad(owner * share_rows + place // LANES, pad, constant_values=-1)
    low = jnp.pad(place % LANES, pad, constant_values=-1)
    blank = jnp.zeros((1, LANES), F32)
    tgt = jnp.pad(targets, (0, share_rows * LANES - share)).reshape(share_rows, LANES)
    msg_in = jnp.concatenate(
        [blank, blank, high.astype(F32), low.astype(F32)]
        + [jnp.zeros((msg_rows - 4 - share_rows, LANES), F32), tgt],
        axis=0,
    )
    head = w_head.T.reshape(4, 4, chan).transpose(1, 0, 2).astype(F32)
    wall = jnp.broadcast_to(head[:, None], (4, crows, 4, chan)).reshape(16 * crows, chan)

    feat = features.transpose(0, 2, 1)
    msg1 = HALO * ccols + ccols // 2
    pre_first, act, bm, m2, w_wide = call(
        embed_kernel,
        [
            ((crows * ccols, chan), F32),
            ((crows, ccols, chan), BF16),
            ((ccols, LANES), F32),
            ((msg1, chan), BF16),
            ((512, chan), BF16),
        ],
        [
            ((rows, c_in, cols), BF16),
            ((16 * c_in, chan), BF16),
            ((rows, cols), jnp.int32),
            ((nblk, 1, LANES), jnp.int32),
            ((7,), None),
        ],
        hbm=4,
    )(
        *(
            pltpu.with_memory_space_constraint(x, pltpu.HBM)
            for x in (feat, w_embed, land_mask, cell_blocks.reshape(nblk, 1, LANES))
        )
    )
    def pack_first():
        return call(pack_kernel, [((msg1, chan), BF16)])(act, bm)[0]

    p1, p2 = exchange(pack_first, lambda: m2, "band")
    msg2 = HALO * (crows + 2 * HALO) + 16

    def edges(second):
        kernel = functools.partial(edges_kernel, second=second)
        return call(kernel, [((msg2, chan), BF16)])(act, bm, p1, p2)[0]

    t1, t2 = exchange(lambda: edges(False), lambda: edges(True), "tile")
    slope_first, msg_in = call(
        count_kernel, [((crows * ccols, chan), F32), ((msg_rows, LANES), F32)]
    )(pre_first, bm, msg_in)
    nrow = crows + 2 * HALO
    field, act_mix, pre_mix, pre_deep, pred, msg = call(
        forward_kernel,
        [
            ((crows + 4, width, chan), F32),
            ((crows + 2, width, chan), F32),
            ((crows + 2, width, chan), F32),
            ((crows, width, chan), F32),
            ((ccols, LANES), F32),
            ((msg_rows, LANES), F32),
        ],
        [((crows + 2, width, chan), F32)],
    )(act, bm, p1, p2, t1, t2, w_mix, k_first, k_deep, wall, msg_in)

    def slopes(after):
        return call(
            slope_kernel,
            [
                ((crows + 2, width, chan), F32),
                ((crows, width, chan), F32),
                ((rows, cols), F32),
            ],
            hbm=1,
        )(after, pre_mix, pre_deep, pred, land_mask)

    def rim(side, after):
        return call(
            functools.partial(rim_kernel, side=side),
            [((2, width, chan), F32)],
            [((4, width, chan), F32), ((2, width, chan), F32)],
            hbm=1,
        )(after, act, p1, p2, t1, t2, w_mix, k_first, k_deep, field, act_mix)

    def send(x, mask):
        pairs = [(n, n ^ mask) for n in range(ndev)]
        return lax.ppermute(x, ("tile", "band"), pairs)

    masks = hop_masks(bands, tiles)
    beside = [slopes, functools.partial(rim, 0), functools.partial(rim, 1)]
    made = []
    msgs = msg[None]
    for n, mask in enumerate(masks):
        if n < len(beside):
            made.append(beside[n](msgs))
        msgs = jnp.concatenate([msgs, send(msgs, mask)], axis=0)
    (slope_mix, slope_deep, cell_pred), (rim_above,), (rim_below,) = made

    height = ndev * share_rows
    mean, loss, grad = call(
        functools.partial(
            backward_kernel,
            share_rows=share_rows,
            share=share,
            loss_scale=1.0 / (2.0 * rows * cols * ndev),
            c_in=c_in,
        ),
        [((share_rows, LANES), F32), ((1, 1), F32), ((rows, c_in, cols), BF16)],
        [
            ((height, LANES), F32),
            ((height, LANES), F32),
            ((height, LANES), F32),
            ((nrow - 4, width, chan), F32),
            ((nrow - 4, width, chan), F32),
            ((crows, ccols, chan), BF16),
        ],
    )(
        msgs, bm, p1, p2, t1, t2, slope_deep, rim_above, rim_below, slope_mix,
        slope_first.reshape(crows, ccols, chan), w_mix, k_first, k_deep, wall, w_wide,
    )
    return (
        cell_pred,
        mean.reshape(-1)[:share],
        loss.reshape(1),
        grad.transpose(0, 2, 1),
    )


def solution(mesh):
    in_specs = (
        P(("group", "band"), "tile", None),
        P("band", "tile"),
        P("band", "tile", None, None),
        P("band", "tile", None),
        P(("group", "tile", "band")),
        P(),
        P(),
        P(),
        P(),
        P(),
    )
    out_specs = (
        P(("group", "band"), "tile"),
        P(("group", "tile", "band")),
        P("group"),
        P(("group", "band"), "tile", None),
    )
    return jax.shard_map(
        per_device, mesh=mesh, in_specs=in_specs, out_specs=out_specs, check_vma=False
    )
```

```python
import functools

import jax
import jax.numpy as jnp
from jax import lax
from jax.experimental import pallas as pl
from jax.experimental.pallas import tpu as pltpu
from jax.sharding import PartitionSpec as P

REGIONS = 14000
SQRT_HALF = 0.7071067811865476
INV_ROOT = 0.3989422804014327
F32 = jnp.float32
BF16 = jnp.bfloat16
LANES = 128
HALO = 4
OUTSIDE = -50.0
VMEM_LIMIT = 48 * 1024 * 1024


def gelu_exact(v):
    return 0.5 * v * (1.0 + lax.erf(v * SQRT_HALF))


def gelu_slope(v):
    return 0.5 * (1.0 + lax.erf(v * SQRT_HALF)) + v * jnp.exp(-0.5 * v * v) * INV_ROOT


def rounded(v):
    return v.astype(BF16).astype(F32)


def dot(a, b):
    return jnp.dot(a, b, preferred_element_type=F32)


def dot_nt(a, b):
    return lax.dot_general(a, b, (((1,), (1,)), ((), ())), preferred_element_type=F32)


def iota(shape, dim):
    return lax.broadcasted_iota(jnp.int32, shape, dim)


def spread_matrix(cols, transposed=False):
    quarter = cols // 4
    shape = (cols, cols)
    n = iota(shape, 0)
    c = iota(shape, 1)
    return jnp.where(c == 4 * (n % quarter) + n // quarter, 1.0, 0.0).astype(BF16)


def padded_embed(w_ref, c_in, c_pad):
    w = w_ref[...].astype(F32)
    zeros = jnp.zeros((c_pad - c_in, w.shape[1]), F32)
    parts = []
    for b in range(4):
        for a in range(4):
            start = (4 * a + b) * c_in
            parts += [w[start : start + c_in], zeros]
    return jnp.concatenate(parts, axis=0).astype(BF16)


def parity(axis):
    return lax.axis_index(axis) % 2


def embed_kernel(
    feat_hbm, w_hbm, land_hbm, blocks_hbm, pre_out, act_out, bm_out, m2_out, w_out,
    feat, w_embed, land, blocks, sems,
):
    rows, c_in, cols = feat.shape
    part = rows // 4
    pairs = [(blocks_hbm, blocks), (land_hbm, land), (w_hbm, w_embed)]
    pairs += [
        (feat_hbm.at[pl.ds(part * n, part)], feat.at[pl.ds(part * n, part)]) for n in range(4)
    ]
    copies = [pltpu.make_async_copy(src, dst, sems.at[n]) for n, (src, dst) in enumerate(pairs)]
    for copy in copies:
        copy.start()
    c_pad = 32
    crows, ccols = rows // 4, cols // 4
    nblk = blocks.shape[0]
    spread = spread_matrix(cols)

    for copy in copies:
        copy.wait()
    shift_row = cols.bit_length() - 1
    chunk = next(c for c in (9, 8, 7, 6, 5, 4, 3, 2, 1) if nblk % c == 0)
    total = jnp.zeros((ccols, LANES), F32)
    sub_a = iota((LANES, LANES), 0).astype(F32).astype(BF16)
    sub_b = iota((ccols, LANES), 0).astype(F32).astype(BF16)
    one, none = jnp.ones((), BF16), jnp.zeros((), BF16)
    cells = blocks[...].reshape(nblk, LANES)
    named = cells < rows * cols
    all_q = jnp.where(named, (cells & 3) * rows + (cells >> shift_row), -1).astype(F32)
    all_j = ((cells & (cols - 1)) >> 2).astype(F32)
    for first in range(0, nblk, chunk):
        hot_q, hot_j = [], []
        for k in range(first, first + chunk):
            q = all_q[k : k + 1].astype(BF16)
            j = all_j[k : k + 1].astype(BF16)
            hot_q.append(jnp.where(sub_a == q, one, none))
            hot_j.append(jnp.where(sub_b == j, jnp.array(k + 1, BF16), none))
        total = total + dot_nt(
            jnp.concatenate(hot_j, axis=1), jnp.concatenate(hot_q, axis=1)
        )
    land_moved = dot_nt(spread, land[...].astype(F32).astype(BF16))
    land_q = jnp.concatenate(
        [land_moved[b * ccols : (b + 1) * ccols, :] for b in range(4)], axis=1
    )
    bm = total * land_q
    bm_out[...] = bm

    field = feat[...].astype(F32)
    field = jnp.concatenate([field, jnp.zeros((rows, c_pad - c_in, cols), F32)], axis=1)
    field = field.reshape(rows * c_pad, cols).astype(BF16)
    moved = dot_nt(spread, field).astype(BF16)
    wide = 4 * c_pad
    lhs = jnp.concatenate(
        [
            jnp.concatenate(
                [
                    moved[b * ccols : (b + 1) * ccols, i * wide : (i + 1) * wide]
                    for b in range(4)
                ],
                axis=1,
            )
            for i in range(crows)
        ],
        axis=0,
    )
    weights = padded_embed(w_embed, c_in, c_pad)
    w_out[...] = weights
    pre = dot(lhs, weights)
    chan = pre.shape[1]
    pre_out[...] = pre
    act_out[...] = gelu_exact(pre).astype(BF16).reshape(crows, ccols, chan)
    pack(act_out, bm, parity("band"), m2_out)


def pack(act, bm, low, out):
    crows, ccols, chan = act.shape
    half = ccols // 2
    start = low * (crows - HALO)
    out[0 : HALO * ccols] = act[pl.ds(start, HALO)].reshape(HALO * ccols, chan)
    out[HALO * ccols :] = jnp.concatenate([bm[:half], bm[half:]], axis=1).astype(BF16)


def pack_kernel(act, bm, m1_out):
    pack(act, bm[...], 1 - parity("band"), m1_out)


def edges_kernel(act, bm, p1, p2, out, second):
    crows, ccols, chan = act.shape
    odd_b = parity("band") == 1
    odd_t = parity("tile") == 1
    n = HALO * ccols
    up = jnp.where(odd_b, p1[...].astype(F32), p2[...].astype(F32))
    down = jnp.where(odd_b, p2[...].astype(F32), p1[...].astype(F32))
    left, right = [], []
    for r in range(crows + 2 * HALO):
        if r < HALO:
            row = up[r * ccols : (r + 1) * ccols]
        elif r < HALO + crows:
            row = act[r - HALO].astype(F32)
        else:
            row = down[(r - HALO - crows) * ccols : (r - HALO - crows + 1) * ccols]
        left.append(row[:HALO])
        right.append(row[ccols - HALO :])
    half = ccols // 2
    own = bm[...]
    zeros = jnp.zeros((10, LANES), F32)
    bm_left = [up[n : n + 2, :LANES], own[0:2], down[n : n + 2, :LANES], zeros]
    bm_right = [
        up[n + half - 2 : n + half, LANES:],
        own[ccols - 2 :],
        down[n + half - 2 : n + half, LANES:],
        zeros,
    ]
    def message(cells, maps):
        maps = jnp.concatenate(maps, axis=0)
        maps = jnp.concatenate([maps, jnp.zeros((16, chan - LANES), F32)], axis=1)
        return jnp.concatenate(cells + [maps], axis=0)

    left = message(left, bm_left)
    right = message(right, bm_right)
    low = ~odd_t if second else odd_t
    out[...] = jnp.where(low, left, right).astype(BF16)


def conv_pass(src, count, kernel, emit, chan):
    width = src.shape[1]
    for h in range(0, chan, LANES):
        span = slice(h, h + LANES)
        taps = [kernel[t : t + 1, span] for t in range(9)]
        sums = [None] * (count - 2)
        for r in range(count):
            x = src[r, :, span]
            before = pltpu.roll(x, 1, 0)
            after = pltpu.roll(x, width - 1, 0)
            for a in range(3):
                if 0 <= r - a < count - 2:
                    part = taps[3 * a] * before + taps[3 * a + 1] * x + taps[3 * a + 2] * after
                    sums[r - a] = part if a == 0 else sums[r - a] + part
            if r >= 2:
                emit(r - 2, span, sums[r - 2])


def halo_rows(act, p1, p2, t1, t2):
    crows, ccols, chan = act.shape
    odd_b = parity("band") == 1
    odd_t = parity("tile") == 1

    def edge(first, second, odd, at, n):
        return jnp.where(odd, first[at : at + n].astype(F32), second[at : at + n].astype(F32))

    def row(r):
        if r < HALO:
            own = edge(p1, p2, odd_b, r * ccols, ccols)
        elif r < HALO + crows:
            own = act[r - HALO].astype(F32)
        else:
            own = edge(p2, p1, odd_b, (r - HALO - crows) * ccols, ccols)
        base = HALO * r // 16 * 16
        at = HALO * r - base
        left = edge(t1, t2, odd_t, base, 16)[at : at + HALO]
        right = edge(t2, t1, odd_t, base, 16)[at : at + HALO]
        return own, jnp.concatenate([right, left], axis=0)

    return row


def inside_columns(shape, ccols):
    tile = lax.axis_index("tile")
    first = tile == 0
    last = tile == lax.axis_size("tile") - 1
    col = iota(shape, len(shape) - 2)
    low = jnp.where(last, ccols, ccols + HALO)
    high = jnp.where(first, ccols + 2 * HALO, ccols + HALO)
    return (col < low) | (col >= high)


def mix_pair(pair, base, weights, ok):
    _, width, chan = pair.shape
    pre = dot(pair.reshape(2 * width, chan).astype(BF16), weights).reshape(2, width, chan)
    pre = jnp.where(ok, pre, OUTSIDE)
    return pre, rounded(base + gelu_exact(pre))


def forward_kernel(
    act, bm, p1, p2, t1, t2, w_mix, k_first, k_deep, wall, msg_in,
    field, act_mix, pre_mix, pre_deep, pred_out, msg_out, mixed,
):
    crows, ccols, chan = act.shape
    width = ccols + 2 * HALO
    row = halo_rows(act, p1, p2, t1, t2)
    for r in range(crows + 4):
        own, edge = row(r + 2)
        field[r, 0:ccols, :] = own
        field[r, ccols:, :] = edge

    def keep_mixed(r, span, value):
        mixed[r, :, span] = value

    conv_pass(field, crows + 4, k_first[...].astype(F32), keep_mixed, chan)

    shape = (2, width, chan)
    col_ok = inside_columns(shape, ccols)
    band = lax.axis_index("band")
    first_row = jnp.where(band == 0, 1, 0)
    last_row = jnp.where(band == lax.axis_size("band") - 1, crows + 1, crows + 2)
    weights = w_mix[...]
    for g in range((crows + 2) // 2):
        at = iota(shape, 0) + 2 * g
        ok = col_ok & (at >= first_row) & (at < last_row)
        pair = slice(2 * g, 2 * g + 2)
        pre, post = mix_pair(mixed[pair], field[2 * g + 1 : 2 * g + 3], weights, ok)
        pre_mix[pair] = pre
        act_mix[pair] = post

    def keep_deep(r, span, value):
        pre_deep[r, :, span] = value

    conv_pass(act_mix, crows + 2, k_deep[...].astype(F32), keep_deep, chan)

    head = wall[...]
    head_row = (iota(head.shape, 0) % (4 * crows)) // 4
    pred = jnp.zeros((ccols, LANES), F32)
    for i in range(crows):
        out = act_mix[i + 1, 0:ccols, :] + gelu_exact(pre_deep[i, 0:ccols, :])
        pred = pred + dot_nt(
            out.astype(BF16), jnp.where(head_row == i, head, 0.0).astype(BF16)
        )
    pred_out[...] = pred

    maps = bm[...]
    slots = iota((LANES, LANES), 0).astype(F32)[:88]
    sums = jnp.zeros((88, LANES), F32)
    for j in range(ccols):
        sums = sums + jnp.where(maps[j : j + 1, :] == slots, pred[j : j + 1, :], 0.0)
    msg_out[...] = msg_in[...]
    msg_out[0:1, :] = across_lanes(sums)


def across_lanes(acc):
    rest = jnp.zeros((LANES - acc.shape[0], LANES), F32)
    turned = jnp.concatenate([acc, rest], axis=0).T
    total = jnp.sum(turned, axis=0, keepdims=True)
    return jnp.where(iota((1, LANES), 1) > 0, total, 0.0)


def count_kernel(pre_first, bm, msg_in, slope_first, msg_out):
    slope_first[...] = gelu_slope(pre_first[...])
    maps = bm[...]
    slots = iota((LANES, LANES), 0).astype(F32)[:88]
    counts = jnp.zeros((88, LANES), F32)
    for j in range(maps.shape[0]):
        counts = counts + jnp.where(maps[j : j + 1, :] == slots, 1.0, 0.0)
    msg_out[...] = msg_in[...]
    msg_out[1:2, :] = across_lanes(counts)


def rim_kernel(
    after, act, p1, p2, t1, t2, w_mix, k_first, k_deep, field, act_mix, slope_rim,
    ext, mixed, side,
):
    del after
    crows, ccols, chan = act.shape
    width = ccols + 2 * HALO
    row = halo_rows(act, p1, p2, t1, t2)
    outer = (0, 1) if side == 0 else (crows + 6, crows + 7)
    inner = (0, 1) if side == 0 else (crows + 2, crows + 3)
    near = (2, 3) if side == 0 else (0, 1)
    far = (0, 1) if side == 0 else (2, 3)
    for r, at in zip(outer, far):
        own, edge = row(r)
        ext[at, 0:ccols, :] = own
        ext[at, ccols:, :] = edge
    for r, at in zip(inner, near):
        ext[at] = field[r]

    def keep(r, span, value):
        mixed[r, :, span] = value

    conv_pass(ext, 4, k_first[...].astype(F32), keep, chan)
    edge_band = 0 if side == 0 else lax.axis_size("band") - 1
    ok = inside_columns((2, width, chan), ccols) & (lax.axis_index("band") != edge_band)
    _, post = mix_pair(mixed[...], ext[1:3], w_mix[...], ok)
    have = (0, 1) if side == 0 else (crows, crows + 1)
    for n in range(2):
        ext[far[n]] = post[n]
        ext[near[n]] = act_mix[have[n]]
    conv_pass(ext, 4, k_deep[...].astype(F32), keep, chan)
    slope_rim[...] = gelu_slope(mixed[...])


def slope_kernel(after, mix, deep, slope_mix, slope_deep):
    del after
    slope_mix[...] = gelu_slope(mix[...])
    slope_deep[...] = gelu_slope(deep[...])


def pred_kernel(after, pred, land, cells):
    del after
    rows, cols = land.shape
    turned = pred[...].T
    wide = jnp.concatenate([turned[b * rows : (b + 1) * rows] for b in range(4)], axis=1)
    high = wide.astype(BF16)
    low = (wide - high.astype(F32)).astype(BF16)
    spread = spread_matrix(cols)
    cells[...] = (dot(high, spread) + dot(low, spread)) * land[...].astype(F32)


def backward_kernel(
    gathered, bm, p1, p2, t1, t2, slope_deep, rim_above, rim_below, slope_mix,
    slope_first,
    w_mix, k_first, k_deep, wall, w_wide,
    mean_out, loss_out, grad_out,
    targets, table, grads, field, mixing, proj, share_rows, share, loss_scale, c_in,
):
    ndev = gathered.shape[0]
    crows = slope_first.shape[0]
    ccols = slope_first.shape[1]
    chan = slope_first.shape[2]
    width = ccols + 2 * HALO
    band, tile = lax.axis_index("band"), lax.axis_index("tile")
    bands, tiles = lax.axis_size("band"), lax.axis_size("tile")
    me = tile * bands + band
    masks = hop_masks(bands, tiles)

    def slot_at(owner):
        apart = owner ^ me
        return sum(jnp.where(apart & mask > 0, 2**n, 0) for n, mask in enumerate(masks))

    def slot_of(v, t):
        other_band, other_tile = band + v, tile + t
        ok = (other_band >= 0) & (other_band < bands) & (other_tile >= 0) & (other_tile < tiles)
        return jnp.where(ok, slot_at(other_tile * bands + other_band), 0)

    height = ndev * share_rows
    chunk = min(16, ndev)
    first_target = gathered.shape[1] - share_rows
    sub = iota((height, LANES), 0).astype(F32).astype(BF16)
    sub_lo = iota((LANES, LANES), 0).astype(F32).astype(BF16)
    one, none = jnp.ones((), BF16), jnp.zeros((), BF16)

    def gather_chunk(c, acc):
        hot_hi, hot_lo = [], []
        for o in range(chunk):
            owner = c * chunk + o
            m = gathered[slot_at(owner)]
            hot_hi.append(jnp.where(sub == m[2:3].astype(BF16), one, none))
            low_hit = sub_lo == m[3:4].astype(BF16)
            high = rounded(m[0:1])
            parts = [high, m[0:1] - high, m[1:2]]
            hot_lo.append(
                jnp.concatenate(
                    [jnp.where(low_hit, part.astype(BF16), none) for part in parts], axis=0
                )
            )
            targets[pl.ds(owner * share_rows, share_rows)] = m[first_target:]
        return acc + dot_nt(
            jnp.concatenate(hot_hi, axis=1), jnp.concatenate(hot_lo, axis=1)
        )

    acc = jnp.zeros((height, 3 * LANES), F32)
    if ndev == chunk:
        acc = gather_chunk(0, acc)
    else:
        acc = lax.fori_loop(0, ndev // chunk, gather_chunk, acc)
    region_sum = acc[:, :LANES] + acc[:, LANES : 2 * LANES]
    region_count = acc[:, 2 * LANES :]
    at_least = jnp.maximum(region_count, 1.0)
    mean = region_sum / at_least
    table[...] = mean
    misfit = mean - targets[...]
    row = iota((height, LANES), 0)
    place = (row % share_rows) * LANES + iota((height, LANES), 1)
    inside = (place < share) & ((row // share_rows) * share + place < REGIONS)
    terms = jnp.where(inside, region_count * misfit * misfit, 0.0)
    loss_out[...] = jnp.sum(
        jnp.sum(terms, axis=0, keepdims=True), axis=1, keepdims=True
    ) * loss_scale
    grads[...] = jnp.where(inside, region_count * misfit / at_least, 0.0)
    mean_out[...] = table[pl.ds(me * share_rows, share_rows)]

    sub8 = iota((8, LANES), 0).astype(F32)

    def block_grads(slot):
        m = gathered[slot]
        low = jnp.broadcast_to(jnp.maximum(m[3:4], 0.0), (8, LANES)).astype(jnp.int32)
        high = m[2:3]
        total = jnp.zeros((8, LANES), F32)
        for at in range(0, height, 8):
            found = jnp.take_along_axis(grads[at : at + 8], low, axis=1)
            total = total + jnp.where(high == sub8 + float(at), found, 0.0)
        return jnp.sum(total, axis=0, keepdims=True)

    n = HALO * ccols
    half = ccols // 2
    odd_b = parity("band") == 1
    odd_t = parity("tile") == 1
    up = jnp.where(odd_b, p1[n:].astype(F32), p2[n:].astype(F32))
    down = jnp.where(odd_b, p2[n:].astype(F32), p1[n:].astype(F32))
    m = HALO * (crows + 2 * HALO)
    left = jnp.where(odd_t, t1[m:].astype(F32), t2[m:].astype(F32))[:, :LANES]
    right = jnp.where(odd_t, t2[m:].astype(F32), t1[m:].astype(F32))[:, :LANES]
    maps = [
        jnp.concatenate([up[:, :LANES], up[:, LANES:]], axis=0),
        bm[...],
        jnp.concatenate([down[:, :LANES], down[:, LANES:]], axis=0),
    ]
    cells = []
    gap = jnp.zeros((4, LANES), F32)
    for v in range(3):
        mid = block_grads(slot_of(v - 1, 0))
        lo = block_grads(slot_of(v - 1, -1))
        hi = block_grads(slot_of(v - 1, 1))
        source = jnp.broadcast_to(mid, (8, LANES))
        parts = [
            jnp.take_along_axis(source, maps[v][at : at + 8].astype(jnp.int32), axis=1)
            for at in range(0, ccols, 8)
        ]
        edge = jnp.concatenate(
            [right[2 * v : 2 * v + 2], gap, left[2 * v : 2 * v + 2]], axis=0
        ).astype(jnp.int32)
        source = jnp.concatenate(
            [jnp.broadcast_to(hi, (4, LANES)), jnp.broadcast_to(lo, (4, LANES))], axis=0
        )
        parts.append(jnp.take_along_axis(source, edge, axis=1))
        cells.append(jnp.concatenate(parts, axis=0).astype(BF16))

    head = wall[...]
    head_row = (iota(head.shape, 0) % (4 * crows)) // 4
    nrow = crows + 4
    for r in range(nrow):
        v = 0 if r < 2 else 1 if r < crows + 2 else 2
        i = (crows - 2 + r) if v == 0 else (r - 2) if v == 1 else r - crows - 2
        weights = jnp.where(head_row == i, head, 0.0).astype(BF16)
        deep = rounded(dot(cells[v], weights))
        mixing[r] = deep
        slope = rim_above[r] if v == 0 else slope_deep[i] if v == 1 else rim_below[r - crows - 2]
        field[r] = deep * slope

    def keep_mix(r, span, value):
        mixing[r + 1, :, span] = rounded(mixing[r + 1, :, span] + value)

    def reversed_taps(k):
        k = k[...].astype(F32)
        return jnp.concatenate([k[t : t + 1] for t in range(8, -1, -1)], axis=0)

    conv_pass(field, nrow, reversed_taps(k_deep), keep_mix, chan)
    weights = w_mix[...]

    for g in range((nrow - 2) // 2):
        pre = (mixing[2 * g + 1 : 2 * g + 3] * slope_mix[2 * g : 2 * g + 2]).reshape(
            2 * width, chan
        )
        field[2 * g : 2 * g + 2] = dot_nt(pre.astype(BF16), weights).reshape(2, width, chan)

    def keep_first(r, span, value):
        total = mixing[r + 2, 0:ccols, span] + value[0:ccols]
        proj[r, :, span] = (total * slope_first[r, :, span]).astype(BF16)

    conv_pass(field, nrow - 2, reversed_taps(k_first), keep_first, chan)

    c_pad = 32
    out = dot_nt(w_wide[...], proj[...].reshape(crows * ccols, chan))
    wide = 4 * c_pad
    spread = spread_matrix(4 * ccols)
    group = crows // 4
    for g in range(4):
        lhs = jnp.concatenate(
            [
                jnp.concatenate(
                    [
                        out[b * wide : (b + 1) * wide, i * ccols : (i + 1) * ccols]
                        for b in range(4)
                    ],
                    axis=1,
                )
                for i in range(g * group, (g + 1) * group)
            ],
            axis=0,
        )
        fine = dot(lhs.astype(BF16), spread)
        for r in range(4 * group):
            grad_out[4 * group * g + r] = fine[r * c_pad : r * c_pad + c_in].astype(BF16)


def call(kernel, outs, scratch=(), hbm=0):
    def run(*args):
        space = [pl.BlockSpec(memory_space=pl.ANY)] * hbm
        space += [pl.BlockSpec(memory_space=pltpu.VMEM)] * (len(args) - hbm)
        return pl.pallas_call(
            kernel,
            out_shape=[jax.ShapeDtypeStruct(s, d) for s, d in outs],
            in_specs=space,
            out_specs=[pl.BlockSpec(memory_space=pltpu.VMEM)] * len(outs),
            scratch_shapes=[
                pltpu.SemaphoreType.DMA(s) if d is None else pltpu.VMEM(s, d)
                for s, d in scratch
            ],
            compiler_params=pltpu.CompilerParams(vmem_limit_bytes=VMEM_LIMIT),
            cost_estimate=pl.CostEstimate(
                flops=10**6, bytes_accessed=10**6, transcendentals=0
            ),
        )(*args)

    return run


def hop_masks(bands, tiles):
    return [2**n for n in range((bands * tiles).bit_length() - 2, -1, -1)]


def exchange(first, second, axis):
    size = lax.axis_size(axis)
    results = []
    for message, start in ((second, 1), (first, 0)):
        pairs = [(i, i + 1) for i in range(start, size - 1, 2)]
        results.append(lax.ppermute(message(), axis, pairs + [(j, i) for i, j in pairs]))
    return results[1], results[0]


def per_device(
    features, land_mask, cell_blocks, region_ids, targets, w_embed, k_first, w_mix, k_deep, w_head
):
    rows, cols = land_mask.shape
    crows, ccols = rows // 4, cols // 4
    c_in = features.shape[2]
    chan = w_embed.shape[1]
    width = ccols + 2 * HALO
    nblk = cell_blocks.shape[-2]
    bands, tiles = lax.axis_size("band"), lax.axis_size("tile")
    ndev = bands * tiles
    share = targets.shape[0]
    share_rows = pl.next_power_of_2(pl.cdiv(share, LANES))
    msg_rows = pl.cdiv(4 + share_rows, 8) * 8

    rid = region_ids.reshape(1, nblk)
    owner, place = rid // share, rid % share
    pad = ((0, 0), (1, LANES - 1 - nblk))
    high = jnp.pad(owner * share_rows + place // LANES, pad, constant_values=-1)
    low = jnp.pad(place % LANES, pad, constant_values=-1)
    blank = jnp.zeros((1, LANES), F32)
    tgt = jnp.pad(targets, (0, share_rows * LANES - share)).reshape(share_rows, LANES)
    msg_in = jnp.concatenate(
        [blank, blank, high.astype(F32), low.astype(F32)]
        + [jnp.zeros((msg_rows - 4 - share_rows, LANES), F32), tgt],
        axis=0,
    )
    head = w_head.T.reshape(4, 4, chan).transpose(1, 0, 2).astype(F32)
    wall = jnp.broadcast_to(head[:, None], (4, crows, 4, chan)).reshape(16 * crows, chan)

    feat = features.transpose(0, 2, 1)
    msg1 = HALO * ccols + ccols // 2
    pre_first, act, bm, m2, w_wide = call(
        embed_kernel,
        [
            ((crows * ccols, chan), F32),
            ((crows, ccols, chan), BF16),
            ((ccols, LANES), F32),
            ((msg1, chan), BF16),
            ((512, chan), BF16),
        ],
        [
            ((rows, c_in, cols), BF16),
            ((16 * c_in, chan), BF16),
            ((rows, cols), jnp.int32),
            ((nblk, 1, LANES), jnp.int32),
            ((7,), None),
        ],
        hbm=4,
    )(
        *(
            pltpu.with_memory_space_constraint(x, pltpu.HBM)
            for x in (feat, w_embed, land_mask, cell_blocks.reshape(nblk, 1, LANES))
        )
    )
    def pack_first():
        return call(pack_kernel, [((msg1, chan), BF16)])(act, bm)[0]

    p1, p2 = exchange(pack_first, lambda: m2, "band")
    msg2 = HALO * (crows + 2 * HALO) + 16

    def edges(second):
        kernel = functools.partial(edges_kernel, second=second)
        return call(kernel, [((msg2, chan), BF16)])(act, bm, p1, p2)[0]

    t1, t2 = exchange(lambda: edges(False), lambda: edges(True), "tile")
    slope_first, msg_in = call(
        count_kernel, [((crows * ccols, chan), F32), ((msg_rows, LANES), F32)]
    )(pre_first, bm, msg_in)
    nrow = crows + 2 * HALO
    field, act_mix, pre_mix, pre_deep, pred, msg = call(
        forward_kernel,
        [
            ((crows + 4, width, chan), F32),
            ((crows + 2, width, chan), F32),
            ((crows + 2, width, chan), F32),
            ((crows, width, chan), F32),
            ((ccols, LANES), F32),
            ((msg_rows, LANES), F32),
        ],
        [((crows + 2, width, chan), F32)],
    )(act, bm, p1, p2, t1, t2, w_mix, k_first, k_deep, wall, msg_in)

    def slopes(after):
        return call(
            slope_kernel,
            [((crows + 2, width, chan), F32), ((crows, width, chan), F32)],
            hbm=1,
        )(after, pre_mix, pre_deep)

    def cells(after):
        return call(pred_kernel, [((rows, cols), F32)], hbm=1)(after, pred, land_mask)

    def rim(side, after):
        return call(
            functools.partial(rim_kernel, side=side),
            [((2, width, chan), F32)],
            [((4, width, chan), F32), ((2, width, chan), F32)],
            hbm=1,
        )(after, act, p1, p2, t1, t2, w_mix, k_first, k_deep, field, act_mix)

    def send(x, mask):
        pairs = [(n, n ^ mask) for n in range(ndev)]
        return lax.ppermute(x, ("tile", "band"), pairs)

    masks = hop_masks(bands, tiles)
    beside = [slopes, lambda after: (rim(0, after), rim(1, after)), cells]
    made = []
    msgs = msg[None]
    for n, mask in enumerate(masks):
        if n < len(beside):
            made.append(beside[n](msgs))
        msgs = jnp.concatenate([msgs, send(msgs, mask)], axis=0)
    (slope_mix, slope_deep), ((rim_above,), (rim_below,)), (cell_pred,) = made

    height = ndev * share_rows
    mean, loss, grad = call(
        functools.partial(
            backward_kernel,
            share_rows=share_rows,
            share=share,
            loss_scale=1.0 / (2.0 * rows * cols * ndev),
            c_in=c_in,
        ),
        [((share_rows, LANES), F32), ((1, 1), F32), ((rows, c_in, cols), BF16)],
        [
            ((height, LANES), F32),
            ((height, LANES), F32),
            ((height, LANES), F32),
            ((nrow - 4, width, chan), F32),
            ((nrow - 4, width, chan), F32),
            ((crows, ccols, chan), BF16),
        ],
    )(
        msgs, bm, p1, p2, t1, t2, slope_deep, rim_above, rim_below, slope_mix,
        slope_first.reshape(crows, ccols, chan), w_mix, k_first, k_deep, wall, w_wide,
    )
    return (
        cell_pred,
        mean.reshape(-1)[:share],
        loss.reshape(1),
        grad.transpose(0, 2, 1),
    )


def solution(mesh):
    in_specs = (
        P(("group", "band"), "tile", None),
        P("band", "tile"),
        P("band", "tile", None, None),
        P("band", "tile", None),
        P(("group", "tile", "band")),
        P(),
        P(),
        P(),
        P(),
        P(),
    )
    out_specs = (
        P(("group", "band"), "tile"),
        P(("group", "tile", "band")),
        P("group"),
        P(("group", "band"), "tile", None),
    )
    return jax.shard_map(
        per_device, mesh=mesh, in_specs=in_specs, out_specs=out_specs, check_vma=False
    )
```

```python
import functools

import jax
import jax.numpy as jnp
from jax import lax
from jax.experimental import pallas as pl
from jax.experimental.pallas import tpu as pltpu
from jax.sharding import PartitionSpec as P

REGIONS = 14000
SQRT_HALF = 0.7071067811865476
INV_ROOT = 0.3989422804014327
F32 = jnp.float32
BF16 = jnp.bfloat16
LANES = 128
HALO = 4
OUTSIDE = -50.0
VMEM_LIMIT = 48 * 1024 * 1024


def gelu_exact(v):
    return 0.5 * v * (1.0 + lax.erf(v * SQRT_HALF))


def gelu_slope(v):
    return 0.5 * (1.0 + lax.erf(v * SQRT_HALF)) + v * jnp.exp(-0.5 * v * v) * INV_ROOT


def rounded(v):
    return v.astype(BF16).astype(F32)


def dot(a, b):
    return jnp.dot(a, b, preferred_element_type=F32)


def dot_nt(a, b):
    return lax.dot_general(a, b, (((1,), (1,)), ((), ())), preferred_element_type=F32)


def iota(shape, dim):
    return lax.broadcasted_iota(jnp.int32, shape, dim)


def spread_matrix(cols, transposed=False):
    quarter = cols // 4
    shape = (cols, cols)
    n = iota(shape, 0)
    c = iota(shape, 1)
    return jnp.where(c == 4 * (n % quarter) + n // quarter, 1.0, 0.0).astype(BF16)


def padded_embed(w_ref, c_in, c_pad):
    w = w_ref[...].astype(F32)
    zeros = jnp.zeros((c_pad - c_in, w.shape[1]), F32)
    parts = []
    for b in range(4):
        for a in range(4):
            start = (4 * a + b) * c_in
            parts += [w[start : start + c_in], zeros]
    return jnp.concatenate(parts, axis=0).astype(BF16)


def parity(axis):
    return lax.axis_index(axis) % 2


def embed_kernel(
    feat_hbm, w_hbm, land_hbm, blocks_hbm, pre_out, act_out, bm_out, m2_out, w_out,
    feat, w_embed, land, blocks, sems,
):
    rows, c_in, cols = feat.shape
    part = rows // 4
    pairs = [(blocks_hbm, blocks), (land_hbm, land), (w_hbm, w_embed)]
    pairs += [
        (feat_hbm.at[pl.ds(part * n, part)], feat.at[pl.ds(part * n, part)]) for n in range(4)
    ]
    copies = [pltpu.make_async_copy(src, dst, sems.at[n]) for n, (src, dst) in enumerate(pairs)]
    for copy in copies:
        copy.start()
    c_pad = 32
    crows, ccols = rows // 4, cols // 4
    nblk = blocks.shape[0]
    spread = spread_matrix(cols)

    for copy in copies:
        copy.wait()
    shift_row = cols.bit_length() - 1
    chunk = next(c for c in (9, 8, 7, 6, 5, 4, 3, 2, 1) if nblk % c == 0)
    total = jnp.zeros((ccols, LANES), F32)
    sub_a = iota((LANES, LANES), 0).astype(F32).astype(BF16)
    sub_b = iota((ccols, LANES), 0).astype(F32).astype(BF16)
    one, none = jnp.ones((), BF16), jnp.zeros((), BF16)
    cells = blocks[...].reshape(nblk, LANES)
    named = cells < rows * cols
    all_q = jnp.where(named, (cells & 3) * rows + (cells >> shift_row), -1).astype(F32)
    all_j = ((cells & (cols - 1)) >> 2).astype(F32)
    for first in range(0, nblk, chunk):
        hot_q, hot_j = [], []
        for k in range(first, first + chunk):
            q = all_q[k : k + 1].astype(BF16)
            j = all_j[k : k + 1].astype(BF16)
            hot_q.append(jnp.where(sub_a == q, one, none))
            hot_j.append(jnp.where(sub_b == j, jnp.array(k + 1, BF16), none))
        total = total + dot_nt(
            jnp.concatenate(hot_j, axis=1), jnp.concatenate(hot_q, axis=1)
        )
    land_moved = dot_nt(spread, land[...].astype(F32).astype(BF16))
    land_q = jnp.concatenate(
        [land_moved[b * ccols : (b + 1) * ccols, :] for b in range(4)], axis=1
    )
    bm = total * land_q
    bm_out[...] = bm

    field = feat[...].astype(F32)
    field = jnp.concatenate([field, jnp.zeros((rows, c_pad - c_in, cols), F32)], axis=1)
    field = field.reshape(rows * c_pad, cols).astype(BF16)
    moved = dot_nt(spread, field).astype(BF16)
    wide = 4 * c_pad
    lhs = jnp.concatenate(
        [
            jnp.concatenate(
                [
                    moved[b * ccols : (b + 1) * ccols, i * wide : (i + 1) * wide]
                    for b in range(4)
                ],
                axis=1,
            )
            for i in range(crows)
        ],
        axis=0,
    )
    weights = padded_embed(w_embed, c_in, c_pad)
    w_out[...] = weights
    pre = dot(lhs, weights)
    chan = pre.shape[1]
    pre_out[...] = pre
    act_out[...] = gelu_exact(pre).astype(BF16).reshape(crows, ccols, chan)
    pack(act_out, bm, parity("band"), m2_out)


def pack(act, bm, low, out):
    crows, ccols, chan = act.shape
    half = ccols // 2
    start = low * (crows - HALO)
    out[0 : HALO * ccols] = act[pl.ds(start, HALO)].reshape(HALO * ccols, chan)
    out[HALO * ccols :] = jnp.concatenate([bm[:half], bm[half:]], axis=1).astype(BF16)


def pack_kernel(act, bm, m1_out):
    pack(act, bm[...], 1 - parity("band"), m1_out)


def edges_kernel(act, bm, p1, p2, out, second):
    crows, ccols, chan = act.shape
    odd_b = parity("band") == 1
    odd_t = parity("tile") == 1
    n = HALO * ccols
    up = jnp.where(odd_b, p1[...].astype(F32), p2[...].astype(F32))
    down = jnp.where(odd_b, p2[...].astype(F32), p1[...].astype(F32))
    left, right = [], []
    for r in range(crows + 2 * HALO):
        if r < HALO:
            row = up[r * ccols : (r + 1) * ccols]
        elif r < HALO + crows:
            row = act[r - HALO].astype(F32)
        else:
            row = down[(r - HALO - crows) * ccols : (r - HALO - crows + 1) * ccols]
        left.append(row[:HALO])
        right.append(row[ccols - HALO :])
    half = ccols // 2
    own = bm[...]
    zeros = jnp.zeros((10, LANES), F32)
    bm_left = [up[n : n + 2, :LANES], own[0:2], down[n : n + 2, :LANES], zeros]
    bm_right = [
        up[n + half - 2 : n + half, LANES:],
        own[ccols - 2 :],
        down[n + half - 2 : n + half, LANES:],
        zeros,
    ]
    def message(cells, maps):
        maps = jnp.concatenate(maps, axis=0)
        maps = jnp.concatenate([maps, jnp.zeros((16, chan - LANES), F32)], axis=1)
        return jnp.concatenate(cells + [maps], axis=0)

    left = message(left, bm_left)
    right = message(right, bm_right)
    low = ~odd_t if second else odd_t
    out[...] = jnp.where(low, left, right).astype(BF16)


def conv_pass(src, count, kernel, emit, chan):
    width = src.shape[1]
    for h in range(0, chan, LANES):
        span = slice(h, h + LANES)
        taps = [kernel[t : t + 1, span] for t in range(9)]
        sums = [None] * (count - 2)
        for r in range(count):
            x = src[r, :, span]
            before = pltpu.roll(x, 1, 0)
            after = pltpu.roll(x, width - 1, 0)
            for a in range(3):
                if 0 <= r - a < count - 2:
                    part = taps[3 * a] * before + taps[3 * a + 1] * x + taps[3 * a + 2] * after
                    sums[r - a] = part if a == 0 else sums[r - a] + part
            if r >= 2:
                emit(r - 2, span, sums[r - 2])


def halo_rows(act, p1, p2, t1, t2):
    crows, ccols, chan = act.shape
    odd_b = parity("band") == 1
    odd_t = parity("tile") == 1

    def edge(first, second, odd, at, n):
        return jnp.where(odd, first[at : at + n].astype(F32), second[at : at + n].astype(F32))

    def row(r):
        if r < HALO:
            own = edge(p1, p2, odd_b, r * ccols, ccols)
        elif r < HALO + crows:
            own = act[r - HALO].astype(F32)
        else:
            own = edge(p2, p1, odd_b, (r - HALO - crows) * ccols, ccols)
        base = HALO * r // 16 * 16
        at = HALO * r - base
        left = edge(t1, t2, odd_t, base, 16)[at : at + HALO]
        right = edge(t2, t1, odd_t, base, 16)[at : at + HALO]
        return own, jnp.concatenate([right, left], axis=0)

    return row


def inside_columns(shape, ccols):
    tile = lax.axis_index("tile")
    first = tile == 0
    last = tile == lax.axis_size("tile") - 1
    col = iota(shape, len(shape) - 2)
    low = jnp.where(last, ccols, ccols + HALO)
    high = jnp.where(first, ccols + 2 * HALO, ccols + HALO)
    return (col < low) | (col >= high)


def mix_pair(pair, base, weights, ok):
    _, width, chan = pair.shape
    pre = dot(pair.reshape(2 * width, chan).astype(BF16), weights).reshape(2, width, chan)
    pre = jnp.where(ok, pre, OUTSIDE)
    return pre, rounded(base + gelu_exact(pre))


def forward_kernel(
    act, bm, p1, p2, t1, t2, w_mix, k_first, k_deep, wall, msg_in,
    field, act_mix, pre_mix, pre_deep, pred_out, msg_out, mixed,
):
    crows, ccols, chan = act.shape
    width = ccols + 2 * HALO
    row = halo_rows(act, p1, p2, t1, t2)
    for r in range(crows + 4):
        own, edge = row(r + 2)
        field[r, 0:ccols, :] = own
        field[r, ccols:, :] = edge

    def keep_mixed(r, span, value):
        mixed[r, :, span] = value

    conv_pass(field, crows + 4, k_first[...].astype(F32), keep_mixed, chan)

    shape = (2, width, chan)
    col_ok = inside_columns(shape, ccols)
    band = lax.axis_index("band")
    first_row = jnp.where(band == 0, 1, 0)
    last_row = jnp.where(band == lax.axis_size("band") - 1, crows + 1, crows + 2)
    weights = w_mix[...]
    for g in range((crows + 2) // 2):
        at = iota(shape, 0) + 2 * g
        ok = col_ok & (at >= first_row) & (at < last_row)
        pair = slice(2 * g, 2 * g + 2)
        pre, post = mix_pair(mixed[pair], field[2 * g + 1 : 2 * g + 3], weights, ok)
        pre_mix[pair] = pre
        act_mix[pair] = post

    def keep_deep(r, span, value):
        pre_deep[r, :, span] = value

    conv_pass(act_mix, crows + 2, k_deep[...].astype(F32), keep_deep, chan)

    head = wall[...]
    head_row = (iota(head.shape, 0) % (4 * crows)) // 4
    pred = jnp.zeros((ccols, LANES), F32)
    for i in range(crows):
        out = act_mix[i + 1, 0:ccols, :] + gelu_exact(pre_deep[i, 0:ccols, :])
        pred = pred + dot_nt(
            out.astype(BF16), jnp.where(head_row == i, head, 0.0).astype(BF16)
        )
    pred_out[...] = pred

    maps = bm[...]
    slots = iota((LANES, LANES), 0).astype(F32)[:88]
    sums = jnp.zeros((88, LANES), F32)
    for j in range(ccols):
        sums = sums + jnp.where(maps[j : j + 1, :] == slots, pred[j : j + 1, :], 0.0)
    msg_out[...] = msg_in[...]
    msg_out[0] = across_lanes(sums)


def across_lanes(acc):
    rest = jnp.zeros((LANES - acc.shape[0], LANES), F32)
    turned = jnp.concatenate([acc, rest], axis=0).T
    total = jnp.sum(turned, axis=0, keepdims=True)
    return jnp.where(iota((1, LANES), 1) > 0, total, 0.0)


def count_kernel(pre_first, bm, msg_in, slope_first, msg_out):
    slope_first[...] = gelu_slope(pre_first[...])
    maps = bm[...]
    slots = iota((LANES, LANES), 0).astype(F32)[:88]
    counts = jnp.zeros((88, LANES), F32)
    for j in range(maps.shape[0]):
        counts = counts + jnp.where(maps[j : j + 1, :] == slots, 1.0, 0.0)
    msg_out[...] = msg_in[...]
    msg_out[1] = across_lanes(counts)


def rim_kernel(
    after, act, p1, p2, t1, t2, w_mix, k_first, k_deep, field, act_mix, slope_rim,
    ext, mixed, side,
):
    del after
    crows, ccols, chan = act.shape
    width = ccols + 2 * HALO
    row = halo_rows(act, p1, p2, t1, t2)
    outer = (0, 1) if side == 0 else (crows + 6, crows + 7)
    inner = (0, 1) if side == 0 else (crows + 2, crows + 3)
    near = (2, 3) if side == 0 else (0, 1)
    far = (0, 1) if side == 0 else (2, 3)
    for r, at in zip(outer, far):
        own, edge = row(r)
        ext[at, 0:ccols, :] = own
        ext[at, ccols:, :] = edge
    for r, at in zip(inner, near):
        ext[at] = field[r]

    def keep(r, span, value):
        mixed[r, :, span] = value

    conv_pass(ext, 4, k_first[...].astype(F32), keep, chan)
    edge_band = 0 if side == 0 else lax.axis_size("band") - 1
    ok = inside_columns((2, width, chan), ccols) & (lax.axis_index("band") != edge_band)
    _, post = mix_pair(mixed[...], ext[1:3], w_mix[...], ok)
    have = (0, 1) if side == 0 else (crows, crows + 1)
    for n in range(2):
        ext[far[n]] = post[n]
        ext[near[n]] = act_mix[have[n]]
    conv_pass(ext, 4, k_deep[...].astype(F32), keep, chan)
    slope_rim[...] = gelu_slope(mixed[...])


def slope_kernel(after, mix, deep, pred, land, slope_mix, slope_deep, cells):
    del after
    slope_mix[...] = gelu_slope(mix[...])
    slope_deep[...] = gelu_slope(deep[...])
    rows, cols = land.shape
    turned = pred[...].T
    wide = jnp.concatenate([turned[b * rows : (b + 1) * rows] for b in range(4)], axis=1)
    high = wide.astype(BF16)
    low = (wide - high.astype(F32)).astype(BF16)
    spread = spread_matrix(cols)
    cells[...] = (dot(high, spread) + dot(low, spread)) * land[...].astype(F32)


def backward_kernel(
    gathered, bm, p1, p2, t1, t2, slope_deep, rim_above, rim_below, slope_mix,
    slope_first,
    w_mix, k_first, k_deep, wall, w_wide,
    mean_out, loss_out, grad_out,
    targets, table, grads, field, mixing, proj, share_rows, share, loss_scale, c_in,
):
    ndev = gathered.shape[0]
    crows = slope_first.shape[0]
    ccols = slope_first.shape[1]
    chan = slope_first.shape[2]
    width = ccols + 2 * HALO
    band, tile = lax.axis_index("band"), lax.axis_index("tile")
    bands, tiles = lax.axis_size("band"), lax.axis_size("tile")
    me = tile * bands + band
    masks = hop_masks(bands, tiles)

    def slot_at(owner):
        apart = owner ^ me
        return sum(jnp.where(apart & mask > 0, 2**n, 0) for n, mask in enumerate(masks))

    def slot_of(v, t):
        other_band, other_tile = band + v, tile + t
        ok = (other_band >= 0) & (other_band < bands) & (other_tile >= 0) & (other_tile < tiles)
        return jnp.where(ok, slot_at(other_tile * bands + other_band), 0)

    height = ndev * share_rows
    chunk = min(16, ndev)
    target_rows = gathered.shape[1] - 4
    sub = iota((height, LANES), 0).astype(F32).astype(BF16)
    sub_lo = iota((LANES, LANES), 0).astype(F32).astype(BF16)
    one, none = jnp.ones((), BF16), jnp.zeros((), BF16)

    def gather_chunk(c, acc):
        hot_hi, hot_lo = [], []
        for o in range(chunk):
            owner = c * chunk + o
            m = gathered[slot_at(owner)]
            hot_hi.append(jnp.where(sub == m[2].astype(BF16), one, none))
            low_hit = sub_lo == m[3].astype(BF16)
            high = rounded(m[0])
            parts = [high, m[0] - high, m[1]]
            hot_lo.append(
                jnp.concatenate(
                    [jnp.where(low_hit, part.astype(BF16), none) for part in parts], axis=0
                )
            )
            for n in range(target_rows):
                targets[pl.ds(owner * share_rows + n, 1)] = m[4 + n]
        return acc + dot_nt(
            jnp.concatenate(hot_hi, axis=1), jnp.concatenate(hot_lo, axis=1)
        )

    acc = jnp.zeros((height, 3 * LANES), F32)
    if ndev == chunk:
        acc = gather_chunk(0, acc)
    else:
        acc = lax.fori_loop(0, ndev // chunk, gather_chunk, acc)
    region_sum = acc[:, :LANES] + acc[:, LANES : 2 * LANES]
    region_count = acc[:, 2 * LANES :]
    at_least = jnp.maximum(region_count, 1.0)
    mean = region_sum / at_least
    table[...] = mean
    misfit = mean - targets[...]
    row = iota((height, LANES), 0)
    place = (row % share_rows) * LANES + iota((height, LANES), 1)
    inside = (place < share) & ((row // share_rows) * share + place < REGIONS)
    terms = jnp.where(inside, region_count * misfit * misfit, 0.0)
    loss_out[...] = jnp.sum(
        jnp.sum(terms, axis=0, keepdims=True), axis=1, keepdims=True
    ) * loss_scale
    grads[...] = jnp.where(inside, region_count * misfit / at_least, 0.0)
    mean_out[...] = table[pl.ds(me * share_rows, share_rows)]

    sub8 = iota((8, LANES), 0).astype(F32)

    def block_grads(slot):
        m = gathered[slot]
        low = jnp.broadcast_to(jnp.maximum(m[3], 0.0), (8, LANES)).astype(jnp.int32)
        high = m[2]
        total = jnp.zeros((8, LANES), F32)
        for at in range(0, height, 8):
            found = jnp.take_along_axis(grads[at : at + 8], low, axis=1)
            total = total + jnp.where(high == sub8 + float(at), found, 0.0)
        return jnp.sum(total, axis=0, keepdims=True)

    n = HALO * ccols
    half = ccols // 2
    odd_b = parity("band") == 1
    odd_t = parity("tile") == 1
    up = jnp.where(odd_b, p1[n:].astype(F32), p2[n:].astype(F32))
    down = jnp.where(odd_b, p2[n:].astype(F32), p1[n:].astype(F32))
    m = HALO * (crows + 2 * HALO)
    left = jnp.where(odd_t, t1[m:].astype(F32), t2[m:].astype(F32))[:, :LANES]
    right = jnp.where(odd_t, t2[m:].astype(F32), t1[m:].astype(F32))[:, :LANES]
    maps = [
        jnp.concatenate([up[:, :LANES], up[:, LANES:]], axis=0),
        bm[...],
        jnp.concatenate([down[:, :LANES], down[:, LANES:]], axis=0),
    ]
    cells = []
    gap = jnp.zeros((4, LANES), F32)
    for v in range(3):
        mid = block_grads(slot_of(v - 1, 0))
        lo = block_grads(slot_of(v - 1, -1))
        hi = block_grads(slot_of(v - 1, 1))
        source = jnp.broadcast_to(mid, (8, LANES))
        parts = [
            jnp.take_along_axis(source, maps[v][at : at + 8].astype(jnp.int32), axis=1)
            for at in range(0, ccols, 8)
        ]
        edge = jnp.concatenate(
            [right[2 * v : 2 * v + 2], gap, left[2 * v : 2 * v + 2]], axis=0
        ).astype(jnp.int32)
        source = jnp.concatenate(
            [jnp.broadcast_to(hi, (4, LANES)), jnp.broadcast_to(lo, (4, LANES))], axis=0
        )
        parts.append(jnp.take_along_axis(source, edge, axis=1))
        cells.append(jnp.concatenate(parts, axis=0).astype(BF16))

    head = wall[...]
    head_row = (iota(head.shape, 0) % (4 * crows)) // 4
    nrow = crows + 4
    for r in range(nrow):
        v = 0 if r < 2 else 1 if r < crows + 2 else 2
        i = (crows - 2 + r) if v == 0 else (r - 2) if v == 1 else r - crows - 2
        weights = jnp.where(head_row == i, head, 0.0).astype(BF16)
        deep = rounded(dot(cells[v], weights))
        mixing[r] = deep
        slope = rim_above[r] if v == 0 else slope_deep[i] if v == 1 else rim_below[r - crows - 2]
        field[r] = deep * slope

    def keep_mix(r, span, value):
        mixing[r + 1, :, span] = rounded(mixing[r + 1, :, span] + value)

    def reversed_taps(k):
        k = k[...].astype(F32)
        return jnp.concatenate([k[t : t + 1] for t in range(8, -1, -1)], axis=0)

    conv_pass(field, nrow, reversed_taps(k_deep), keep_mix, chan)
    weights = w_mix[...]

    for g in range((nrow - 2) // 2):
        pre = (mixing[2 * g + 1 : 2 * g + 3] * slope_mix[2 * g : 2 * g + 2]).reshape(
            2 * width, chan
        )
        field[2 * g : 2 * g + 2] = dot_nt(pre.astype(BF16), weights).reshape(2, width, chan)

    def keep_first(r, span, value):
        total = mixing[r + 2, 0:ccols, span] + value[0:ccols]
        proj[r, :, span] = (total * slope_first[r, :, span]).astype(BF16)

    conv_pass(field, nrow - 2, reversed_taps(k_first), keep_first, chan)

    c_pad = 32
    out = dot_nt(w_wide[...], proj[...].reshape(crows * ccols, chan))
    wide = 4 * c_pad
    spread = spread_matrix(4 * ccols)
    group = crows // 4
    for g in range(4):
        lhs = jnp.concatenate(
            [
                jnp.concatenate(
                    [
                        out[b * wide : (b + 1) * wide, i * ccols : (i + 1) * ccols]
                        for b in range(4)
                    ],
                    axis=1,
                )
                for i in range(g * group, (g + 1) * group)
            ],
            axis=0,
        )
        fine = dot(lhs.astype(BF16), spread)
        for r in range(4 * group):
            grad_out[4 * group * g + r] = fine[r * c_pad : r * c_pad + c_in].astype(BF16)


def call(kernel, outs, scratch=(), hbm=0):
    def run(*args):
        space = [pl.BlockSpec(memory_space=pl.ANY)] * hbm
        space += [pl.BlockSpec(memory_space=pltpu.VMEM)] * (len(args) - hbm)
        return pl.pallas_call(
            kernel,
            out_shape=[jax.ShapeDtypeStruct(s, d) for s, d in outs],
            in_specs=space,
            out_specs=[pl.BlockSpec(memory_space=pltpu.VMEM)] * len(outs),
            scratch_shapes=[
                pltpu.SemaphoreType.DMA(s) if d is None else pltpu.VMEM(s, d)
                for s, d in scratch
            ],
            compiler_params=pltpu.CompilerParams(vmem_limit_bytes=VMEM_LIMIT),
            cost_estimate=pl.CostEstimate(
                flops=10**6, bytes_accessed=10**6, transcendentals=0
            ),
        )(*args)

    return run


def hop_masks(bands, tiles):
    return [2**n for n in range((bands * tiles).bit_length() - 2, -1, -1)]


def exchange(first, second, axis):
    size = lax.axis_size(axis)
    results = []
    for message, start in ((second, 1), (first, 0)):
        pairs = [(i, i + 1) for i in range(start, size - 1, 2)]
        results.append(lax.ppermute(message(), axis, pairs + [(j, i) for i, j in pairs]))
    return results[1], results[0]


def per_device(
    features, land_mask, cell_blocks, region_ids, targets, w_embed, k_first, w_mix, k_deep, w_head
):
    rows, cols = land_mask.shape
    crows, ccols = rows // 4, cols // 4
    c_in = features.shape[2]
    chan = w_embed.shape[1]
    width = ccols + 2 * HALO
    nblk = cell_blocks.shape[-2]
    bands, tiles = lax.axis_size("band"), lax.axis_size("tile")
    ndev = bands * tiles
    share = targets.shape[0]
    share_rows = pl.next_power_of_2(pl.cdiv(share, LANES))
    target_rows = pl.cdiv(share, LANES)
    msg_rows = 4 + target_rows

    rid = region_ids.reshape(1, nblk)
    owner, place = rid // share, rid % share
    pad = ((0, 0), (1, LANES - 1 - nblk))
    high = jnp.pad(owner * share_rows + place // LANES, pad, constant_values=-1)
    low = jnp.pad(place % LANES, pad, constant_values=-1)
    blank = jnp.zeros((1, LANES), F32)
    tgt = jnp.pad(targets, (0, target_rows * LANES - share)).reshape(target_rows, LANES)
    msg_in = jnp.concatenate(
        [blank, blank, high.astype(F32), low.astype(F32), tgt], axis=0
    ).reshape(msg_rows, 1, LANES)
    head = w_head.T.reshape(4, 4, chan).transpose(1, 0, 2).astype(F32)
    wall = jnp.broadcast_to(head[:, None], (4, crows, 4, chan)).reshape(16 * crows, chan)

    feat = features.transpose(0, 2, 1)
    msg1 = HALO * ccols + ccols // 2
    pre_first, act, bm, m2, w_wide = call(
        embed_kernel,
        [
            ((crows * ccols, chan), F32),
            ((crows, ccols, chan), BF16),
            ((ccols, LANES), F32),
            ((msg1, chan), BF16),
            ((512, chan), BF16),
        ],
        [
            ((rows, c_in, cols), BF16),
            ((16 * c_in, chan), BF16),
            ((rows, cols), jnp.int32),
            ((nblk, 1, LANES), jnp.int32),
            ((7,), None),
        ],
        hbm=4,
    )(
        *(
            pltpu.with_memory_space_constraint(x, pltpu.HBM)
            for x in (feat, w_embed, land_mask, cell_blocks.reshape(nblk, 1, LANES))
        )
    )
    def pack_first():
        return call(pack_kernel, [((msg1, chan), BF16)])(act, bm)[0]

    p1, p2 = exchange(pack_first, lambda: m2, "band")
    msg2 = HALO * (crows + 2 * HALO) + 16

    def edges(second):
        kernel = functools.partial(edges_kernel, second=second)
        return call(kernel, [((msg2, chan), BF16)])(act, bm, p1, p2)[0]

    t1, t2 = exchange(lambda: edges(False), lambda: edges(True), "tile")
    slope_first, msg_in = call(
        count_kernel, [((crows * ccols, chan), F32), ((msg_rows, 1, LANES), F32)]
    )(pre_first, bm, msg_in)
    nrow = crows + 2 * HALO
    field, act_mix, pre_mix, pre_deep, pred, msg = call(
        forward_kernel,
        [
            ((crows + 4, width, chan), F32),
            ((crows + 2, width, chan), F32),
            ((crows + 2, width, chan), F32),
            ((crows, width, chan), F32),
            ((ccols, LANES), F32),
            ((msg_rows, 1, LANES), F32),
        ],
        [((crows + 2, width, chan), F32)],
    )(act, bm, p1, p2, t1, t2, w_mix, k_first, k_deep, wall, msg_in)

    def slopes(after):
        return call(
            slope_kernel,
            [
                ((crows + 2, width, chan), F32),
                ((crows, width, chan), F32),
                ((rows, cols), F32),
            ],
            hbm=1,
        )(after, pre_mix, pre_deep, pred, land_mask)

    def rim(side, after):
        return call(
            functools.partial(rim_kernel, side=side),
            [((2, width, chan), F32)],
            [((4, width, chan), F32), ((2, width, chan), F32)],
            hbm=1,
        )(after, act, p1, p2, t1, t2, w_mix, k_first, k_deep, field, act_mix)

    def send(x, mask):
        pairs = [(n, n ^ mask) for n in range(ndev)]
        return lax.ppermute(x, ("tile", "band"), pairs)

    masks = hop_masks(bands, tiles)
    beside = [slopes, functools.partial(rim, 0), functools.partial(rim, 1)]
    made = []
    msgs = msg[None]
    for n, mask in enumerate(masks):
        if n < len(beside):
            made.append(beside[n](msgs))
        msgs = jnp.concatenate([msgs, send(msgs, mask)], axis=0)
    (slope_mix, slope_deep, cell_pred), (rim_above,), (rim_below,) = made

    height = ndev * share_rows
    mean, loss, grad = call(
        functools.partial(
            backward_kernel,
            share_rows=share_rows,
            share=share,
            loss_scale=1.0 / (2.0 * rows * cols * ndev),
            c_in=c_in,
        ),
        [((share_rows, LANES), F32), ((1, 1), F32), ((rows, c_in, cols), BF16)],
        [
            ((height, LANES), F32),
            ((height, LANES), F32),
            ((height, LANES), F32),
            ((nrow - 4, width, chan), F32),
            ((nrow - 4, width, chan), F32),
            ((crows, ccols, chan), BF16),
        ],
    )(
        msgs, bm, p1, p2, t1, t2, slope_deep, rim_above, rim_below, slope_mix,
        slope_first.reshape(crows, ccols, chan), w_mix, k_first, k_deep, wall, w_wide,
    )
    return (
        cell_pred,
        mean.reshape(-1)[:share],
        loss.reshape(1),
        grad.transpose(0, 2, 1),
    )


def solution(mesh):
    in_specs = (
        P(("group", "band"), "tile", None),
        P("band", "tile"),
        P("band", "tile", None, None),
        P("band", "tile", None),
        P(("group", "tile", "band")),
        P(),
        P(),
        P(),
        P(),
        P(),
    )
    out_specs = (
        P(("group", "band"), "tile"),
        P(("group", "tile", "band")),
        P("group"),
        P(("group", "band"), "tile", None),
    )
    return jax.shard_map(
        per_device, mesh=mesh, in_specs=in_specs, out_specs=out_specs, check_vma=False
    )
```
